32 devices in a mesh: dp: 8 (over y, x, core), seq: 4 (over z).
Axes of the slice: x: 2, y: 2, z: 4, core: 2. Of those that a mesh axis runs over, the one named last changes fastest.
Arguments:
- tokens: bfloat16 [64, 512, 768], P('dp', 'seq'), may hold values from -6 to 6
- cotangent: bfloat16 [64, 512, 768], P('dp', 'seq'), may hold values from -6 to 6
- lengths: int32 [64, 4], P('dp'), may hold values from 1 to 448, 512 in all within a row
- packed_weight: float32 [768, 2304], P(('dp', 'seq')), may hold values from -0.21875 to 0.21875
- query_bias: float32 [768], P(('dp', 'seq')), may hold values from -3 to 3
- value_bias: float32 [768], P(('dp', 'seq')), may hold values from -3 to 3
- output_weight: float32 [768, 768], P(('dp', 'seq')), may hold values from -2.5 to 2.5
- output_bias: float32 [768], P(('dp', 'seq')), may hold values from -3 to 3
- first_gain: float32 [768], P(('dp', 'seq')), may hold values from 0.25 to 1.75
- first_shift: float32 [768], P(('dp', 'seq')), may hold values from -2 to 2
- inner_weight: float32 [768, 3072], P(('dp', 'seq')), may hold values from -0.21875 to 0.21875
- inner_bias: float32 [3072], P(('dp', 'seq')), may hold values from -3 to 3
- outer_weight: float32 [3072, 768], P(('dp', 'seq')), may hold values from -0.109375 to 0.109375
- outer_bias: float32 [768], P(('dp', 'seq')), may hold values from -3 to 3
- second_gain: float32 [768], P(('dp', 'seq')), may hold values from 0.25 to 1.75
- second_shift: float32 [768], P(('dp', 'seq')), may hold values from -2 to 2
Outputs:
- output: bfloat16 [64, 512, 768], P('dp', 'seq')
- tokens_grad: float32 [64, 512, 768], P('dp', 'seq')
- packed_weight_grad: float32 [768, 2304], P(('dp', 'seq'))
- query_bias_grad: float32 [768], P(('dp', 'seq'))
- value_bias_grad: float32 [768], P(('dp', 'seq'))
- output_weight_grad: float32 [768, 768], P(('dp', 'seq'))
- output_bias_grad: float32 [768], P(('dp', 'seq'))
- first_gain_grad: float32 [768], P(('dp', 'seq'))
- first_shift_grad: float32 [768], P(('dp', 'seq'))
- inner_weight_grad: float32 [768, 3072], P(('dp', 'seq'))
- inner_bias_grad: float32 [3072], P(('dp', 'seq'))
- outer_weight_grad: float32 [3072, 768], P(('dp', 'seq'))
- outer_bias_grad: float32 [768], P(('dp', 'seq'))
- second_gain_grad: float32 [768], P(('dp', 'seq'))
- second_shift_grad: float32 [768], P(('dp', 'seq'))
The draws below stay inside these ranges and needn't reach their ends.
Inputs may be any that keep to these rules, and one draw needn't show every extreme that they name: Each row's 4 lengths add up to 512, and in every row the longest is exactly 448.
All inputs are finite; a program needn't handle non-finite values.
Results may differ from the reference program's by a relative error of at most 0.014.
The reference program's roundings to bfloat16 on the way count: a program that leaves them out, or rounds other values in their place, can miss the bound.
Values may be sent and summed in bfloat16 or wider, within the bound.
No kernel may reach another device: no remote copies, remote signals or barrier semaphores. Data moves between devices by JAX's collectives and lax.ppermute only.
A program may use at most 192 MiB of HBM per device.

```python
import math
import jax
import jax.numpy as jnp
import numpy as np
from jax import lax

D = 768
HEADS = 12
HEAD_DIM = 64
FF = 3072
L = 512
PAIRS = 4
ROWS = 64
LONGEST = 448


def block_scale(stream_key, extent, cuts, least, high):
    def one(dim, shards_of):
        draws = jax.random.uniform(jax.random.fold_in(jax.random.fold_in(stream_key, 6), dim), (shards_of,), jnp.float32, least / len(cuts), high / len(cuts))
        return jnp.repeat(jnp.exp(draws), extent[dim] // shards_of).reshape((-1,) + (1,) * (len(extent) - dim - 1))

    level = one(*cuts[0])
    for cut in cuts[1:]:
        level = level * one(*cut)
    return level


def length_profile(number_of, total, most, skew):
    weights = [(1 << 20) // math.isqrt(rank ** skew) + 1 for rank in range(2, number_of + 1)]
    spare, holding = total - most - (number_of - 1), [1] * (number_of - 1)
    while spare > 0:
        candidates = [i for i in range(number_of - 1) if holding[i] < most]
        whole, left = sum([weights[i] for i in candidates]), spare
        for i in candidates:
            extra = min(most - holding[i], max(1, left * weights[i] // whole), spare)
            holding[i] = holding[i] + extra
            spare = spare - extra
    return np.array([most] + holding)


def uneven(own_key, number_of, total, limit, skew):
    if number_of == 2:
        one = jax.random.randint(own_key, (), max(1, total - limit), min(limit, total - 1) + 1)
        return jnp.stack([one, total - one])
    sizes = jnp.asarray(length_profile(number_of, total, limit, skew), jnp.int32)
    couples = (number_of - 1) // 2
    giver, sink = sizes[1:1 + 2 * couples:2], sizes[2:2 + 2 * couples:2]
    margin = jnp.minimum(giver - 1, limit - sink)
    shifted = jax.random.randint(jax.random.fold_in(own_key, 1), (couples,), 0, 1 << 20) % (margin + 1)
    sizes = sizes.at[1:1 + 2 * couples:2].set(giver - shifted).at[2:2 + 2 * couples:2].set(sink + shifted)
    return sizes[jax.random.permutation(jax.random.fold_in(own_key, 2), number_of)]


def scatter_about(own_key, shape, spread, limit, cuts=(), held_as=jnp.bfloat16):
    drawn = spread * jax.random.normal(own_key, shape, jnp.float32)
    if cuts:
        drawn = drawn * block_scale(own_key, shape, cuts, -0.22, 0.18)
    return jnp.clip(drawn, -limit, limit).astype(held_as)


def setup_inputs(seed: int = 0) -> dict:
    key_list = jax.random.split(jax.random.key(seed), 17)
    tokens = scatter_about(key_list[0], (ROWS, L, D), 1.0, 6.0, ((0, 8), (1, 4)))
    cotangent = scatter_about(key_list[1], (ROWS, L, D), 1.0, 6.0, ((0, 8), (1, 4)))
    lengths = jax.vmap(lambda own: uneven(own, PAIRS, L, LONGEST, 1))(jax.random.split(key_list[2], ROWS)).reshape((ROWS, PAIRS)).astype(jnp.int32)
    packed_weight = scatter_about(key_list[3], (D, 3 * D), D ** -0.5, 0.21875, ((0, 32),), jnp.float32)
    query_bias = scatter_about(key_list[4], (D,), 0.5, 3.0, ((0, 32),), jnp.float32)
    value_bias = scatter_about(key_list[5], (D,), 0.5, 3.0, ((0, 32),), jnp.float32)
    output_weight = scatter_about(key_list[6], (D, D), (D // 128) ** -0.5, 2.5, ((0, 32),), jnp.float32)
    output_bias = scatter_about(key_list[7], (D,), 0.5, 3.0, ((0, 32),), jnp.float32)
    first_gain = jnp.clip(1.0 + 0.15 * jax.random.normal(key_list[8], (D,), jnp.float32), 0.25, 1.75)
    first_shift = scatter_about(key_list[9], (D,), 0.3, 2.0, ((0, 32),), jnp.float32)
    inner_weight = scatter_about(key_list[10], (D, FF), D ** -0.5, 0.21875, ((0, 32),), jnp.float32)
    inner_bias = scatter_about(key_list[11], (FF,), 0.5, 3.0, ((0, 32),), jnp.float32)
    outer_weight = scatter_about(key_list[12], (FF, D), FF ** -0.5, 0.109375, ((0, 32),), jnp.float32)
    outer_bias = scatter_about(key_list[13], (D,), 0.5, 3.0, ((0, 32),), jnp.float32)
    second_gain = jnp.clip(1.0 + 0.15 * jax.random.normal(key_list[14], (D,), jnp.float32), 0.25, 1.75)
    second_shift = scatter_about(key_list[15], (D,), 0.3, 2.0, ((0, 32),), jnp.float32)
    return {"tokens": tokens, "cotangent": cotangent, "lengths": lengths, "packed_weight": packed_weight, "query_bias": query_bias, "value_bias": value_bias, "output_weight": output_weight, "output_bias": output_bias, "first_gain": first_gain, "first_shift": first_shift, "inner_weight": inner_weight, "inner_bias": inner_bias, "outer_weight": outer_weight, "outer_bias": outer_bias, "second_gain": second_gain, "second_shift": second_shift}


@jax.custom_vjp
def low(v):
    return lax.optimization_barrier(v.astype(jnp.bfloat16)).astype(jnp.float32)

@jax.custom_vjp
def low_back(v):
    return v

def low_keep(v):
    return (low(v), None)

def low_pass(kept, grad):
    return (grad,)

def back_keep(v):
    return (v, None)

def back_low(kept, grad):
    return (low(grad),)
low.defvjp(low_keep, low_pass)
low_back.defvjp(back_keep, back_low)
EPSILON = 1e-06
HIGHEST = lax.Precision.HIGHEST

def pair_labels(lengths, length):
    bounds = jnp.cumsum(lengths, axis=-1).astype(jnp.int32)[..., :-1]
    places = jnp.arange(length, dtype=jnp.int32)
    return lax.optimization_barrier(jnp.sum((places[None, :, None] >= bounds[:, None, :]).astype(jnp.int32), axis=-1)).astype(jnp.int32)

def normalize(summed, gain, shift):
    average = lax.optimization_barrier(jnp.mean(summed, axis=-1, keepdims=True))
    centred = summed - average
    variance = lax.optimization_barrier(jnp.mean(centred * centred, axis=-1, keepdims=True))
    return centred * lax.rsqrt(variance + EPSILON) * gain + shift

def attend_row(pieces):
    packed, labels = pieces
    query_rows, key_rows, value_rows = (packed[:, 0], packed[:, 1], packed[:, 2])
    scores = jnp.einsum('qhd,khd->hqk', query_rows, key_rows, precision=HIGHEST) * HEAD_DIM ** (-0.5)
    scores = low_back(scores)
    allowed = labels[:, None] == labels[None, :]
    scores = jnp.where(allowed[None], scores, -1e+30)
    softmaxed = jax.nn.softmax(scores, axis=-1)
    context = jnp.einsum('hqk,khd->qhd', low(softmaxed), value_rows, precision=HIGHEST)
    return low(low_back(context))

def forward(tokens, packed_weight, query_bias, value_bias, output_weight, output_bias, first_gain, first_shift, inner_weight, inner_bias, outer_weight, outer_bias, second_gain, second_shift, labels):
    flat = tokens.reshape(-1, D)
    middle = jnp.zeros((D,), flat.dtype)
    bias_row = jnp.concatenate([low(query_bias), middle, low(value_bias)])
    mixed = jnp.dot(flat, low(packed_weight), precision=HIGHEST) + bias_row
    packed = low(low_back(mixed)).reshape(ROWS, L, 3, HEADS, HEAD_DIM)
    context = lax.map(jax.checkpoint(attend_row), (packed, labels)).reshape(-1, D)
    projected = low_back(jnp.dot(context, low(output_weight), precision=HIGHEST) + low(output_bias))
    hidden = normalize(flat + projected, low(first_gain), low(first_shift))
    inner = low_back(jnp.dot(low(hidden), low(inner_weight), precision=HIGHEST) + low(inner_bias))
    active = low(jax.nn.gelu(inner, approximate=False))
    branch = low_back(jnp.dot(active, low(outer_weight), precision=HIGHEST) + low(outer_bias))
    return normalize(hidden + branch, low(second_gain), low(second_shift)).reshape(ROWS, L, D)

def reference(tokens, cotangent, lengths, packed_weight, query_bias, value_bias, output_weight, output_bias, first_gain, first_shift, inner_weight, inner_bias, outer_weight, outer_bias, second_gain, second_shift):
    labels = pair_labels(lengths, L)
    params = (packed_weight, query_bias, value_bias, output_weight, output_bias, first_gain, first_shift, inner_weight, inner_bias, outer_weight, outer_bias, second_gain, second_shift)
    widened = [param.astype(jnp.float32) for param in params]

    def apply(*inputs):
        return forward(*inputs, labels)
    result, pullback = jax.vjp(apply, tokens.astype(jnp.float32), *widened)
    grads = pullback(cotangent.astype(jnp.float32))
    return (result.astype(jnp.bfloat16), grads[0], grads[1], grads[2], grads[3], grads[4], grads[5], grads[6], grads[7], grads[8], grads[9], grads[10], grads[11], grads[12], grads[13])
```

```python
from functools import partial

import jax
import jax.numpy as jnp
from jax import lax
from jax.sharding import PartitionSpec as P

HEAD_DIM = 64


EPSILON = 1e-06
AXES = ("dp", "seq")


def narrow(value):
    return value.astype(jnp.bfloat16)


def widen(value):
    return value.astype(jnp.float32)


def normalize(summed, gain, shift):
    average = jnp.mean(summed, axis=-1, keepdims=True)
    centred = summed - average
    variance = jnp.mean(centred * centred, axis=-1, keepdims=True)
    inverse = lax.rsqrt(variance + EPSILON)
    normed = centred * inverse
    return (normed * gain + shift, normed, inverse)


def normalize_back(upstream, normed, inverse, gain):
    scaled = upstream * gain
    first_mean = jnp.mean(scaled, axis=-1, keepdims=True)
    second_mean = jnp.mean(scaled * normed, axis=-1, keepdims=True)
    result = inverse * (scaled - first_mean - normed * second_mean)
    return (result, jnp.sum(upstream * normed, axis=0), jnp.sum(upstream, axis=0))


def masked_scores(query_rows, key_rows, labels):
    scale = query_rows.shape[-1] ** (-0.5)
    scores = (
        jnp.einsum("qhd,khd->hqk", query_rows, key_rows, preferred_element_type=jnp.float32) * scale
    )
    allowed = labels[:, None] == labels[None, :]
    return jnp.where(allowed[None], scores, -1e30)


def attend_forward(pieces):
    packed, labels = pieces
    query_rows, key_rows, value_rows = (packed[:, 0], packed[:, 1], packed[:, 2])
    scores = masked_scores(query_rows, key_rows, labels)
    highest = jnp.max(scores, axis=-1, keepdims=True)
    raised = jnp.exp(scores - highest)
    summed = jnp.sum(raised, axis=-1, keepdims=True)
    softmaxed = raised / summed
    context = jnp.einsum(
        "hqk,khd->qhd", narrow(softmaxed), value_rows, preferred_element_type=jnp.float32
    )
    return (narrow(context), (highest + jnp.log(summed))[..., 0])


def attend_backward(pieces):
    packed, labels, log_total, upstream = pieces
    query_rows, key_rows, value_rows = (packed[:, 0], packed[:, 1], packed[:, 2])
    scale = query_rows.shape[-1] ** (-0.5)
    scores = masked_scores(query_rows, key_rows, labels)
    softmaxed = jnp.exp(scores - log_total[..., None])
    value_grad = jnp.einsum(
        "hqk,qhd->khd", narrow(softmaxed), upstream, preferred_element_type=jnp.float32
    )
    prob_grad = jnp.einsum("qhd,khd->hqk", upstream, value_rows, preferred_element_type=jnp.float32)
    weighted = jnp.sum(softmaxed * prob_grad, axis=-1, keepdims=True)
    score_grad = narrow(softmaxed * (prob_grad - weighted))
    query_grad = (
        jnp.einsum("hqk,khd->qhd", score_grad, key_rows, preferred_element_type=jnp.float32) * scale
    )
    key_grad = (
        jnp.einsum("hqk,qhd->khd", score_grad, query_rows, preferred_element_type=jnp.float32)
        * scale
    )
    return narrow(jnp.stack([query_grad, key_grad, value_grad], axis=1))


def block_at(blocks, index, axis=0):
    return lax.dynamic_index_in_dim(blocks, index, axis, keepdims=False)


class Links:
    def __init__(self, mesh):
        self.dp, self.seq = mesh.shape["dp"], mesh.shape["seq"]
        self.bits = self.dp.bit_length() - 1
        assert self.dp == 1 << self.bits

    def along(self, value, step):
        pairs = [
            (d * self.seq + s, d * self.seq + (s + step) % self.seq)
            for d in range(self.dp)
            for s in range(self.seq)
        ]
        return lax.ppermute(value, AXES, pairs)

    def across(self, value, bit):
        pairs = [
            (d * self.seq + s, (d ^ (1 << bit)) * self.seq + s)
            for d in range(self.dp)
            for s in range(self.seq)
        ]
        return lax.ppermute(value, AXES, pairs)

    def digit(self, bit):
        return (lax.axis_index("dp") >> bit) & 1

    def orders(self):
        upward = list(range(1, self.bits))
        return upward, upward[::-1]

    def gather(self, shard, order):
        place = lax.axis_index("seq")
        held = jnp.zeros((self.seq,) + shard.shape, shard.dtype)
        held = lax.dynamic_update_index_in_dim(held, shard, place, 0)
        for step in range(1, self.seq):
            held = lax.dynamic_update_index_in_dim(
                held, self.along(shard, step), (place - step) % self.seq, 0
            )
        done = []
        for bit in order + [0]:
            axis = sum(other > bit for other in done)
            other = self.across(held, bit)
            mine = self.digit(bit)
            whole = jnp.zeros(held.shape[:axis] + (2,) + held.shape[axis:], held.dtype)
            whole = lax.dynamic_update_index_in_dim(whole, held, mine, axis)
            held = lax.dynamic_update_index_in_dim(whole, other, 1 - mine, axis)
            done.append(bit)
        return held.reshape(self.dp * self.seq * shard.shape[0], *shard.shape[1:])

    def reduce(self, whole, order):
        rows = whole.shape[0] // (self.dp * self.seq)
        held = whole.reshape((2,) * self.bits + (self.seq, rows) + whole.shape[1:])
        left = list(range(self.bits))[::-1]
        for bit in [0] + order:
            axis = left.index(bit)
            mine = self.digit(bit)
            other = self.across(block_at(held, 1 - mine, axis), bit)
            held = narrow(widen(block_at(held, mine, axis)) + widen(other))
            left.remove(bit)
        place = lax.axis_index("seq")
        total = widen(block_at(held, place))
        for step in range(1, self.seq):
            sent = block_at(held, (place + step) % self.seq)
            total = total + widen(self.along(sent, step))
        return total

    def to_rows(self, value):
        place = lax.axis_index("seq")
        blocks = value.reshape(self.seq, value.shape[0] // self.seq, *value.shape[1:])
        pieces = [block_at(blocks, place)]
        for step in range(1, self.seq):
            pieces.append(self.along(block_at(blocks, (place + step) % self.seq), step))
        return jnp.stack(pieces)

    def from_rows(self, value):
        place = lax.axis_index("seq")
        blocks = jnp.zeros_like(value)
        for step in range(self.seq):
            piece = value[step]
            if step:
                piece = self.along(piece, -step)
            blocks = lax.dynamic_update_index_in_dim(blocks, piece, (place + step) % self.seq, 0)
        return blocks.reshape(self.seq * value.shape[1], *value.shape[2:])


def columns(vectors, rows):
    block = jnp.concatenate([vector.reshape(rows, -1) for vector in vectors], axis=1)
    return jnp.pad(block, ((0, 0), (0, 128 - block.shape[1])))


def shards(
    links,
    tokens,
    cotangent,
    lengths,
    packed_weight,
    query_bias,
    value_bias,
    output_weight,
    output_bias,
    first_gain,
    first_shift,
    inner_weight,
    inner_bias,
    outer_weight,
    outer_bias,
    second_gain,
    second_shift,
):
    row_count, local_length, width = tokens.shape
    heads_all = width // HEAD_DIM
    seq = links.seq
    place = lax.axis_index("seq")
    rows = row_count // seq
    length = seq * local_length
    small = packed_weight.shape[0]
    first_order, second_order = links.orders()

    tokens_mine = links.to_rows(tokens)
    attention_vectors = columns(
        [narrow(v) for v in (query_bias, value_bias, output_bias, first_gain, first_shift)], small
    )
    half_one = links.gather(narrow(packed_weight[:, : 2 * width]), first_order)
    half_two = links.gather(
        jnp.concatenate(
            [narrow(packed_weight[:, 2 * width :]), narrow(output_weight), attention_vectors], axis=1
        ),
        second_order,
    )
    whole_packed = jnp.concatenate([half_one, half_two[:, :width]], axis=1)
    whole_output = half_two[:, width : 2 * width]
    vectors = widen(half_two[:, 2 * width : 2 * width + 8].T)
    whole_query, whole_value, whole_outbias, gain_one, shift_one = (vectors[i] for i in range(5))

    feed_vectors = columns(
        [narrow(v) for v in (outer_bias, second_gain, second_shift, inner_bias)], small
    )
    feed_one = links.gather(
        jnp.concatenate([narrow(inner_weight), feed_vectors], axis=1), first_order
    )
    whole_outer = links.gather(narrow(outer_weight), second_order)
    whole_inner = feed_one[:, : inner_weight.shape[1]]
    feed_rows = feed_one[:, inner_weight.shape[1] :]
    vectors = widen(feed_rows[:, :3].T)
    whole_outerbias, gain_two, shift_two = (vectors[i] for i in range(3))
    whole_innerbias = widen(feed_rows[:, 3 : 3 + inner_weight.shape[1] // width]).reshape(-1)

    starts = (place - jnp.arange(seq, dtype=jnp.int32)) % seq * local_length
    places = (starts[:, None] + jnp.arange(local_length, dtype=jnp.int32)[None]).reshape(-1)
    mine = lax.dynamic_slice_in_dim(lengths, place * rows, rows, 0)
    bounds = jnp.cumsum(mine, axis=-1)[..., :-1]
    labels = jnp.sum((places[None, :, None] >= bounds[:, None, :]).astype(jnp.int32), axis=-1)

    flat = tokens_mine.reshape(-1, width)
    middle = jnp.zeros((width,), jnp.float32)
    bias_row = jnp.concatenate([whole_query, middle, whole_value])
    mixed = jnp.dot(flat, whole_packed, preferred_element_type=jnp.float32) + bias_row
    packed = narrow(mixed).reshape(seq, rows, local_length, 3, heads_all, HEAD_DIM)
    spread_rows = packed.swapaxes(0, 1).reshape(rows, length, 3, heads_all, HEAD_DIM)
    context_rows, log_totals = lax.map(attend_forward, (spread_rows, labels))
    context = (
        context_rows.reshape(rows, seq, local_length, width).swapaxes(0, 1).reshape(-1, width)
    )
    projected = jnp.dot(context, whole_output, preferred_element_type=jnp.float32) + whole_outbias
    hidden, first_normed, first_inverse = normalize(widen(flat) + projected, gain_one, shift_one)
    hidden_low = narrow(hidden)
    inner = (
        jnp.dot(hidden_low, whole_inner, preferred_element_type=jnp.float32) + whole_innerbias
    )
    active = narrow(jax.nn.gelu(inner, approximate=False))
    branch = jnp.dot(active, whole_outer, preferred_element_type=jnp.float32) + whole_outerbias
    result, second_normed, second_inverse = normalize(hidden + branch, gain_two, shift_two)
    output = links.from_rows(narrow(result).reshape(seq, rows, local_length, width))

    upstream = widen(links.to_rows(cotangent)).reshape(-1, width)
    second_up, second_gain_grad, second_shift_grad = normalize_back(
        upstream, second_normed, second_inverse, gain_two
    )
    branch_grad = narrow(second_up)
    outer_weight_grad = narrow(
        jnp.einsum("tf,td->fd", active, branch_grad, preferred_element_type=jnp.float32)
    )
    outer_bias_grad = jnp.sum(widen(branch_grad), axis=0)
    active_grad = jnp.einsum(
        "td,fd->tf", branch_grad, whole_outer, preferred_element_type=jnp.float32
    )
    gelu_pull = jax.vjp(partial(jax.nn.gelu, approximate=False), inner)[1]
    inner_grad = narrow(gelu_pull(active_grad)[0])
    inner_weight_grad = narrow(
        jnp.einsum("td,tf->df", hidden_low, inner_grad, preferred_element_type=jnp.float32)
    )
    inner_bias_grad = jnp.sum(widen(inner_grad), axis=0)
    hidden_grad = second_up + jnp.einsum(
        "tf,df->td", inner_grad, whole_inner, preferred_element_type=jnp.float32
    )
    feed_sums = columns(
        [
            narrow(v)
            for v in (outer_bias_grad, second_gain_grad, second_shift_grad, inner_bias_grad)
        ],
        width,
    )
    feed_share = links.reduce(
        jnp.concatenate([inner_weight_grad, feed_sums], axis=1), first_order
    )
    outer_share = links.reduce(outer_weight_grad, second_order)

    first_up, first_gain_grad, first_shift_grad = normalize_back(
        hidden_grad, first_normed, first_inverse, gain_one
    )
    projected_grad = narrow(first_up)
    output_weight_grad = narrow(
        jnp.einsum("td,te->de", context, projected_grad, preferred_element_type=jnp.float32)
    )
    output_bias_grad = jnp.sum(widen(projected_grad), axis=0)
    context_grad = narrow(
        jnp.einsum("te,de->td", projected_grad, whole_output, preferred_element_type=jnp.float32)
    )
    context_grad_rows = (
        context_grad.reshape(seq, rows, local_length, width)
        .swapaxes(0, 1)
        .reshape(rows, length, heads_all, HEAD_DIM)
    )
    packed_grad_rows = lax.map(
        attend_backward, (spread_rows, labels, log_totals, context_grad_rows)
    )
    packed_grad = (
        packed_grad_rows.reshape(rows, seq, local_length, 3 * width)
        .swapaxes(0, 1)
        .reshape(-1, 3 * width)
    )
    packed_weight_grad = narrow(
        jnp.einsum("td,tc->dc", flat, packed_grad, preferred_element_type=jnp.float32)
    )
    column_sums = jnp.sum(widen(packed_grad), axis=0)
    tokens_grad = first_up + jnp.einsum(
        "tc,dc->td", packed_grad, whole_packed, preferred_element_type=jnp.float32
    )
    tokens_grad = widen(
        links.from_rows(narrow(tokens_grad).reshape(seq, rows, local_length, width))
    )
    attention_sums = columns(
        [
            narrow(v)
            for v in (
                column_sums[:width],
                column_sums[2 * width :],
                output_bias_grad,
                first_gain_grad,
                first_shift_grad,
            )
        ],
        width,
    )
    one_share = links.reduce(packed_weight_grad[:, : 2 * width], first_order)
    two_share = links.reduce(
        jnp.concatenate(
            [packed_weight_grad[:, 2 * width :], output_weight_grad, attention_sums], axis=1
        ),
        second_order,
    )
    feed = inner_weight.shape[1]
    wide = feed // width
    return (
        output,
        tokens_grad,
        jnp.concatenate([one_share, two_share[:, :width]], axis=1),
        two_share[:, 2 * width],
        two_share[:, 2 * width + 1],
        two_share[:, width : 2 * width],
        two_share[:, 2 * width + 2],
        two_share[:, 2 * width + 3],
        two_share[:, 2 * width + 4],
        feed_share[:, :feed],
        feed_share[:, feed + 3 : feed + 3 + wide].reshape(-1),
        outer_share,
        feed_share[:, feed],
        feed_share[:, feed + 1],
        feed_share[:, feed + 2],
    )


def solution(mesh):
    split = P(AXES)
    split_rows = P(AXES, None)
    packed_rows = P("dp", "seq", None)
    return jax.shard_map(
        partial(shards, Links(mesh)),
        mesh=mesh,
        in_specs=(
            packed_rows,
            packed_rows,
            P("dp", None),
            split_rows,
            split,
            split,
            split_rows,
            split,
            split,
            split,
            split_rows,
            split,
            split_rows,
            split,
            split,
            split,
        ),
        out_specs=(
            packed_rows,
            packed_rows,
            split_rows,
            split,
            split,
            split_rows,
            split,
            split,
            split,
            split_rows,
            split,
            split_rows,
            split,
            split,
            split,
        ),
        check_vma=False,
    )
```

```python
from functools import partial
import math

import jax
import jax.numpy as jnp
from jax import lax
from jax.experimental import pallas as pl
from jax.experimental.pallas import tpu as pltpu
from jax.sharding import PartitionSpec as P

HEAD_DIM = 64
LANES = 128
EPSILON = 1e-06
AXES = ("dp", "seq")
BF16, F32 = jnp.bfloat16, jnp.float32

NN = (((1,), (0,)), ((), ()))
NT = (((1,), (1,)), ((), ()))
TN = (((0,), (0,)), ((), ()))


def narrow(value):
    return value.astype(BF16)


def widen(value):
    return value.astype(F32)


def after(value, *others):
    return lax.optimization_barrier((value,) + others)[0]


def dot(left, right, dims=NN):
    return lax.dot_general(left, right, dims, preferred_element_type=F32)


def shape(dims, dtype=BF16):
    return jax.ShapeDtypeStruct(dims, dtype)


def whole_block(dims):
    return pl.BlockSpec(dims, lambda *_: (0,) * len(dims))


def row_sum(value):
    return jnp.sum(value, axis=0, keepdims=True)


def kernel(body, name, flops, touched, **options):
    return pl.pallas_call(
        body,
        name=name,
        compiler_params=pltpu.CompilerParams(vmem_limit_bytes=60 << 20),
        cost_estimate=pl.CostEstimate(flops=flops, bytes_accessed=touched, transcendentals=0),
        **options,
    )


def project_body(tokens, first, second, vectors, packed, rows):
    part = pl.program_id(0)
    turned = widen(vectors[...]).T

    @pl.when(part == 0)
    def _():
        rows[...] = turned[:8]
        packed[...] = narrow(dot(tokens[...], first[...]) + turned[0:1])

    @pl.when(part == 1)
    def _():
        packed[...] = narrow(dot(tokens[...], first[...]))

    @pl.when(part == 2)
    def _():
        packed[...] = narrow(dot(tokens[...], second[...]) + turned[1:2])


def project(tokens, first, second):
    count, width = tokens.shape
    square = (width, width)
    return kernel(
        project_body,
        "project",
        6 * count * width * width,
        8 * count * width,
        grid=(3,),
        in_specs=[
            whole_block(tokens.shape),
            pl.BlockSpec(square, lambda i: (0, jnp.minimum(i, 1))),
            pl.BlockSpec(square, lambda i: (0, 0)),
            pl.BlockSpec((width, LANES), lambda i: (0, 2 * width // LANES)),
        ],
        out_specs=[pl.BlockSpec((count, width), lambda i: (0, i)), whole_block((8, width))],
        out_shape=[shape((count, 3 * width)), shape((8, width), F32)],
    )(tokens, first, second, first)


def attend_body(labels_down, labels_along, query, key, value, context, probs, bias):
    @pl.when(pl.program_id(1) == 0)
    def _():
        bias[...] = jnp.where(labels_down[0] == labels_along[0], 0.0, -1e30)

    lane = lax.broadcasted_iota(jnp.int32, (1, LANES), 1)
    keys, values = key[0], value[0]
    queries = query[0] * BF16(HEAD_DIM**-0.5)
    parts = []
    for head in range(2):
        mine = (lane >= HEAD_DIM) == bool(head)
        scores = dot(jnp.where(mine, queries, BF16(0)), keys, NT) + bias[...]
        raised = jnp.exp(scores - jnp.max(scores, axis=-1, keepdims=True))
        total = jnp.sum(raised, axis=-1, keepdims=True)
        low = narrow(raised * (1.0 / total))
        probs[0, head] = low
        parts.append(dot(low, values))
    context[0] = narrow(jnp.where(lane < HEAD_DIM, parts[0], parts[1]))


def head_pair(length, offset):
    return pl.BlockSpec((1, length, LANES), lambda r, p: (r, 0, offset + p))


def attend(packed, labels):
    rows, length, _ = packed.shape
    width = packed.shape[2] // 3
    pairs = width // LANES
    return kernel(
        attend_body,
        "attend",
        rows * pairs * 16 * length * length * LANES,
        rows * pairs * 8 * length * length,
        grid=(rows, pairs),
        in_specs=[
            pl.BlockSpec((1, length, 1), lambda r, p: (r, 0, 0)),
            pl.BlockSpec((1, 1, length), lambda r, p: (r, 0, 0)),
            head_pair(length, 0),
            head_pair(length, pairs),
            head_pair(length, 2 * pairs),
        ],
        out_specs=[
            head_pair(length, 0),
            pl.BlockSpec((1, 2, length, length), lambda r, p: (r, p, 0, 0)),
        ],
        out_shape=[shape((rows, length, width)), shape((rows, 2 * pairs, length, length))],
        scratch_shapes=[pltpu.VMEM((length, length), F32)],
    )(labels[:, :, None], labels[:, None, :], packed, packed, packed)


def attend_back_body(query, key, value, upstream, probs, grads, sums):
    pair, pairs = pl.program_id(1), pl.num_programs(1)
    lane = lax.broadcasted_iota(jnp.int32, (1, LANES), 1)
    scale = BF16(HEAD_DIM**-0.5)
    queries, keys, values, up = query[0] * scale, key[0], value[0], upstream[0]
    scaled_keys = keys * scale
    query_parts, key_grad, value_grad = [], 0.0, 0.0
    for head in range(2):
        mine = (lane >= HEAD_DIM) == bool(head)
        up_mine = jnp.where(mine, up, BF16(0))
        queries_mine = jnp.where(mine, queries, BF16(0))
        low = probs[0, head]
        prob_grad = dot(up_mine, values, NT)
        softmaxed = widen(low)
        weighted = jnp.sum(softmaxed * prob_grad, axis=-1, keepdims=True)
        score_grad = narrow(softmaxed * (prob_grad - weighted))
        query_parts.append(dot(score_grad, scaled_keys))
        key_grad = key_grad + dot(queries_mine, score_grad, TN)
        value_grad = value_grad + dot(up_mine, low, TN)
    query_grad = jnp.where(lane < HEAD_DIM, query_parts[0], query_parts[1])
    for part, grad in enumerate((query_grad, key_grad.T, value_grad.T)):
        at = pl.ds(pl.multiple_of((part * pairs + pair) * LANES, LANES), LANES)
        rounded = narrow(grad)
        grads[0, :, at] = rounded
        sums[0, :, at] = row_sum(widen(rounded))


def attend_back(packed, probs, upstream):
    rows, length, wide = packed.shape
    pairs = wide // 3 // LANES
    return kernel(
        attend_back_body,
        "attend_back",
        rows * pairs * 16 * length * length * LANES,
        rows * pairs * 8 * length * length,
        grid=(rows, pairs),
        in_specs=[
            head_pair(length, 0),
            head_pair(length, pairs),
            head_pair(length, 2 * pairs),
            head_pair(length, 0),
            pl.BlockSpec((1, 2, length, length), lambda r, p: (r, p, 0, 0)),
        ],
        out_specs=[
            pl.BlockSpec((1, length, wide), lambda r, p: (r, 0, 0)),
            pl.BlockSpec((1, 1, wide), lambda r, p: (r, 0, 0)),
        ],
        out_shape=[shape((rows, length, wide)), shape((rows, 1, wide), F32)],
    )(packed, packed, packed, upstream, probs)


def normed_of(summed):
    centred = summed - jnp.mean(summed, axis=-1, keepdims=True)
    variance = jnp.mean(centred * centred, axis=-1, keepdims=True)
    inverse = lax.rsqrt(variance + EPSILON)
    return centred * inverse, inverse


def norm_back(upstream, normed, inverse, gain):
    scaled = upstream * gain
    first_mean = jnp.mean(scaled, axis=-1, keepdims=True)
    second_mean = jnp.mean(scaled * normed, axis=-1, keepdims=True)
    return inverse * (scaled - first_mean - normed * second_mean)


def settle_body(context, weight, tokens, rows, normed, inverse, low):
    summed = widen(tokens[...]) + dot(context[...], weight[...]) + rows[2:3]
    normed[...], inverse[...] = normed_of(summed)
    low[...] = narrow(normed[...] * rows[3:4] + rows[4:5])


def settle(context, second, tokens, rows):
    count, width = context.shape
    block = count // 4
    tall = pl.BlockSpec((block, width), lambda i: (i, 0))
    return kernel(
        settle_body,
        "settle",
        2 * count * width * width,
        10 * count * width,
        grid=(4,),
        in_specs=[
            tall,
            pl.BlockSpec((width, width), lambda i: (0, 1)),
            tall,
            whole_block(rows.shape),
        ],
        out_specs=[tall, pl.BlockSpec((block, 1), lambda i: (i, 0)), tall],
        out_shape=[shape((count, width), F32), shape((count, 1), F32), shape((count, width))],
    )(context, second, tokens, rows)


def feed_body(
    low, inner_weight, inner_bias, outer_weight, normed_one, rows_one, rows_two,
    active, slope, normed_two, inverse_two, *pieces_and_branch,
):
    pieces, branch = pieces_and_branch[:-1], pieces_and_branch[-1]
    step, steps = pl.program_id(0), pl.num_programs(0)
    inner = dot(low[...], inner_weight[...]) + inner_bias[...]
    share = 0.5 * (1.0 + lax.erf(inner * math.sqrt(0.5)))
    raised = jnp.exp(-0.5 * inner * inner) * (1.0 / math.sqrt(2.0 * math.pi))
    acted = narrow(inner * share)
    active[...] = acted
    slope[...] = narrow(share + inner * raised)
    part = dot(acted, outer_weight[...])

    @pl.when(step == 0)
    def _():
        branch[...] = part

    @pl.when(step > 0)
    def _():
        branch[...] += part

    @pl.when(step == steps - 1)
    def _():
        hidden = normed_one[...] * rows_one[3:4] + rows_one[4:5]
        normed_two[...], inverse_two[...] = normed_of(hidden + branch[...] + rows_two[0:1])
        result = narrow(normed_two[...] * rows_two[1:2] + rows_two[2:3])
        rows, places, width = pieces[0].shape
        result = result.reshape(rows, len(pieces), places, width)
        for index, piece in enumerate(pieces):
            piece[...] = result[:, index]


def feed(low, inner_weight, inner_bias, outer_weight, normed_one, rows_one, rows_two, piece, seq):
    count, width = low.shape
    wide = outer_weight.shape[0]
    block = 512
    all_of = whole_block((count, width))
    across = pl.BlockSpec((count, block), lambda f: (0, f))
    return kernel(
        feed_body,
        "feed",
        4 * count * width * wide,
        12 * count * wide,
        grid=(wide // block,),
        in_specs=[
            all_of,
            pl.BlockSpec((width, block), lambda f: (0, f)),
            pl.BlockSpec((1, block), lambda f: (0, f)),
            pl.BlockSpec((block, width), lambda f: (f, 0)),
            all_of,
            whole_block(rows_one.shape),
            whole_block(rows_two.shape),
        ],
        out_specs=[across, across, all_of, whole_block((count, 1))] + [whole_block(piece)] * seq,
        out_shape=[
            shape((count, wide)),
            shape((count, wide)),
            shape((count, width), F32),
            shape((count, 1), F32),
        ]
        + [shape(piece)] * seq,
        scratch_shapes=[pltpu.VMEM((count, width), F32)],
    )(low, inner_weight, inner_bias, outer_weight, normed_one, rows_one, rows_two)


def feed_back_body(
    cotangent, normed_two, inverse_two, rows_two, low, inner_weight, outer_weight, active, slope,
    inner_grad_out, inner_bias_out, outer_grad_out, hidden_grad, sums, up,
):
    step = pl.program_id(0)

    @pl.when(step == 0)
    def _():
        upstream = widen(cotangent[...])
        normed = normed_two[...]
        hidden_grad[...] = norm_back(upstream, normed, inverse_two[...], rows_two[1:2])
        up[...] = narrow(hidden_grad[...])
        sums[0:1] = row_sum(widen(up[...]))
        sums[1:2] = row_sum(upstream * normed)
        sums[2:3] = row_sum(upstream)
        sums[3:8] = jnp.zeros_like(sums[3:8])

    inner_grad = narrow(dot(up[...], outer_weight[...], NT) * widen(slope[...]))
    inner_bias_out[...] = row_sum(widen(inner_grad))
    outer_grad_out[...] = narrow(dot(active[...], up[...], TN))
    inner_grad_out[...] = narrow(dot(low[...], inner_grad, TN))
    hidden_grad[...] += dot(inner_grad, inner_weight[...], NT)


def feed_back(cotangent, normed_two, inverse_two, rows_two, low, inner_weight, outer_weight, active, slope):
    count, width = low.shape
    wide = outer_weight.shape[0]
    block = 512
    all_of = whole_block((count, width))
    across = pl.BlockSpec((count, block), lambda f: (0, f))
    right = pl.BlockSpec((width, block), lambda f: (0, f))
    down = pl.BlockSpec((block, width), lambda f: (f, 0))
    return kernel(
        feed_back_body,
        "feed_back",
        8 * count * width * wide,
        12 * count * wide,
        grid=(wide // block,),
        in_specs=[
            all_of,
            all_of,
            whole_block((count, 1)),
            whole_block(rows_two.shape),
            all_of,
            right,
            down,
            across,
            across,
        ],
        out_specs=[
            right,
            pl.BlockSpec((1, block), lambda f: (0, f)),
            down,
            all_of,
            whole_block((8, width)),
        ],
        out_shape=[
            shape((width, wide)),
            shape((1, wide), F32),
            shape((wide, width)),
            shape((count, width), F32),
            shape((8, width), F32),
        ],
        scratch_shapes=[pltpu.VMEM((count, width), BF16)],
    )(cotangent, normed_two, inverse_two, rows_two, low, inner_weight, outer_weight, active, slope)


def settle_back_body(
    hidden_grad, normed, inverse, rows, context, weight,
    first_up, context_grad, weight_grad, sums, total,
):
    step, steps = pl.program_id(0), pl.num_programs(0)

    @pl.when(step == 0)
    def _():
        sums[...] = jnp.zeros_like(sums)
        total[...] = jnp.zeros_like(total)

    upstream = hidden_grad[...]
    up = norm_back(upstream, normed[...], inverse[...], rows[3:4])
    first_up[...] = up
    low = narrow(up)
    context_grad[...] = narrow(dot(low, weight[...], NT))
    total[...] += dot(context[...], low, TN)
    sums[0:1] += row_sum(widen(low))
    sums[1:2] += row_sum(upstream * normed[...])
    sums[2:3] += row_sum(upstream)

    @pl.when(step == steps - 1)
    def _():
        weight_grad[...] = narrow(total[...])


def settle_back(hidden_grad, normed, inverse, rows, context, second):
    count, width = context.shape
    block = count // 2
    tall = pl.BlockSpec((block, width), lambda i: (i, 0))
    return kernel(
        settle_back_body,
        "settle_back",
        4 * count * width * width,
        16 * count * width,
        grid=(2,),
        in_specs=[
            tall,
            tall,
            pl.BlockSpec((block, 1), lambda i: (i, 0)),
            whole_block(rows.shape),
            tall,
            pl.BlockSpec((width, width), lambda i: (0, 1)),
        ],
        out_specs=[tall, tall, whole_block((width, width)), whole_block((8, width))],
        out_shape=[
            shape((count, width), F32),
            shape((count, width)),
            shape((width, width)),
            shape((8, width), F32),
        ],
        scratch_shapes=[pltpu.VMEM((width, width), F32)],
    )(hidden_grad, normed, inverse, rows, context, second)


def project_back_body(packed_grad, tokens, first, second, first_up, weight_grad, *pieces_and_total):
    pieces, total = pieces_and_total[:-1], pieces_and_total[-1]
    part = pl.program_id(0)
    grad = packed_grad[...]
    weight_grad[...] = narrow(dot(tokens[...], grad, TN))

    @pl.when(part == 0)
    def _():
        total[...] = first_up[...] + dot(grad, first[...], NT)

    @pl.when(part == 1)
    def _():
        total[...] += dot(grad, first[...], NT)

    @pl.when(part == 2)
    def _():
        result = narrow(total[...] + dot(grad, second[...], NT))
        rows, places, width = pieces[0].shape
        result = result.reshape(rows, len(pieces), places, width)
        for index, piece in enumerate(pieces):
            piece[...] = result[:, index]


def project_back(packed_grad, tokens, first, second, first_up, piece, seq):
    count, width = tokens.shape
    square = (width, width)
    return kernel(
        project_back_body,
        "project_back",
        12 * count * width * width,
        12 * count * width,
        grid=(3,),
        in_specs=[
            pl.BlockSpec((count, width), lambda i: (0, i)),
            whole_block(tokens.shape),
            pl.BlockSpec(square, lambda i: (0, jnp.minimum(i, 1))),
            pl.BlockSpec(square, lambda i: (0, 0)),
            whole_block(tokens.shape),
        ],
        out_specs=[pl.BlockSpec(square, lambda i: (0, i))] + [whole_block(piece)] * seq,
        out_shape=[shape((width, 3 * width))] + [shape(piece)] * seq,
        scratch_shapes=[pltpu.VMEM((count, width), F32)],
    )(packed_grad, tokens, first, second, first_up)


def block_at(blocks, index, axis=0):
    return lax.dynamic_index_in_dim(blocks, index, axis, keepdims=False)


class Links:
    def __init__(self, mesh):
        self.dp, self.seq = mesh.shape["dp"], mesh.shape["seq"]
        self.bits = self.dp.bit_length() - 1
        assert self.dp == 1 << self.bits
        upward = list(range(1, self.bits))
        self.orders = (upward, upward[::-1])

    def along(self, value, step):
        pairs = [
            (d * self.seq + s, d * self.seq + (s + step) % self.seq)
            for d in range(self.dp)
            for s in range(self.seq)
        ]
        return lax.ppermute(value, AXES, pairs)

    def across(self, value, bit):
        pairs = [
            (d * self.seq + s, (d ^ (1 << bit)) * self.seq + s)
            for d in range(self.dp)
            for s in range(self.seq)
        ]
        return lax.ppermute(value, AXES, pairs)

    def digit(self, bit):
        return (lax.axis_index("dp") >> bit) & 1

    def gather_seq(self, shard):
        place = lax.axis_index("seq")
        held = jnp.zeros((self.seq,) + shard.shape, shard.dtype)
        held = lax.dynamic_update_index_in_dim(held, shard, place, 0)
        for step in range(1, self.seq):
            held = lax.dynamic_update_index_in_dim(
                held, self.along(shard, step), (place - step) % self.seq, 0
            )
        return held

    def gather_digit(self, held, bit, done):
        axis = sum(other > bit for other in done)
        other = self.across(held, bit)
        mine = self.digit(bit)
        return jnp.where(
            mine == 0, jnp.stack([held, other], axis=axis), jnp.stack([other, held], axis=axis)
        )

    def flat(self, held):
        return held.reshape(-1, held.shape[-1])

    def spread(self, whole):
        rows = whole.shape[0] // (self.dp * self.seq)
        return whole.reshape((2,) * self.bits + (self.seq, rows) + whole.shape[1:])

    def reduce_digit(self, held, bit, done):
        axis = sum(1 for other in range(bit + 1, self.bits) if other not in done)
        mine = self.digit(bit)
        other = self.across(block_at(held, 1 - mine, axis), bit)
        return narrow(widen(block_at(held, mine, axis)) + widen(other))

    def reduce_seq(self, held):
        place = lax.axis_index("seq")
        total = widen(block_at(held, place))
        for step in range(1, self.seq):
            sent = block_at(held, (place + step) % self.seq)
            total = total + widen(self.along(sent, step))
        return total

    def to_rows(self, value, *others):
        place = lax.axis_index("seq")
        blocks = value.reshape(self.seq, value.shape[0] // self.seq, *value.shape[1:])
        pieces = [block_at(blocks, place)]
        sent = [block_at(blocks, (place + step) % self.seq) for step in range(1, self.seq)]
        if others:
            sent = [after(piece, *others) for piece in sent]
        for step in range(1, self.seq):
            pieces.append(self.along(sent[step - 1], step))
        return jnp.concatenate(pieces, axis=1)

    def from_rows(self, pieces):
        return [pieces[0]] + [self.along(pieces[step], -step) for step in range(1, self.seq)]

    def placed(self, pieces):
        place = lax.axis_index("seq")
        blocks = jnp.zeros((self.seq,) + pieces[0].shape, pieces[0].dtype)
        for step, piece in enumerate(pieces):
            blocks = lax.dynamic_update_index_in_dim(blocks, piece, (place + step) % self.seq, 0)
        return blocks.reshape(self.seq * pieces[0].shape[0], *pieces[0].shape[1:])


def columns(vectors, rows):
    block = jnp.concatenate([vector.reshape(rows, -1) for vector in vectors], axis=1)
    return jnp.pad(block, ((0, 0), (0, LANES - block.shape[1])))


def shards(
    links,
    tokens,
    cotangent,
    lengths,
    packed_weight,
    query_bias,
    value_bias,
    output_weight,
    output_bias,
    first_gain,
    first_shift,
    inner_weight,
    inner_bias,
    outer_weight,
    outer_bias,
    second_gain,
    second_shift,
):
    row_count, local_length, width = tokens.shape
    seq = links.seq
    place = lax.axis_index("seq")
    rows = row_count // seq
    length = seq * local_length
    small = packed_weight.shape[0]
    feed_width = inner_weight.shape[1]
    wide = feed_width // width
    piece = (rows, local_length, width)
    order_a, order_b = links.orders

    attention_vectors = columns(
        [narrow(v) for v in (query_bias, value_bias, output_bias, first_gain, first_shift)], small
    )
    attention_shard = jnp.concatenate(
        [
            narrow(packed_weight[:, : 2 * width]),
            attention_vectors,
            narrow(packed_weight[:, 2 * width :]),
            narrow(output_weight),
        ],
        axis=1,
    )
    cut = 2 * width + LANES
    held = links.gather_seq(attention_shard)
    tokens_mine = links.to_rows(tokens, held)
    first, second = held[..., :cut], held[..., cut:]
    for index in range(links.bits - 1):
        first = links.gather_digit(first, order_a[index], order_a[:index])
        second = links.gather_digit(second, order_b[index], order_b[:index])
        if index == 0:
            feed_shard = jnp.concatenate(
                [
                    narrow(inner_weight),
                    columns(
                        [narrow(v) for v in (outer_bias, second_gain, second_shift, inner_bias)],
                        small,
                    ),
                ],
                axis=1,
            )
            feed_shard, outer_shard = after(feed_shard, first), after(narrow(outer_weight), first)
            feed_first = links.gather_seq(feed_shard)
            feed_second = links.gather_seq(outer_shard)
    first = links.flat(links.gather_digit(first, 0, order_a))
    second = links.flat(links.gather_digit(second, 0, order_b))

    starts = (place - jnp.arange(seq, dtype=jnp.int32)) % seq * local_length
    places = (starts[:, None] + jnp.arange(local_length, dtype=jnp.int32)[None]).reshape(-1)
    mine = lax.dynamic_slice_in_dim(lengths, place * rows, rows, 0)
    bounds = jnp.cumsum(mine, axis=-1)[..., :-1]
    labels = jnp.sum((places[None, :, None] >= bounds[:, None, :]).astype(jnp.int32), axis=-1)

    flat = tokens_mine.reshape(-1, width)
    feed_first = links.gather_digit(feed_first, order_a[0], [])
    feed_second = links.gather_digit(feed_second, order_b[0], [])
    flat = after(flat, feed_first, feed_second)
    packed, rows_one = project(flat, first, second)
    packed = packed.reshape(rows, length, 3 * width)
    cotangent_mine = links.to_rows(cotangent, packed).reshape(-1, width)
    feed_first, feed_second = after(feed_first, packed), after(feed_second, packed)
    for index in range(1, links.bits - 1):
        feed_first = links.gather_digit(feed_first, order_a[index], order_a[:index])
        feed_second = links.gather_digit(feed_second, order_b[index], order_b[:index])
    context, probs = attend(packed, labels)
    context = context.reshape(-1, width)
    normed_one, inverse_one, low = settle(context, second, flat, rows_one)
    feed_first, feed_second = after(feed_first, low), after(feed_second, low)
    feed_first = links.flat(links.gather_digit(feed_first, 0, order_a))
    feed_second = links.flat(links.gather_digit(feed_second, 0, order_b))
    feed_vectors = widen(feed_first[:, feed_width:])
    rows_two = feed_vectors[:, :8].T
    inner_row = feed_vectors[:, 3 : 3 + wide].reshape(1, -1)

    active, slope, normed_two, inverse_two, *pieces = feed(
        low, feed_first, inner_row, feed_second, normed_one, rows_one, rows_two, piece, seq
    )
    output = links.placed(links.from_rows(pieces))

    inner_grad, inner_bias_grad, outer_grad, hidden_grad, feed_sums = feed_back(
        cotangent_mine, normed_two, inverse_two, rows_two, low, feed_first, feed_second, active, slope
    )
    feed_columns = columns(
        [narrow(v) for v in (feed_sums[0], feed_sums[1], feed_sums[2], inner_bias_grad)], width
    )
    feed_first = links.reduce_digit(
        links.spread(jnp.concatenate([inner_grad, feed_columns], axis=1)), 0, []
    )
    feed_second = links.reduce_digit(links.spread(outer_grad), 0, [])

    first_up, context_grad, output_grad, attention_sums = settle_back(
        hidden_grad, normed_one, inverse_one, rows_one, context, second
    )
    context_grad = after(context_grad, feed_first, feed_second, output)
    packed_grad, packed_sums = attend_back(
        packed, probs, context_grad.reshape(rows, length, width)
    )
    feed_first = links.reduce_digit(feed_first, order_a[0], [0])
    feed_second = links.reduce_digit(feed_second, order_b[0], [0])
    packed_grad = after(packed_grad, feed_first, feed_second)
    packed_weight_grad, *pieces = project_back(
        packed_grad.reshape(-1, 3 * width), flat, first, second, first_up, piece, seq
    )
    pieces = links.from_rows(pieces)
    for index in range(1, links.bits - 1):
        feed_first = links.reduce_digit(feed_first, order_a[index], [0] + order_a[:index])
        feed_second = links.reduce_digit(feed_second, order_b[index], [0] + order_b[:index])

    packed_sums = jnp.sum(packed_sums, axis=(0, 1))
    attention_columns = columns(
        [
            narrow(v)
            for v in (
                packed_sums[:width],
                packed_sums[2 * width :],
                attention_sums[0],
                attention_sums[1],
                attention_sums[2],
            )
        ],
        width,
    )
    first = links.spread(
        jnp.concatenate([packed_weight_grad[:, : 2 * width], attention_columns], axis=1)
    )
    second = links.spread(
        jnp.concatenate([packed_weight_grad[:, 2 * width :], output_grad], axis=1)
    )
    order_a, order_b = [0] + order_a, [0] + order_b
    for index in range(links.bits):
        first = links.reduce_digit(first, order_a[index], order_a[:index])
        second = links.reduce_digit(second, order_b[index], order_b[:index])
    feed_first, feed_second = links.reduce_seq(feed_first), links.reduce_seq(feed_second)
    tokens_grad = widen(links.placed(pieces))
    first, second = links.reduce_seq(first), links.reduce_seq(second)
    return (
        output,
        tokens_grad,
        jnp.concatenate([first[:, : 2 * width], second[:, :width]], axis=1),
        first[:, 2 * width],
        first[:, 2 * width + 1],
        second[:, width:],
        first[:, 2 * width + 2],
        first[:, 2 * width + 3],
        first[:, 2 * width + 4],
        feed_first[:, :feed_width],
        feed_first[:, feed_width + 3 : feed_width + 3 + wide].reshape(-1),
        feed_second,
        feed_first[:, feed_width],
        feed_first[:, feed_width + 1],
        feed_first[:, feed_width + 2],
    )


def solution(mesh):
    split = P(AXES)
    split_rows = P(AXES, None)
    packed_rows = P("dp", "seq", None)
    return jax.shard_map(
        partial(shards, Links(mesh)),
        mesh=mesh,
        in_specs=(
            packed_rows,
            packed_rows,
            P("dp", None),
            split_rows,
            split,
            split,
            split_rows,
            split,
            split,
            split,
            split_rows,
            split,
            split_rows,
            split,
            split,
            split,
        ),
        out_specs=(
            packed_rows,
            packed_rows,
            split_rows,
            split,
            split,
            split_rows,
            split,
            split,
            split,
            split_rows,
            split,
            split_rows,
            split,
            split,
            split,
        ),
        check_vma=False,
    )
```

```python
from functools import partial
import math

import jax
import jax.numpy as jnp
from jax import lax
from jax.experimental import pallas as pl
from jax.experimental.pallas import tpu as pltpu
from jax.sharding import PartitionSpec as P

HEAD_DIM = 64
LANES = 128
STEPS = 4
EPSILON = 1e-06
AXES = ("dp", "seq")
BF16, F32 = jnp.bfloat16, jnp.float32

NN = (((1,), (0,)), ((), ()))
NT = (((1,), (1,)), ((), ()))
TN = (((0,), (0,)), ((), ()))


def narrow(value):
    return value.astype(BF16)


def widen(value):
    return value.astype(F32)


def after(value, *others):
    return lax.optimization_barrier((value,) + others)[0]


def dot(left, right, dims=NN):
    return lax.dot_general(left, right, dims, preferred_element_type=F32)


def shape(dims, dtype=BF16):
    return jax.ShapeDtypeStruct(dims, dtype)


def like(value):
    return jax.ShapeDtypeStruct(value.shape, value.dtype)


def fixed(dims, *index):
    at = tuple(index) or (0,) * len(dims)
    return pl.BlockSpec(dims, lambda *_: at)


SCALARS = pl.BlockSpec(memory_space=pltpu.SMEM)
ANYWHERE = pl.BlockSpec(memory_space=pl.ANY)


def row_sum(value):
    return jnp.sum(value, axis=0, keepdims=True)


def kernel(body, name, flops, touched, **options):
    return pl.pallas_call(
        body,
        name=name,
        compiler_params=pltpu.CompilerParams(vmem_limit_bytes=60 << 20),
        cost_estimate=pl.CostEstimate(flops=flops, bytes_accessed=touched, transcendentals=0),
        **options,
    )


def unite(target, own, other, side):
    count, rows = own.shape[:2]
    for index in range(count):
        for half, value in ((side, own), (1 - side, other)):
            start = pl.multiple_of((2 * index + half) * rows, rows)
            target[pl.ds(start, rows), :] = value[index]


def divide(source, keep, send, side, columns):
    count, rows = keep.shape[:2]
    for index in range(count):
        for half, target in ((side, keep), (1 - side, send)):
            start = pl.multiple_of((2 * index + half) * rows, rows)
            target[index, :, columns] = source[pl.ds(start, rows), :]


def as_columns(rows):
    width = rows[0].shape[1]
    padding = jnp.zeros((LANES - len(rows), width), F32)
    return jnp.concatenate(list(rows) + [padding], axis=0).T


def project_body(
    spots, tokens, own_first, other_first, own_second, other_second, own_vectors, other_vectors,
    packed, rows, weight, vectors,
):
    part, side = pl.program_id(0), spots[1]

    @pl.when(part == 0)
    def _():
        unite(vectors, own_vectors, other_vectors, side)
        rows[...] = widen(vectors[...]).T[:8]

    @pl.when(part < 2)
    def _():
        unite(weight, own_first, other_first, side)

    @pl.when(part == 2)
    def _():
        unite(weight, own_second, other_second, side)

    query, value = rows[0:1], rows[1:2]
    bias = jnp.where(part == 0, query, jnp.where(part == 2, value, jnp.zeros_like(query)))
    packed[...] = narrow(dot(tokens[...], weight[...]) + bias)


def project(spots, tokens, first, second):
    count, width = tokens.shape
    parts, rows, _ = first[0].shape
    pick = pl.BlockSpec((parts, rows, width), lambda i: (0, 0, jnp.minimum(i, 1)))
    value = fixed((parts, rows, width))
    vectors = fixed((parts, rows, LANES), 0, 0, 2 * width // LANES)
    return kernel(
        project_body,
        "project",
        6 * count * width * width,
        8 * count * width,
        grid=(3,),
        in_specs=[SCALARS, fixed(tokens.shape), pick, pick, value, value, vectors, vectors],
        out_specs=[pl.BlockSpec((count, width), lambda i: (0, i)), fixed((8, width))],
        out_shape=[shape((count, 3 * width)), shape((8, width), F32)],
        scratch_shapes=[pltpu.VMEM((width, width), BF16), pltpu.VMEM((width, LANES), BF16)],
    )(spots, tokens, *first, *second, *first)


def pair_labels(places, lengths, row):
    label, bound = jnp.zeros_like(places), 0
    for pair in range(lengths.shape[1] - 1):
        bound = bound + lengths[row, pair]
        label = label + (places >= bound).astype(jnp.int32)
    return label


def row_of(block):
    return block[...].reshape(-1, block.shape[-1])


def attend_body(spots, lengths, query, key, value, context, probs, bias):
    length = bias.shape[0]

    @pl.when(pl.program_id(1) == 0)
    def _():
        row = spots[0] * pl.num_programs(0) + pl.program_id(0)
        down = pair_labels(lax.broadcasted_iota(jnp.int32, (length, 1), 0), lengths, row)
        along = pair_labels(lax.broadcasted_iota(jnp.int32, (1, length), 1), lengths, row)
        bias[...] = jnp.where(down == along, 0.0, -1e30)

    lane = lax.broadcasted_iota(jnp.int32, (1, LANES), 1)
    keys, values = row_of(key), row_of(value)
    queries = row_of(query) * BF16(HEAD_DIM**-0.5)
    parts = []
    for head in range(2):
        mine = (lane >= HEAD_DIM) == bool(head)
        scores = dot(jnp.where(mine, queries, BF16(0)), keys, NT) + bias[...]
        raised = jnp.exp(scores - jnp.max(scores, axis=-1, keepdims=True))
        total = jnp.sum(raised, axis=-1, keepdims=True)
        low = narrow(raised * (1.0 / total))
        probs[0, head] = low
        parts.append(dot(low, values))
    result = narrow(jnp.where(lane < HEAD_DIM, parts[0], parts[1]))
    context[...] = result.reshape(context.shape)


def head_pair(seq, places, offset):
    return pl.BlockSpec((seq, 1, places, LANES), lambda r, p: (0, r, 0, offset + p))


def attend(spots, lengths, packed):
    seq, rows, places, wide = packed.shape
    length, pairs = seq * places, wide // 3 // LANES
    return kernel(
        attend_body,
        "attend",
        rows * pairs * 16 * length * length * LANES,
        rows * pairs * 8 * length * length,
        grid=(rows, pairs),
        in_specs=[
            SCALARS,
            SCALARS,
            head_pair(seq, places, 0),
            head_pair(seq, places, pairs),
            head_pair(seq, places, 2 * pairs),
        ],
        out_specs=[
            head_pair(seq, places, 0),
            pl.BlockSpec((1, 2, length, length), lambda r, p: (r, p, 0, 0)),
        ],
        out_shape=[shape((seq, rows, places, wide // 3)), shape((rows, 2 * pairs, length, length))],
        scratch_shapes=[pltpu.VMEM((length, length), F32)],
    )(spots, lengths, packed, packed, packed)


def attend_back_body(query, key, value, upstream, probs, grads, sums):
    pair, pairs = pl.program_id(1), pl.num_programs(1)
    lane = lax.broadcasted_iota(jnp.int32, (1, LANES), 1)
    scale = BF16(HEAD_DIM**-0.5)
    queries, keys, values, up = row_of(query) * scale, row_of(key), row_of(value), row_of(upstream)
    scaled_keys = keys * scale
    query_parts, key_grad, value_grad = [], 0.0, 0.0
    for head in range(2):
        mine = (lane >= HEAD_DIM) == bool(head)
        up_mine = jnp.where(mine, up, BF16(0))
        queries_mine = jnp.where(mine, queries, BF16(0))
        low = probs[0, head]
        prob_grad = dot(up_mine, values, NT)
        softmaxed = widen(low)
        weighted = jnp.sum(softmaxed * prob_grad, axis=-1, keepdims=True)
        score_grad = narrow(softmaxed * (prob_grad - weighted))
        query_parts.append(dot(score_grad, scaled_keys))
        key_grad = key_grad + dot(queries_mine, score_grad, TN)
        value_grad = value_grad + dot(up_mine, low, TN)
    query_grad = jnp.where(lane < HEAD_DIM, query_parts[0], query_parts[1])
    for part, grad in enumerate((query_grad, key_grad.T, value_grad.T)):
        at = pl.ds(pl.multiple_of((part * pairs + pair) * LANES, LANES), LANES)
        rounded = narrow(grad)
        grads[:, :, :, at] = rounded.reshape(grads.shape[:3] + (LANES,))
        sums[0, :, at] = row_sum(widen(rounded))


def attend_back(packed, probs, upstream):
    seq, rows, places, wide = packed.shape
    length, pairs = seq * places, wide // 3 // LANES
    return kernel(
        attend_back_body,
        "attend_back",
        rows * pairs * 16 * length * length * LANES,
        rows * pairs * 8 * length * length,
        grid=(rows, pairs),
        in_specs=[
            head_pair(seq, places, 0),
            head_pair(seq, places, pairs),
            head_pair(seq, places, 2 * pairs),
            head_pair(seq, places, 0),
            pl.BlockSpec((1, 2, length, length), lambda r, p: (r, p, 0, 0)),
        ],
        out_specs=[
            pl.BlockSpec((seq, 1, places, wide), lambda r, p: (0, r, 0, 0)),
            pl.BlockSpec((1, 1, wide), lambda r, p: (r, 0, 0)),
        ],
        out_shape=[shape(packed.shape), shape((rows, 1, wide), F32)],
    )(packed, packed, packed, upstream, probs)


def normed_of(summed):
    centred = summed - jnp.mean(summed, axis=-1, keepdims=True)
    variance = jnp.mean(centred * centred, axis=-1, keepdims=True)
    inverse = lax.rsqrt(variance + EPSILON)
    return centred * inverse, inverse


def norm_back(upstream, normed, inverse, gain):
    scaled = upstream * gain
    first_mean = jnp.mean(scaled, axis=-1, keepdims=True)
    second_mean = jnp.mean(scaled * normed, axis=-1, keepdims=True)
    return inverse * (scaled - first_mean - normed * second_mean)


def settle_body(spots, context, own, other, tokens, rows, normed, inverse, low, weight):
    @pl.when(pl.program_id(0) == 0)
    def _():
        unite(weight, own, other, spots[1])

    summed = widen(tokens[...]) + dot(context[...], weight[...]) + rows[2:3]
    normed[...], inverse[...] = normed_of(summed)
    low[...] = narrow(normed[...] * rows[3:4] + rows[4:5])


def settle(spots, context, second, tokens, rows):
    count, width = context.shape
    block = count // 4
    tall = pl.BlockSpec((block, width), lambda i: (i, 0))
    half = fixed(second[0].shape[:2] + (width,), 0, 0, 1)
    return kernel(
        settle_body,
        "settle",
        2 * count * width * width,
        10 * count * width,
        grid=(4,),
        in_specs=[SCALARS, tall, half, half, tall, fixed(rows.shape)],
        out_specs=[tall, pl.BlockSpec((block, 1), lambda i: (i, 0)), tall],
        out_shape=[shape((count, width), F32), shape((count, 1), F32), shape((count, width))],
        scratch_shapes=[pltpu.VMEM((width, width), BF16)],
    )(spots, context, *second, tokens, rows)


def spread_mask(rows, per, column):
    down = lax.broadcasted_iota(jnp.int32, (rows, rows * per), 0)
    along = lax.broadcasted_iota(jnp.int32, (rows, rows * per), 1)
    return along == down * per + column


def feed_body(
    spots, low, own_inner, other_inner, own_outer, other_outer, own_vectors, other_vectors,
    normed_one, rows_one,
    active, slope, normed_two, inverse_two, rows_two, output,
    branch, inner_weight, outer_weight, vectors,
):
    step, steps, side = pl.program_id(0), pl.num_programs(0), spots[1]

    @pl.when(step == 0)
    def _():
        unite(vectors, own_vectors, other_vectors, side)
        rows_two[...] = widen(vectors[...]).T[:8]

    unite(inner_weight, own_inner, other_inner, side)
    unite(outer_weight, own_outer, other_outer, side)
    block = inner_weight.shape[1]
    share_rows = vectors.shape[0] // STEPS
    per = block // share_rows
    own_rows = vectors[pl.ds(pl.multiple_of(step * share_rows, share_rows), share_rows), :]
    bias = 0.0
    for column in range(per):
        value = widen(own_rows[:, 3 + column : 4 + column])
        bias = bias + jnp.where(spread_mask(share_rows, per, column), value, 0.0)
    inner = dot(low[...], inner_weight[...]) + row_sum(bias)
    share = 0.5 * (1.0 + lax.erf(inner * math.sqrt(0.5)))
    raised = jnp.exp(-0.5 * inner * inner) * (1.0 / math.sqrt(2.0 * math.pi))
    acted = narrow(inner * share)
    active[...] = acted
    slope[...] = narrow(share + inner * raised)
    part = dot(acted, outer_weight[...])

    @pl.when(step == 0)
    def _():
        branch[...] = part

    @pl.when(step > 0)
    def _():
        branch[...] += part

    @pl.when(step == steps - 1)
    def _():
        hidden = normed_one[...] * rows_one[3:4] + rows_one[4:5]
        normed_two[...], inverse_two[...] = normed_of(hidden + branch[...] + rows_two[0:1])
        output[...] = narrow(normed_two[...] * rows_two[1:2] + rows_two[2:3])


def feed_specs(width, inner, outer):
    parts, rows, _ = inner[0].shape
    block = outer[0].shape[0] * outer[0].shape[1] * 2 // STEPS
    right = pl.BlockSpec((parts, rows, block), lambda f: (0, 0, f))
    down = pl.BlockSpec((outer[0].shape[0] // STEPS, outer[0].shape[1], width), lambda f: (f, 0, 0))
    return block, right, down


def feed(spots, low, inner, outer, normed_one, rows_one):
    count, width = low.shape
    block, right, down = feed_specs(width, inner, outer)
    wide = block * STEPS
    all_of = fixed((count, width))
    across = pl.BlockSpec((count, block), lambda f: (0, f))
    vectors = fixed(inner[0].shape[:2] + (LANES,), 0, 0, wide // LANES)
    return kernel(
        feed_body,
        "feed",
        4 * count * width * wide,
        12 * count * wide,
        grid=(STEPS,),
        in_specs=[SCALARS, all_of, right, right, down, down, vectors, vectors, all_of]
        + [fixed(rows_one.shape)],
        out_specs=[across, across, all_of, fixed((count, 1)), fixed((8, width)), all_of],
        out_shape=[
            shape((count, wide)),
            shape((count, wide)),
            shape((count, width), F32),
            shape((count, 1), F32),
            shape((8, width), F32),
            shape((count, width)),
        ],
        scratch_shapes=[
            pltpu.VMEM((count, width), F32),
            pltpu.VMEM((width, block), BF16),
            pltpu.VMEM((block, width), BF16),
            pltpu.VMEM((width, LANES), BF16),
        ],
    )(spots, low, *inner, *outer, *inner, normed_one, rows_one)


def feed_back_body(
    spots, cotangent, normed_two, inverse_two, rows_two, low,
    own_inner, other_inner, own_outer, other_outer, active, slope,
    keep_inner, send_inner, keep_outer, send_outer, hidden_grad,
    up, inner_weight, outer_weight, made, columns,
):
    step, steps, side = pl.program_id(0), pl.num_programs(0), spots[1]
    block = inner_weight.shape[1]

    @pl.when(step == 0)
    def _():
        upstream = widen(cotangent[...])
        normed = normed_two[...]
        hidden_grad[...] = norm_back(upstream, normed, inverse_two[...], rows_two[1:2])
        up[...] = narrow(hidden_grad[...])
        columns[...] = as_columns(
            (row_sum(widen(up[...])), row_sum(upstream * normed), row_sum(upstream))
        )

    unite(inner_weight, own_inner, other_inner, side)
    unite(outer_weight, own_outer, other_outer, side)
    inner_grad = narrow(dot(up[...], outer_weight[...], NT) * widen(slope[...]))
    made[...] = narrow(dot(low[...], inner_grad, TN))
    at = pl.ds(pl.multiple_of(step * block, block), block)
    divide(made, keep_inner, send_inner, side, at)
    hidden_grad[...] += dot(inner_grad, inner_weight[...], NT)
    outer_weight[...] = narrow(dot(active[...], up[...], TN))
    divide(outer_weight, keep_outer, send_outer, side, slice(None))

    bias = row_sum(widen(inner_grad))
    share_rows = columns.shape[0] // STEPS
    per = block // share_rows
    lane = lax.broadcasted_iota(jnp.int32, (1, LANES), 1)
    total = 0.0
    for column in range(per):
        value = jnp.sum(
            jnp.where(spread_mask(share_rows, per, column), bias, 0.0), axis=1, keepdims=True
        )
        total = total + jnp.where(lane == 3 + column, value, 0.0)
    columns[pl.ds(pl.multiple_of(step * share_rows, share_rows), share_rows), :] += total

    @pl.when(step == steps - 1)
    def _():
        made[:, :LANES] = narrow(columns[...])
        count, rows, wide = keep_inner.shape
        for index in range(count):
            for half, target in ((side, keep_inner), (1 - side, send_inner)):
                start = pl.multiple_of((2 * index + half) * rows, rows)
                target[index, :, wide - LANES :] = made[pl.ds(start, rows), :LANES]


def feed_back(spots, cotangent, normed_two, inverse_two, rows_two, low, inner, outer, active, slope):
    count, width = low.shape
    block, right, down = feed_specs(width, inner, outer)
    wide = block * STEPS
    all_of = fixed((count, width))
    across = pl.BlockSpec((count, block), lambda f: (0, f))
    return kernel(
        feed_back_body,
        "feed_back",
        8 * count * width * wide,
        12 * count * wide,
        grid=(STEPS,),
        in_specs=[SCALARS, all_of, all_of, fixed((count, 1)), fixed((8, width)), all_of]
        + [right, right, down, down, across, across],
        out_specs=[fixed(inner[0].shape), fixed(inner[0].shape), down, down, all_of],
        out_shape=[like(inner[0]), like(inner[0]), like(outer[0]), like(outer[0])]
        + [shape((count, width), F32)],
        scratch_shapes=[
            pltpu.VMEM((count, width), BF16),
            pltpu.VMEM((width, block), BF16),
            pltpu.VMEM((block, width), BF16),
            pltpu.VMEM((width, block), BF16),
            pltpu.VMEM((width, LANES), F32),
        ],
    )(spots, cotangent, normed_two, inverse_two, rows_two, low, *inner, *outer, active, slope)


def settle_back_body(
    spots, hidden_grad, normed, inverse, rows, context, own, other,
    first_up, context_grad, keep, send, sums, total, weight,
):
    step, steps = pl.program_id(0), pl.num_programs(0)

    @pl.when(step == 0)
    def _():
        unite(weight, own, other, spots[1])
        sums[...] = jnp.zeros_like(sums)
        total[...] = jnp.zeros_like(total)

    upstream = hidden_grad[...]
    up = norm_back(upstream, normed[...], inverse[...], rows[3:4])
    first_up[...] = up
    low = narrow(up)
    context_grad[...] = narrow(dot(low, weight[...], NT))
    total[...] += dot(context[...], low, TN)
    sums[0:1] += row_sum(widen(low))
    sums[1:2] += row_sum(upstream * normed[...])
    sums[2:3] += row_sum(upstream)

    @pl.when(step == steps - 1)
    def _():
        weight[...] = narrow(total[...])
        divide(weight, keep, send, spots[1], slice(None))


def settle_back(spots, hidden_grad, normed, inverse, rows, context, second):
    count, width = context.shape
    block = count // 4
    tall = pl.BlockSpec((block, width), lambda i: (i, 0))
    dims = second[0].shape[:2] + (width,)
    return kernel(
        settle_back_body,
        "settle_back",
        4 * count * width * width,
        16 * count * width,
        grid=(4,),
        in_specs=[SCALARS, tall, tall, pl.BlockSpec((block, 1), lambda i: (i, 0))]
        + [fixed(rows.shape), tall, fixed(dims, 0, 0, 1), fixed(dims, 0, 0, 1)],
        out_specs=[tall, tall, fixed(dims), fixed(dims), fixed((8, width))],
        out_shape=[
            shape((count, width), F32),
            shape((count, width)),
            shape(dims),
            shape(dims),
            shape((8, width), F32),
        ],
        scratch_shapes=[pltpu.VMEM((width, width), F32), pltpu.VMEM((width, width), BF16)],
    )(spots, hidden_grad, normed, inverse, rows, context, *second)


def tokens_back_body(
    spots, packed_grad, own_first, other_first, own_second, other_second, first_up, grad, total, weight
):
    part, side = pl.program_id(0), spots[1]

    @pl.when(part < 2)
    def _():
        unite(weight, own_first, other_first, side)

    @pl.when(part == 2)
    def _():
        unite(weight, own_second, other_second, side)

    added = dot(packed_grad[...], weight[...], NT)

    @pl.when(part == 0)
    def _():
        total[...] = first_up[...] + added

    @pl.when(part == 1)
    def _():
        total[...] += added

    @pl.when(part == 2)
    def _():
        grad[...] = narrow(total[...] + added)


def tokens_back(spots, packed_grad, first, second, first_up):
    count, width = first_up.shape
    dims = first[0].shape[:2] + (width,)
    pick = pl.BlockSpec(dims, lambda i: (0, 0, jnp.minimum(i, 1)))
    return kernel(
        tokens_back_body,
        "tokens_back",
        6 * count * width * width,
        8 * count * width,
        grid=(3,),
        in_specs=[SCALARS, pl.BlockSpec((count, width), lambda i: (0, i)), pick, pick]
        + [fixed(dims), fixed(dims), fixed((count, width))],
        out_specs=fixed((count, width)),
        out_shape=shape((count, width)),
        scratch_shapes=[pltpu.VMEM((count, width), F32), pltpu.VMEM((width, width), BF16)],
    )(spots, packed_grad, *first, *second, first_up)


def weights_back_body(
    spots, packed_grad, tokens, packed_sums, sums, keep_first, send_first, keep_second, send_second, made
):
    part, side = pl.program_id(0), spots[1]
    width = tokens.shape[1]
    half = width // 2
    made[...] = narrow(dot(tokens[...], packed_grad[...], TN))
    low, high = made.at[:, :half], made.at[:, half:]

    @pl.when(part == 0)
    def _():
        divide(made, keep_first, send_first, side, slice(0, width))

    @pl.when(part == 1)
    def _():
        divide(low, keep_first, send_first, side, slice(width, width + half))
        divide(high, keep_second, send_second, side, slice(0, half))

    @pl.when(part == 2)
    def _():
        divide(made, keep_second, send_second, side, slice(half, half + width))
        packed = jnp.sum(packed_sums[...], axis=0)
        made[:, :LANES] = narrow(
            as_columns(
                (packed[:, :width], packed[:, 2 * width :], sums[0:1], sums[1:2], sums[2:3])
            )
        )
        divide(
            made.at[:, :LANES],
            keep_first,
            send_first,
            side,
            slice(width + half, width + half + LANES),
        )


def weights_back(spots, packed_grad, tokens, packed_sums, sums, dims):
    count, width = tokens.shape
    one, two = dims + (width + width // 2 + LANES,), dims + (width + width // 2,)
    return kernel(
        weights_back_body,
        "weights_back",
        6 * count * width * width,
        8 * count * width,
        grid=(3,),
        in_specs=[SCALARS, pl.BlockSpec((count, width), lambda i: (0, i)), fixed(tokens.shape)]
        + [fixed(packed_sums.shape), fixed(sums.shape)],
        out_specs=[fixed(one), fixed(one), fixed(two), fixed(two)],
        out_shape=[shape(one), shape(one), shape(two), shape(two)],
        scratch_shapes=[pltpu.VMEM((width, width), BF16)],
    )(spots, packed_grad, tokens, packed_sums, sums)


def move(name, spots, sources, outs, moves):
    def body(spots, *refs):
        ins, results, sems = refs[: len(sources)], refs[len(sources) : -1], refs[-1]
        copies = []
        for number, (source, source_at, out, out_at) in enumerate(moves):
            taken = ins[source].at[source_at(spots)] if source_at else ins[source]
            put = results[out].at[out_at(spots)] if out_at else results[out]
            copies.append(pltpu.make_async_copy(taken, put, sems.at[number]))
        for copy in copies:
            copy.start()
        for copy in copies:
            copy.wait()

    return kernel(
        body,
        name,
        0,
        4 * sum(math.prod(out.shape) for out in outs),
        in_specs=[SCALARS] + [ANYWHERE] * len(sources),
        out_specs=[pl.BlockSpec(memory_space=pltpu.VMEM)] * len(outs),
        out_shape=outs,
        scratch_shapes=[pltpu.SemaphoreType.DMA((len(moves),))],
    )(spots, *sources)


def combine(name, spots, groups, seq):
    operands, in_specs, out_specs, out_shape, plan = [], [], [], [], []
    for members, axis, spot in groups:
        first = members[0][0].shape
        rest = first[:axis] + first[axis + 1 : -3]
        rows = sum(kept.shape[-2] for kept, _ in members)
        for flip in range(2):
            for kept, came in members:
                dims = kept.shape
                block = dims[:axis] + (None,) + dims[axis + 1 : -3] + (None,) + dims[-2:]

                def index(i, spots, axis=axis, spot=spot, flip=flip, count=len(dims)):
                    at = [0] * count
                    at[axis] = spots[spot] if flip == 0 else 1 - spots[spot]
                    at[count - 3] = i
                    return tuple(at)

                operands += [kept, came]
                in_specs += [pl.BlockSpec(block, index)] * 2
            dims = rest + (seq, rows, first[-1])
            out_shape.append(shape(dims))
            out_specs.append(
                pl.BlockSpec(
                    rest + (None,) + dims[-2:],
                    lambda i, spots, count=len(rest): (0,) * count + (i, 0, 0),
                )
            )
            plan.append([kept.shape[-2] for kept, _ in members])

    def body(spots, *refs):
        ins, outs = iter(refs[: len(operands)]), refs[len(operands) :]
        for out, heights in zip(outs, plan):
            start = 0
            for height in heights:
                total = narrow(widen(next(ins)[...]) + widen(next(ins)[...]))
                out[..., start : start + height, :] = total
                start += height

    outs = kernel(
        body,
        name,
        0,
        3 * sum(2 * math.prod(out.shape) for out in out_shape),
        grid_spec=pltpu.PrefetchScalarGridSpec(
            num_scalar_prefetch=1, grid=(seq,), in_specs=in_specs, out_specs=out_specs
        ),
        out_shape=out_shape,
    )(spots, *operands)
    return [tuple(outs[2 * i : 2 * i + 2]) for i in range(len(groups))]


def total_of(kept, came):
    return narrow(widen(kept) + widen(came))


def block_at(blocks, index, axis=0):
    return lax.dynamic_index_in_dim(blocks, index, axis, keepdims=False)


class Links:
    def __init__(self, mesh):
        self.dp, self.seq = mesh.shape["dp"], mesh.shape["seq"]
        self.bits = self.dp.bit_length() - 1
        assert self.dp == 1 << self.bits
        upward = list(range(1, self.bits))
        self.orders = (upward, upward[::-1])
        self.direct = self.bits == 3

    def turn(self, blocks):
        return lax.all_to_all(blocks, "seq", split_axis=0, concat_axis=0, tiled=True)

    def gather_seq(self, shard):
        return self.turn(jnp.broadcast_to(shard, (self.seq,) + shard.shape))

    def reduce_seq(self, blocks):
        return jnp.sum(widen(self.turn(blocks)), axis=0)

    def by_seq(self, value):
        return value.reshape(self.seq, value.shape[0] // self.seq, *value.shape[1:])

    def across(self, value, bit):
        pairs = [
            (d * self.seq + s, (d ^ (1 << bit)) * self.seq + s)
            for d in range(self.dp)
            for s in range(self.seq)
        ]
        return lax.ppermute(value, AXES, pairs)

    def digit(self, bit):
        return (lax.axis_index("dp") >> bit) & 1

    def spots(self):
        digits = [self.digit(bit) for bit in range(self.bits)]
        if not self.direct:
            digits[0] = jnp.zeros_like(digits[0])
        return jnp.stack([lax.axis_index("seq")] + digits).astype(jnp.int32)


    def gather_digits(self, name, spots, arrays, bits, done, wait=()):
        others = [after(self.across(held, bit), *wait) for held, bit in zip(arrays, bits)]
        outs, moves = [], []
        for out, (held, bit) in enumerate(zip(arrays, bits)):
            axis = sum(other > bit for other in done[out])
            outs.append(shape(held.shape[:axis] + (2,) + held.shape[axis:]))
            for flip in range(2):

                def at(spots, axis=axis, bit=bit, flip=flip):
                    mine = spots[1 + bit]
                    return (slice(None),) * axis + (1 - mine if flip else mine,)

                moves.append((2 * out + flip, None, out, at))
        sources = [value for pair in zip(arrays, others) for value in pair]
        return move(name, spots, sources, outs, moves)

    def halves(self, held):
        if self.direct:
            held = held.reshape(STEPS, -1, held.shape[-1])
            return held, self.across(held, 0)
        whole = self.gather_rest(held)
        whole = whole.reshape(STEPS, 2, -1, whole.shape[-1])
        return whole[:, 0], whole[:, 1]

    def gather_rest(self, held):
        done = []
        for bit in self.orders[0] + [0]:
            axis = sum(other > bit for other in done)
            other, mine = self.across(held, bit), self.digit(bit)
            held = jnp.where(
                mine == 0, jnp.stack([held, other], axis=axis), jnp.stack([other, held], axis=axis)
            )
            done.append(bit)
        return held


    def swapped(self, keep, send, wait=()):
        return keep, after(self.across(send, 0), *wait)

    def reduce_whole(self, keep, send):
        rows = keep.shape[0] * keep.shape[1] * 2 // (self.dp * self.seq)
        whole = jnp.stack([keep, send], axis=1)
        held = whole.reshape((2,) * self.bits + (self.seq, rows, keep.shape[-1]))
        left = list(range(self.bits))[::-1]
        for bit in [0] + self.orders[0]:
            axis = left.index(bit)
            mine = self.digit(bit)
            other = self.across(block_at(held, 1 - mine, axis), bit)
            held = narrow(widen(block_at(held, mine, axis)) + widen(other))
            left.remove(bit)
        return self.reduce_seq(held)

    def by_digits(self, value):
        return value.reshape(2, 2, self.seq, -1, value.shape[-1])


def columns(vectors, rows):
    block = jnp.concatenate([vector.reshape(rows, -1) for vector in vectors], axis=1)
    return jnp.pad(block, ((0, 0), (0, LANES - block.shape[1])))


def shards(
    links,
    tokens,
    cotangent,
    lengths,
    packed_weight,
    query_bias,
    value_bias,
    output_weight,
    output_bias,
    first_gain,
    first_shift,
    inner_weight,
    inner_bias,
    outer_weight,
    outer_bias,
    second_gain,
    second_shift,
):
    width = tokens.shape[-1]
    seq, direct = links.seq, links.direct
    small = packed_weight.shape[0]
    feed_width = inner_weight.shape[1]
    wide = feed_width // width
    spots = links.spots()

    attention_vectors = columns(
        [narrow(v) for v in (query_bias, value_bias, output_bias, first_gain, first_shift)], small
    )
    held = [
        links.gather_seq(
            jnp.concatenate([narrow(packed_weight[:, : 2 * width]), attention_vectors], axis=1)
        ),
        links.gather_seq(
            jnp.concatenate([narrow(packed_weight[:, 2 * width :]), narrow(output_weight)], axis=1)
        ),
    ]
    feed_vectors = columns(
        [narrow(v) for v in (outer_bias, second_gain, second_shift, inner_bias)], small
    )
    feed_shard = jnp.concatenate([narrow(inner_weight), feed_vectors], axis=1)
    feed_held = [
        links.gather_seq(after(feed_shard, *held)),
        links.gather_seq(after(narrow(outer_weight), *held)),
    ]
    if direct:
        held = links.gather_digits("attention_one", spots, held, (1, 2), ([], []))
        held = links.gather_digits("attention_two", spots, held, (2, 1), ([1], [2]))
        feed_held = [after(value, *held) for value in feed_held]
    first, second = (links.halves(value) for value in held)
    came = links.turn(after(links.by_seq(tokens), *feed_held))
    if direct:
        feed_held = links.gather_digits("feed_one", spots, feed_held, (1, 2), ([], []))
    came = after(came, *feed_held)
    cotangent_mine = links.turn(after(links.by_seq(cotangent), came))
    dims = came.shape
    flat = came.reshape(-1, width)

    packed, rows_one = project(spots, flat, first, second)
    packed = packed.reshape(dims[:-1] + (3 * width,))
    context, probs = attend(spots, lengths, packed)
    context = context.reshape(-1, width)
    if direct:
        feed_held = links.gather_digits("feed_two", spots, feed_held, (2, 1), ([1], [2]), [context])
    context = after(context, *feed_held)
    normed_one, inverse_one, low = settle(spots, context, second, flat, rows_one)
    inner, outer = (links.halves(value) for value in feed_held)
    active, slope, normed_two, inverse_two, rows_two, output = feed(
        spots, low, inner, outer, normed_one, rows_one
    )
    cotangent_mine = after(cotangent_mine, slope)
    output = after(output, cotangent_mine)
    cotangent_mine = after(cotangent_mine, output)
    keep_inner, send_inner, keep_outer, send_outer, hidden_grad = feed_back(
        spots,
        cotangent_mine.reshape(-1, width),
        normed_two,
        inverse_two,
        rows_two,
        low,
        inner,
        outer,
        active,
        slope,
    )
    output = after(links.turn(output.reshape(dims)), hidden_grad)
    send_inner, send_outer = after(send_inner, output), after(send_outer, output)
    hidden_grad = after(hidden_grad, send_inner, send_outer)
    first_up, context_grad, keep_output, send_output, sums = settle_back(
        spots, hidden_grad, normed_one, inverse_one, rows_one, context, second
    )
    if direct:
        feed_pair = [links.by_digits(x) for x in links.swapped(keep_inner, send_inner, [sums])]
        outer_pair = [links.by_digits(x) for x in links.swapped(keep_outer, send_outer, [sums])]
        output_pair = [links.by_digits(x) for x in links.swapped(keep_output, send_output)]
        feed_sum, outer_sum = combine(
            "feed_sum_one", spots, [([feed_pair], 1, 2), ([outer_pair, output_pair], 0, 3)], seq
        )
        context_grad = after(context_grad, feed_sum[1], outer_sum[1])
    packed_grad, packed_sums = attend_back(packed, probs, context_grad.reshape(dims))
    packed_grad = packed_grad.reshape(-1, 3 * width)
    tokens_grad = tokens_back(spots, packed_grad, first, second, first_up)
    if direct:
        feed_came = after(links.across(feed_sum[1], 1), tokens_grad)
        outer_came = after(links.across(outer_sum[1], 2), tokens_grad)
        feed_sum, outer_sum = combine(
            "feed_sum_two",
            spots,
            [
                ([(feed_sum[0], feed_came)], 0, 3),
                ([(outer_sum[0], outer_came)], 0, 2),
            ],
            seq,
        )
        packed_grad = after(packed_grad, feed_sum[1], outer_sum[1])
    tokens_grad = links.turn(tokens_grad.reshape(dims))
    keep_first, send_first, keep_second, send_second = weights_back(
        spots, packed_grad, flat, packed_sums, sums, first[0].shape[:2]
    )
    if direct:
        first_pair = [links.by_digits(x) for x in links.swapped(keep_first, send_first)]
        second_pair = [links.by_digits(x) for x in links.swapped(keep_second, send_second)]
        first_sum, second_sum = combine(
            "first_sum_one", spots, [([first_pair], 1, 2), ([second_pair], 0, 3)], seq
        )
        first_came, second_came = links.across(first_sum[1], 1), links.across(second_sum[1], 2)
        feed_came = after(links.across(feed_sum[1], 2), first_sum[1])
        outer_came = after(links.across(outer_sum[1], 1), second_sum[1])
        feed_total, outer_total = total_of(feed_sum[0], feed_came), total_of(outer_sum[0], outer_came)
        first_came, second_came = after(first_came, feed_total), after(second_came, outer_total)
        first_sum, second_sum = combine(
            "first_sum_two",
            spots,
            [([(first_sum[0], first_came)], 0, 3), ([(second_sum[0], second_came)], 0, 2)],
            seq,
        )
        first_came, second_came = links.across(first_sum[1], 2), links.across(second_sum[1], 1)
        feed_share, outer_share = links.reduce_seq(feed_total), links.reduce_seq(outer_total)
        first = links.reduce_seq(total_of(first_sum[0], first_came))
        second = links.reduce_seq(total_of(second_sum[0], second_came))
        output_share = outer_share[outer_weight.shape[0] :]
        outer_share = outer_share[: outer_weight.shape[0]]
    else:
        feed_share = links.reduce_whole(keep_inner, send_inner)
        outer_share = links.reduce_whole(keep_outer, send_outer)
        output_share = links.reduce_whole(keep_output, send_output)
        first = links.reduce_whole(keep_first, send_first)
        second = links.reduce_whole(keep_second, send_second)
    tokens_grad = widen(tokens_grad)
    half = width + width // 2
    return (
        output.reshape(tokens.shape),
        tokens_grad.reshape(tokens.shape),
        jnp.concatenate([first[:, :half], second], axis=1),
        first[:, half],
        first[:, half + 1],
        output_share,
        first[:, half + 2],
        first[:, half + 3],
        first[:, half + 4],
        feed_share[:, :feed_width],
        feed_share[:, feed_width + 3 : feed_width + 3 + wide].reshape(-1),
        outer_share,
        feed_share[:, feed_width],
        feed_share[:, feed_width + 1],
        feed_share[:, feed_width + 2],
    )


def solution(mesh):
    split = P(AXES)
    split_rows = P(AXES, None)
    packed_rows = P("dp", "seq", None)
    return jax.shard_map(
        partial(shards, Links(mesh)),
        mesh=mesh,
        in_specs=(
            packed_rows,
            packed_rows,
            P("dp", None),
            split_rows,
            split,
            split,
            split_rows,
            split,
            split,
            split,
            split_rows,
            split,
            split_rows,
            split,
            split,
            split,
        ),
        out_specs=(
            packed_rows,
            packed_rows,
            split_rows,
            split,
            split,
            split_rows,
            split,
            split,
            split,
            split_rows,
            split,
            split_rows,
            split,
            split,
            split,
        ),
        check_vma=False,
    )
```

```python
from functools import partial
import math

import jax
import jax.numpy as jnp
from jax import lax
from jax.experimental import pallas as pl
from jax.experimental.pallas import tpu as pltpu
from jax.sharding import PartitionSpec as P

HEAD_DIM = 64
LANES = 128
PARTS = 4
EPSILON = 1e-06
AXES = ("dp", "seq")
BF16, F32 = jnp.bfloat16, jnp.float32

NN = (((1,), (0,)), ((), ()))
NT = (((1,), (1,)), ((), ()))
TN = (((0,), (0,)), ((), ()))


def narrow(value):
    return value.astype(BF16)


def widen(value):
    return value.astype(F32)


def after(value, *others):
    return lax.optimization_barrier((value,) + others)[0]


def dot(left, right, dims=NN):
    return lax.dot_general(left, right, dims, preferred_element_type=F32)


def shape(dims, dtype=BF16):
    return jax.ShapeDtypeStruct(dims, dtype)


def like(value):
    return jax.ShapeDtypeStruct(value.shape, value.dtype)


def fixed(dims, *index):
    at = tuple(index) or (0,) * len(dims)
    return pl.BlockSpec(dims, lambda *_: at)


SCALARS = pl.BlockSpec(memory_space=pltpu.SMEM)
ANYWHERE = pl.BlockSpec(memory_space=pl.ANY)


def row_sum(value):
    return jnp.sum(value, axis=0, keepdims=True)


def kernel(body, name, flops, touched, **options):
    return pl.pallas_call(
        body,
        name=name,
        compiler_params=pltpu.CompilerParams(vmem_limit_bytes=60 << 20),
        cost_estimate=pl.CostEstimate(flops=flops, bytes_accessed=touched, transcendentals=0),
        **options,
    )


def unite(target, own, other, spots):
    side, chip = spots[1], spots[2]
    rows = own[0].shape[0]
    for index in range(PARTS):
        for half, value in ((side, own[index]), (1 - side, other[index])):
            start = pl.multiple_of((2 * (chip ^ index) + half) * rows, rows)
            target[pl.ds(start, rows), :] = value[...]


def divide(source, keep, send, side, columns):
    count, rows = keep.shape[:2]
    for index in range(count):
        for half, target in ((side, keep), (1 - side, send)):
            start = pl.multiple_of((2 * index + half) * rows, rows)
            target[index, :, columns] = source[pl.ds(start, rows), :]


def gathered_specs(gathered, columns, index):
    block = (gathered[0].shape[0], columns)
    return [pl.BlockSpec(block, lambda *at: (0, index(*at)))] * len(gathered)


def as_columns(rows):
    width = rows[0].shape[1]
    padding = jnp.zeros((LANES - len(rows), width), F32)
    return jnp.concatenate(list(rows) + [padding], axis=0).T


def prepare_attention_body(packed_weight, output_weight, *rest):
    *vectors, out = rest
    seq, small, _ = out.shape
    lane = lax.broadcasted_iota(jnp.int32, (1, LANES), 1)
    block, column = 0.0, 0
    for vector in vectors:
        per = vector.shape[1] // small
        for part in range(per):
            value = jnp.where(spread_mask(small, per, part), vector[...], 0.0)
            value = jnp.sum(value, axis=1, keepdims=True)
            block = block + jnp.where(lane == column, value, 0.0)
            column += 1
    shard = jnp.concatenate(
        [narrow(packed_weight[...]), narrow(output_weight[...]), narrow(block)], axis=1
    )
    for index in range(seq):
        out[index] = shard


def prepare_attention(seq, packed_weight, output_weight, vectors):
    small, wide = packed_weight.shape
    vectors = [vector.reshape(1, -1) for vector in vectors]
    return kernel(
        prepare_attention_body,
        "prepare_attention",
        0,
        16 * small * wide,
        out_shape=shape((seq, small, wide + LANES + output_weight.shape[1])),
    )(packed_weight, output_weight, *vectors)


def prepare_feed_body(inner_weight, outer_weight, out):
    seq, small, _ = out.shape
    wide, width = inner_weight.shape[1], outer_weight.shape[1]
    out[0, :, :wide] = narrow(inner_weight[...])
    for index in range(outer_weight.shape[0] // small):
        start = wide + index * width
        block = outer_weight[index * small : (index + 1) * small]
        out[0, :, start : start + width] = narrow(block)
    for index in range(1, seq):
        out[index] = out[0]


def prepare_feed(seq, inner_weight, outer_weight):
    small, wide = inner_weight.shape
    return kernel(
        prepare_feed_body,
        "prepare_feed",
        0,
        16 * small * wide,
        out_shape=shape((seq, small, 2 * wide)),
    )(inner_weight, outer_weight)


def project_body(spots, tokens, *refs):
    weights, columns = refs[: 2 * PARTS], refs[2 * PARTS : 4 * PARTS]
    packed, flat, weight, rows, vectors = refs[4 * PARTS :]
    part = pl.program_id(0)
    seq, count, places, width = tokens.shape
    length = seq * places

    @pl.when(part == 0)
    def _():
        unite(vectors, columns[:PARTS], columns[PARTS:], spots)
        rows[...] = widen(vectors[...]).T[:8]
        for row in range(count):
            flat[row * length : (row + 1) * length] = tokens[:, row].reshape(length, width)

    unite(weight, weights[:PARTS], weights[PARTS:], spots)
    query, value = rows[0:1], rows[1:2]
    bias = jnp.where(part == 0, query, jnp.where(part == 2, value, jnp.zeros_like(query)))
    result = narrow(dot(flat[...], weight[...]) + bias)
    packed[...] = result.reshape(packed.shape)


def project(spots, tokens, gathered):
    seq, rows, places, width = tokens.shape
    length = seq * places
    return kernel(
        project_body,
        "project",
        6 * rows * length * width * width,
        8 * rows * length * width,
        grid=(3,),
        in_specs=[SCALARS, fixed(tokens.shape)]
        + gathered_specs(gathered, width, lambda i: i)
        + gathered_specs(gathered, LANES, lambda i: 4 * width // LANES),
        out_specs=[
            pl.BlockSpec((rows, length, width), lambda i: (0, 0, i)),
            fixed((rows * length, width)),
            pl.BlockSpec((width, width), lambda i: (0, i)),
            fixed((8, width)),
            fixed((width, LANES)),
        ],
        out_shape=[
            shape((rows, length, 3 * width)),
            shape((rows * length, width)),
            shape((width, 3 * width)),
            shape((8, width), F32),
            shape((width, LANES)),
        ],
    )(spots, tokens, *gathered, *gathered)


def pair_labels(places, lengths, row):
    label, bound = jnp.zeros_like(places), 0
    for pair in range(lengths.shape[1] - 1):
        bound = bound + lengths[row, pair]
        label = label + (places >= bound).astype(jnp.int32)
    return label


def attend_body(spots, lengths, query, key, value, context, probs, bias):
    length = bias.shape[0]

    @pl.when(pl.program_id(1) == 0)
    def _():
        at = spots[0] * pl.num_programs(0) + pl.program_id(0)
        down = pair_labels(lax.broadcasted_iota(jnp.int32, (length, 1), 0), lengths, at)
        along = pair_labels(lax.broadcasted_iota(jnp.int32, (1, length), 1), lengths, at)
        bias[...] = jnp.where(down == along, 0.0, -1e30)

    lane = lax.broadcasted_iota(jnp.int32, (1, LANES), 1)
    keys, values = key[0], value[0]
    queries = query[0] * BF16(HEAD_DIM**-0.5)
    parts = []
    for head in range(2):
        mine = (lane >= HEAD_DIM) == bool(head)
        scores = dot(jnp.where(mine, queries, BF16(0)), keys, NT) + bias[...]
        raised = jnp.exp(scores - jnp.max(scores, axis=-1, keepdims=True))
        total = jnp.sum(raised, axis=-1, keepdims=True)
        low = narrow(raised * (1.0 / total))
        probs[0, head] = low
        parts.append(dot(low, values))
    context[0] = narrow(jnp.where(lane < HEAD_DIM, parts[0], parts[1]))


def head_pair(length, offset):
    return pl.BlockSpec((1, length, LANES), lambda r, p: (r, 0, offset + p))


def attend(spots, lengths, packed):
    rows, length, wide = packed.shape
    pairs = wide // 3 // LANES
    return kernel(
        attend_body,
        "attend",
        rows * pairs * 16 * length * length * LANES,
        rows * pairs * 8 * length * length,
        grid=(rows, pairs),
        in_specs=[SCALARS, SCALARS] + [head_pair(length, part * pairs) for part in range(3)],
        out_specs=[
            head_pair(length, 0),
            pl.BlockSpec((1, 2, length, length), lambda r, p: (r, p, 0, 0)),
        ],
        out_shape=[shape((rows, length, wide // 3)), shape((rows, 2 * pairs, length, length))],
        scratch_shapes=[pltpu.VMEM((length, length), F32)],
    )(spots, lengths, packed, packed, packed)


def attend_back_body(query, key, value, upstream, probs, grads, sums):
    pair, pairs = pl.program_id(1), pl.num_programs(1)
    lane = lax.broadcasted_iota(jnp.int32, (1, LANES), 1)
    scale = BF16(HEAD_DIM**-0.5)
    queries, keys, values, up = query[0] * scale, key[0], value[0], upstream[0]
    scaled_keys = keys * scale
    query_parts, key_grad, value_grad = [], 0.0, 0.0
    for head in range(2):
        mine = (lane >= HEAD_DIM) == bool(head)
        up_mine = jnp.where(mine, up, BF16(0))
        queries_mine = jnp.where(mine, queries, BF16(0))
        low = probs[0, head]
        prob_grad = dot(up_mine, values, NT)
        softmaxed = widen(low)
        weighted = jnp.sum(softmaxed * prob_grad, axis=-1, keepdims=True)
        score_grad = narrow(softmaxed * (prob_grad - weighted))
        query_parts.append(dot(score_grad, scaled_keys))
        key_grad = key_grad + dot(queries_mine, score_grad, TN)
        value_grad = value_grad + dot(up_mine, low, TN)
    query_grad = jnp.where(lane < HEAD_DIM, query_parts[0], query_parts[1])
    for part, grad in enumerate((query_grad, key_grad.T, value_grad.T)):
        at = pl.ds(pl.multiple_of((part * pairs + pair) * LANES, LANES), LANES)
        rounded = narrow(grad)
        grads[0, :, at] = rounded
        sums[0, :, at] = row_sum(widen(rounded))


def attend_back(packed, probs, upstream):
    rows, length, wide = packed.shape
    pairs = wide // 3 // LANES
    return kernel(
        attend_back_body,
        "attend_back",
        rows * pairs * 16 * length * length * LANES,
        rows * pairs * 8 * length * length,
        grid=(rows, pairs),
        in_specs=[head_pair(length, part * pairs) for part in range(3)]
        + [
            head_pair(length, 0),
            pl.BlockSpec((1, 2, length, length), lambda r, p: (r, p, 0, 0)),
        ],
        out_specs=[
            pl.BlockSpec((1, length, wide), lambda r, p: (r, 0, 0)),
            pl.BlockSpec((1, 1, wide), lambda r, p: (r, 0, 0)),
        ],
        out_shape=[shape(packed.shape), shape((rows, 1, wide), F32)],
    )(packed, packed, packed, upstream, probs)


def normed_of(summed):
    centred = summed - jnp.mean(summed, axis=-1, keepdims=True)
    variance = jnp.mean(centred * centred, axis=-1, keepdims=True)
    inverse = lax.rsqrt(variance + EPSILON)
    return centred * inverse, inverse


def norm_back(upstream, normed, inverse, gain):
    scaled = upstream * gain
    first_mean = jnp.mean(scaled, axis=-1, keepdims=True)
    second_mean = jnp.mean(scaled * normed, axis=-1, keepdims=True)
    return inverse * (scaled - first_mean - normed * second_mean)


def settle_body(spots, context, tokens, rows, *refs):
    parts, (normed, inverse, low, weight) = refs[: 2 * PARTS], refs[2 * PARTS :]

    @pl.when(pl.program_id(0) == 0)
    def _():
        unite(weight, parts[:PARTS], parts[PARTS:], spots)

    summed = widen(tokens[...]) + dot(context[...], weight[...]) + rows[2:3]
    normed[...], inverse[...] = normed_of(summed)
    low[...] = narrow(normed[...] * rows[3:4] + rows[4:5])


def settle(spots, context, tokens, rows, gathered):
    count, width = context.shape
    block = count // 4
    tall = pl.BlockSpec((block, width), lambda i: (i, 0))
    return kernel(
        settle_body,
        "settle",
        2 * count * width * width,
        10 * count * width,
        grid=(4,),
        in_specs=[SCALARS, tall, tall, fixed(rows.shape)]
        + gathered_specs(gathered, width, lambda i: 3),
        out_specs=[tall, pl.BlockSpec((block, 1), lambda i: (i, 0)), tall, fixed((width, width))],
        out_shape=[
            shape((count, width), F32),
            shape((count, 1), F32),
            shape((count, width)),
            shape((width, width)),
        ],
    )(spots, context, tokens, rows, *gathered)


def spread_mask(rows, per, column):
    down = lax.broadcasted_iota(jnp.int32, (rows, rows * per), 0)
    along = lax.broadcasted_iota(jnp.int32, (rows, rows * per), 1)
    return along == down * per + column


def stack_blocks(part):
    seq, rows, wide = part.shape
    width = wide // PARTS
    blocks = [
        widen(part[place, :, index * width : (index + 1) * width])
        for place in range(seq)
        for index in range(PARTS)
    ]
    return narrow(jnp.concatenate(blocks, axis=0))


def feed_body(spots, low, vectors, normed_one, rows, *refs):
    inners, outers = refs[: 2 * PARTS], refs[2 * PARTS : 4 * PARTS]
    (
        active, slope, normed_two, inverse_two, output, inner_weight, outer_weight, branch,
    ) = refs[4 * PARTS :]
    step, steps = pl.program_id(0), pl.num_programs(0)
    unite(inner_weight, inners[:PARTS], inners[PARTS:], spots)
    for index in range(PARTS):

        @pl.when(step == spots[2] ^ index)
        def _():
            half = outer_weight.shape[0] // 2
            for side, part in ((spots[1], outers[index]), (1 - spots[1], outers[PARTS + index])):
                start = pl.multiple_of(side * half, half)
                outer_weight[pl.ds(start, half), :] = stack_blocks(part)

    block = inner_weight.shape[-1]
    share_rows = vectors.shape[0] // PARTS
    per = block // share_rows
    own_rows = vectors[pl.ds(pl.multiple_of(step * share_rows, share_rows), share_rows), :]
    bias = 0.0
    for column in range(per):
        value = widen(own_rows[:, 8 + column : 9 + column])
        bias = bias + jnp.where(spread_mask(share_rows, per, column), value, 0.0)
    inner = dot(low[...], inner_weight[...]) + row_sum(bias)
    share = 0.5 * (1.0 + lax.erf(inner * math.sqrt(0.5)))
    raised = jnp.exp(-0.5 * inner * inner) * (1.0 / math.sqrt(2.0 * math.pi))
    acted = narrow(inner * share)
    active[...] = acted
    slope[...] = narrow(share + inner * raised)
    part = dot(acted, outer_weight[...])

    @pl.when(step == 0)
    def _():
        branch[...] = part

    @pl.when(step > 0)
    def _():
        branch[...] += part

    @pl.when(step == steps - 1)
    def _():
        hidden = normed_one[...] * rows[3:4] + rows[4:5]
        normed_two[...], inverse_two[...] = normed_of(hidden + branch[...] + rows[5:6])
        result = narrow(normed_two[...] * rows[6:7] + rows[7:8])
        seq, count, places, width = output.shape
        result = result.reshape(count, seq, places, width)
        for row in range(count):
            output[:, row] = result[row]


def feed(spots, low, vectors, normed_one, rows, gathered, dims):
    count, width = low.shape
    wide = gathered[0].shape[1] // 2
    block = wide // PARTS
    deep = [part.reshape(dims[0], -1, 2 * wide) for part in gathered]
    all_of = fixed((count, width))
    across = pl.BlockSpec((count, block), lambda f: (0, f))
    outer = pl.BlockSpec(
        deep[0].shape[:2] + (wide,), lambda f: (0, 0, 1), pipeline_mode=pl.Buffered(1)
    )
    return kernel(
        feed_body,
        "feed",
        4 * count * width * wide,
        12 * count * wide,
        grid=(PARTS,),
        in_specs=[SCALARS, all_of, fixed(vectors.shape), all_of, fixed(rows.shape)]
        + gathered_specs(gathered, block, lambda f: f)
        + [outer] * len(deep),
        out_specs=[
            across,
            across,
            all_of,
            fixed((count, 1)),
            fixed(dims),
            pl.BlockSpec((width, block), lambda f: (0, f)),
            pl.BlockSpec((block, width), lambda f: (f, 0)),
        ],
        out_shape=[
            shape((count, wide)),
            shape((count, wide)),
            shape((count, width), F32),
            shape((count, 1), F32),
            shape(dims),
            shape((width, wide)),
            shape((wide, width)),
        ],
        scratch_shapes=[pltpu.VMEM((count, width), F32)],
    )(spots, low, vectors, normed_one, rows, *gathered, *deep)


def feed_back_body(
    spots, cotangent, normed_two, inverse_two, rows_one, low, inner_weight, outer_weight, active, slope,
    keep_inner, send_inner, keep_outer, send_outer, hidden_grad,
    up, made, columns,
):
    step, steps, side = pl.program_id(0), pl.num_programs(0), spots[1]
    block = inner_weight.shape[-1]

    @pl.when(step == 0)
    def _():
        rows, width = cotangent.shape[1], cotangent.shape[-1]
        upstream = jnp.concatenate(
            [widen(cotangent[:, row]).reshape(-1, width) for row in range(rows)], axis=0
        )
        normed = normed_two[...]
        hidden_grad[...] = norm_back(upstream, normed, inverse_two[...], rows_one[6:7])
        up[...] = narrow(hidden_grad[...])
        columns[...] = as_columns(
            (row_sum(widen(up[...])), row_sum(upstream * normed), row_sum(upstream))
        )

    inner_grad = narrow(dot(up[...], outer_weight[...], NT) * widen(slope[...]))
    made[...] = narrow(dot(low[...], inner_grad, TN))
    at = pl.ds(pl.multiple_of(step * block, block), block)
    divide(made, keep_inner, send_inner, side, at)
    hidden_grad[...] += dot(inner_grad, inner_weight[...], NT)
    made[...] = narrow(dot(active[...], up[...], TN))
    divide(made, keep_outer, send_outer, side, slice(None))

    bias = row_sum(widen(inner_grad))
    share_rows = columns.shape[0] // PARTS
    per = block // share_rows
    lane = lax.broadcasted_iota(jnp.int32, (1, LANES), 1)
    total = 0.0
    for column in range(per):
        value = jnp.sum(
            jnp.where(spread_mask(share_rows, per, column), bias, 0.0), axis=1, keepdims=True
        )
        total = total + jnp.where(lane == 3 + column, value, 0.0)
    columns[pl.ds(pl.multiple_of(step * share_rows, share_rows), share_rows), :] += total

    @pl.when(step == steps - 1)
    def _():
        made[:, :LANES] = narrow(columns[...])
        count, rows, wide = keep_inner.shape
        for index in range(count):
            for half, target in ((side, keep_inner), (1 - side, send_inner)):
                start = pl.multiple_of((2 * index + half) * rows, rows)
                target[index, :, wide - LANES :] = made[pl.ds(start, rows), :LANES]


def feed_back(spots, cotangent, normed_two, inverse_two, rows, low, inner, outer, active, slope):
    count, width = low.shape
    wide = inner.shape[1]
    block = wide // PARTS
    all_of = fixed((count, width))
    across = pl.BlockSpec((count, block), lambda f: (0, f))
    first = (PARTS, width // PARTS // 2, wide + LANES)
    second = (PARTS, block // 2, width)
    down = pl.BlockSpec((1,) + second[1:], lambda f: (f, 0, 0))
    return kernel(
        feed_back_body,
        "feed_back",
        8 * count * width * wide,
        12 * count * wide,
        grid=(PARTS,),
        in_specs=[SCALARS, fixed(cotangent.shape), all_of, fixed((count, 1)), fixed(rows.shape), all_of]
        + [
            pl.BlockSpec((width, block), lambda f: (0, f)),
            pl.BlockSpec((block, width), lambda f: (f, 0)),
            across,
            across,
        ],
        out_specs=[fixed(first), fixed(first), down, down, all_of],
        out_shape=[shape(first), shape(first), shape(second), shape(second)]
        + [shape((count, width), F32)],
        scratch_shapes=[
            pltpu.VMEM((count, width), BF16),
            pltpu.VMEM((width, block), BF16),
            pltpu.VMEM((width, LANES), F32),
        ],
    )(spots, cotangent, normed_two, inverse_two, rows, low, inner, outer, active, slope)


def settle_back_body(
    spots, hidden_grad, normed, inverse, rows, context, weight,
    first_up, context_grad, keep, send, sums, total, made,
):
    step, steps = pl.program_id(0), pl.num_programs(0)

    @pl.when(step == 0)
    def _():
        sums[...] = jnp.zeros_like(sums)
        total[...] = jnp.zeros_like(total)

    upstream = hidden_grad[...]
    up = norm_back(upstream, normed[...], inverse[...], rows[3:4])
    first_up[...] = up
    low = narrow(up)
    context_grad[...] = narrow(dot(low, weight[...], NT))
    total[...] += dot(context[...], low, TN)
    sums[0:1] += row_sum(widen(low))
    sums[1:2] += row_sum(upstream * normed[...])
    sums[2:3] += row_sum(upstream)

    @pl.when(step == steps - 1)
    def _():
        made[...] = narrow(total[...])
        divide(made, keep, send, spots[1], slice(None))


def settle_back(spots, hidden_grad, normed, inverse, rows, context, weight):
    count, width = context.shape
    block = count // 4
    tall = pl.BlockSpec((block, width), lambda i: (i, 0))
    dims = (PARTS, width // PARTS // 2, width)
    return kernel(
        settle_back_body,
        "settle_back",
        4 * count * width * width,
        16 * count * width,
        grid=(4,),
        in_specs=[SCALARS, tall, tall, pl.BlockSpec((block, 1), lambda i: (i, 0))]
        + [fixed(rows.shape), tall, fixed((width, width))],
        out_specs=[tall, tall, fixed(dims), fixed(dims), fixed((8, width))],
        out_shape=[
            shape((count, width), F32),
            shape((count, width)),
            shape(dims),
            shape(dims),
            shape((8, width), F32),
        ],
        scratch_shapes=[pltpu.VMEM((width, width), F32), pltpu.VMEM((width, width), BF16)],
    )(spots, hidden_grad, normed, inverse, rows, context, weight)


def tokens_back_body(packed_grad, weight, first_up, grad, total):
    part = pl.program_id(0)
    added = dot(packed_grad[...], weight[...], NT)

    @pl.when(part == 0)
    def _():
        total[...] = first_up[...] + added

    @pl.when(part == 1)
    def _():
        total[...] += added

    @pl.when(part == 2)
    def _():
        seq, rows, places, width = grad.shape
        result = narrow(total[...] + added).reshape(rows, seq, places, width)
        for row in range(rows):
            grad[:, row] = result[row]


def tokens_back(packed_grad, weight, first_up, dims):
    count, width = first_up.shape
    return kernel(
        tokens_back_body,
        "tokens_back",
        6 * count * width * width,
        8 * count * width,
        grid=(3,),
        in_specs=[
            pl.BlockSpec((count, width), lambda i: (0, i)),
            pl.BlockSpec((width, width), lambda i: (0, i)),
            fixed((count, width)),
        ],
        out_specs=fixed(dims),
        out_shape=shape(dims),
        scratch_shapes=[pltpu.VMEM((count, width), F32)],
    )(packed_grad, weight, first_up)


def weights_back_body(spots, packed_grad, tokens, packed_sums, sums, keep, send, made):
    part, side = pl.program_id(0), spots[1]
    width = tokens.shape[1]
    made[...] = narrow(dot(tokens[...], packed_grad[...], TN))
    divide(made, keep, send, side, pl.ds(pl.multiple_of(part * width, width), width))

    @pl.when(part == 2)
    def _():
        packed = jnp.sum(packed_sums[...], axis=0)
        made[:, :LANES] = narrow(
            as_columns(
                (packed[:, :width], packed[:, 2 * width :], sums[0:1], sums[1:2], sums[2:3])
            )
        )
        divide(made.at[:, :LANES], keep, send, side, slice(3 * width, 3 * width + LANES))


def weights_back(spots, packed_grad, tokens, packed_sums, sums):
    count, width = tokens.shape
    dims = (PARTS, width // PARTS // 2, 3 * width + LANES)
    return kernel(
        weights_back_body,
        "weights_back",
        6 * count * width * width,
        8 * count * width,
        grid=(3,),
        in_specs=[SCALARS, pl.BlockSpec((count, width), lambda i: (0, i)), fixed(tokens.shape)]
        + [fixed(packed_sums.shape), fixed(sums.shape)],
        out_specs=[fixed(dims), fixed(dims)],
        out_shape=[shape(dims), shape(dims)],
        scratch_shapes=[pltpu.VMEM((width, width), BF16)],
    )(spots, packed_grad, tokens, packed_sums, sums)


def side_by_side(out, start, total):
    small, width = out.shape[0], total.shape[1]
    for height in range(0, total.shape[0], small):
        out[:, start : start + width] = narrow(total[height : height + small])
        start += width
    return start


def chip_sums(name, spots, pairs, seq, small):
    operands, in_specs = [], []
    wide = sum(kept.shape[1] // (seq * small) * kept.shape[2] for kept, _ in pairs)
    for kept, came in pairs:
        height = kept.shape[1] // seq
        for part in range(PARTS):
            block = pl.BlockSpec(
                (None, None, height, kept.shape[2]),
                lambda i, spots, part=part: (spots[2] ^ part, i, 0, 0),
            )
            for value in (kept, came):
                operands.append(value.reshape(PARTS, seq, height, value.shape[2]))
                in_specs.append(block)

    def body(spots, *refs):
        ins, outs = refs[: len(operands)], refs[len(operands) :]
        for part, out in enumerate(outs):
            start = 0
            for pair in range(len(pairs)):
                at = 2 * (pair * PARTS + part)
                start = side_by_side(out, start, widen(ins[at][...]) + widen(ins[at + 1][...]))

    return kernel(
        body,
        name,
        0,
        6 * PARTS * seq * small * wide,
        grid_spec=pltpu.PrefetchScalarGridSpec(
            num_scalar_prefetch=1,
            grid=(seq,),
            in_specs=in_specs,
            out_specs=[pl.BlockSpec((None, small, wide), lambda i, spots: (i, 0, 0))] * PARTS,
        ),
        out_shape=[shape((seq, small, wide))] * PARTS,
    )(spots, *operands)


def total_body(*refs):
    total = widen(refs[0][...])
    for ref in refs[1:-1]:
        total = total + widen(ref[...])
    refs[-1][...] = narrow(total)


def total_of(name, values, flops=0):
    seq, small, wide = values[0].shape
    block = pl.BlockSpec((None, small, wide), lambda i: (i, 0, 0))
    return kernel(
        total_body,
        name,
        flops,
        2 * (len(values) + 1) * seq * small * wide,
        grid=(seq,),
        in_specs=[block] * len(values),
        out_specs=block,
        out_shape=shape(values[0].shape),
    )(*values)


def finish_body(vectors, blocks, came, *outs):
    seq, small, wide = came.shape
    total = widen(came[0])
    for index in range(1, seq):
        total = total + widen(came[index])
    start = 0
    for out, (count, width) in zip(outs, blocks):
        for index in range(count):
            out[index * small : (index + 1) * small] = total[:, start : start + width]
            start += width
    at = wide - LANES
    for out, (column, per) in zip(outs[len(blocks) :], vectors):
        line = 0.0
        for part in range(per):
            value = total[:, at + column + part : at + column + part + 1]
            line = line + jnp.where(spread_mask(small, per, part), value, 0.0)
        out[...] = row_sum(line)


def finish(name, came, blocks, vectors):
    seq, small, wide = came.shape
    return kernel(
        partial(finish_body, vectors, blocks),
        name,
        0,
        4 * seq * small * wide,
        out_shape=[shape((count * small, width), F32) for count, width in blocks]
        + [shape((1, small * per), F32) for _, per in vectors],
    )(came)


def block_at(blocks, index, axis=0):
    return lax.dynamic_index_in_dim(blocks, index, axis, keepdims=False)


class Links:
    def __init__(self, mesh):
        self.dp, self.seq = mesh.shape["dp"], mesh.shape["seq"]
        self.bits = self.dp.bit_length() - 1
        assert self.dp == 1 << self.bits
        self.direct = self.dp == 2 * PARTS

    def across(self, value, flip):
        pairs = [
            (d * self.seq + s, (d ^ flip) * self.seq + s)
            for d in range(self.dp)
            for s in range(self.seq)
        ]
        return lax.ppermute(value, AXES, pairs)

    def digit(self, bit):
        return (lax.axis_index("dp") >> bit) & 1

    def spots(self):
        place, dp = lax.axis_index("seq"), lax.axis_index("dp")
        side, chip = (dp & 1, dp >> 1) if self.direct else (0 * dp, 0 * dp)
        return jnp.stack([place, side, chip]).astype(jnp.int32)

    def turn(self, blocks):
        return lax.all_to_all(blocks, "seq", split_axis=0, concat_axis=0, tiled=True)

    def spread(self, held):
        return [held] + [self.across(held, 2 * part) for part in range(1, PARTS)]

    def swap(self, parts):
        parts = [part.reshape(-1, part.shape[-1]) for part in parts]
        return parts + [self.across(part, 1) for part in parts]

    def gather_whole(self, held):
        done = []
        for bit in range(self.bits):
            other, mine = self.across(held, 1 << bit), self.digit(bit)
            held = jnp.where(mine == 0, jnp.stack([held, other]), jnp.stack([other, held]))
        return held.reshape(self.dp * self.seq, *held.shape[self.bits + 1 :])

    def cut(self, whole):
        whole = whole.reshape(PARTS, 2, -1, whole.shape[-1])
        return [whole[part, side] for side in range(2) for part in range(PARTS)]

    def reduce_whole(self, keep, send):
        rows = keep.shape[0] * keep.shape[1] * 2 // (self.dp * self.seq)
        whole = jnp.stack([keep, send], axis=1)
        held = whole.reshape((2,) * self.bits + (self.seq, rows, keep.shape[-1]))
        for bit in reversed(range(self.bits)):
            mine = self.digit(bit)
            other = self.across(block_at(held, 1 - mine), 1 << bit)
            held = narrow(widen(block_at(held, mine)) + widen(other))
        return held


def shards(
    links,
    tokens,
    cotangent,
    lengths,
    packed_weight,
    query_bias,
    value_bias,
    output_weight,
    output_bias,
    first_gain,
    first_shift,
    inner_weight,
    inner_bias,
    outer_weight,
    outer_bias,
    second_gain,
    second_shift,
):
    row_count, places, width = tokens.shape
    seq, direct = links.seq, links.direct
    rows = row_count // seq
    dims = (seq, rows, places, width)
    small, tall = packed_weight.shape[0], outer_weight.shape[0]
    wide = inner_weight.shape[1]
    per = wide // width
    spots = links.spots()

    vectors = (
        query_bias, value_bias, output_bias, first_gain, first_shift,
        outer_bias, second_gain, second_shift, inner_bias,
    )
    held = links.turn(prepare_attention(seq, packed_weight, output_weight, vectors))
    feed_held = links.turn(after(prepare_feed(seq, inner_weight, outer_weight), held))
    if direct:
        held = links.spread(held)
        came = links.turn(after(tokens.reshape(dims), feed_held, *held))
        gathered = links.swap(held)
        feed_held = links.spread(feed_held)
    else:
        came = links.turn(after(tokens.reshape(dims), feed_held))
        gathered = links.cut(links.gather_whole(held))
        whole = links.gather_whole(feed_held)
        inner, outer = whole[..., :wide], whole[..., wide:]
        outer = outer.reshape(-1, small, per, width).swapaxes(1, 2)
        outer = outer.reshape(2 * PARTS * seq, per, -1, width).swapaxes(1, 2)
        inner, outer = inner.reshape(width, wide), outer.reshape(width, wide)
        feed_gathered = links.cut(jnp.concatenate([inner, outer], axis=1))
    cotangent_mine = links.turn(after(cotangent.reshape(dims), came))
    packed, flat, packed_whole, rows_one, vectors = project(spots, came, gathered)
    context, probs = attend(spots, lengths, packed)
    context = context.reshape(-1, width)
    if direct:
        feed_held = [feed_held[0]] + [after(value, context) for value in feed_held[1:]]
        context = after(context, *feed_held)
        feed_gathered = links.swap(feed_held)
    normed_one, inverse_one, low, output_whole = settle(spots, context, flat, rows_one, gathered)
    active, slope, normed_two, inverse_two, output, inner_whole, outer_whole = feed(
        spots, low, vectors, normed_one, rows_one, feed_gathered, dims
    )
    cotangent_mine = after(cotangent_mine, slope)
    output = after(output, cotangent_mine)
    cotangent_mine = after(cotangent_mine, output)
    keep_inner, send_inner, keep_outer, send_outer, hidden_grad = feed_back(
        spots,
        cotangent_mine,
        normed_two,
        inverse_two,
        rows_one,
        low,
        inner_whole,
        outer_whole,
        active,
        slope,
    )
    output = after(links.turn(output), hidden_grad)
    send_inner, send_outer = after(send_inner, output), after(send_outer, output)
    hidden_grad = after(hidden_grad, send_inner, send_outer)
    first_up, context_grad, keep_output, send_output, sums = settle_back(
        spots, hidden_grad, normed_one, inverse_one, rows_one, context, output_whole
    )
    if direct:
        inner_came = after(links.across(send_inner, 1), sums)
        outer_came = after(links.across(send_outer, 1), sums)
        output_came = links.across(send_output, 1)
        pairs = [(keep_outer, outer_came), (keep_output, output_came), (keep_inner, inner_came)]
        feed_sums = list(chip_sums("feed_chip_sums", spots, pairs, seq, small))
        context_grad = after(context_grad, *feed_sums[1:])
        feed_sums[1:] = [links.across(feed_sums[part], 2 * part) for part in range(1, PARTS)]
    packed_grad, packed_sums = attend_back(
        packed, probs, context_grad.reshape(rows, seq * places, width)
    )
    packed_grad = packed_grad.reshape(-1, 3 * width)
    grad = tokens_back(packed_grad, packed_whole, first_up, dims)
    tokens_grad = links.turn(grad)
    packed_grad = after(packed_grad, grad)
    keep, send = weights_back(spots, packed_grad, flat, packed_sums, sums)
    if direct:
        feed_sums[1:] = [after(value, keep) for value in feed_sums[1:]]
        feed_total = total_of("feed_total", feed_sums, 10**12)
        came = after(links.across(send, 1), feed_total)
        attention_sums = list(
            chip_sums("attention_chip_sums", spots, [(keep, came)], seq, small)
        )
        feed_total = after(feed_total, tokens_grad, *attention_sums[1:])
        attention_sums[1:] = [
            links.across(attention_sums[part], 2 * part) for part in range(1, PARTS)
        ]
        attention_total = total_of("attention_total", attention_sums)
    else:
        reduced = [
            links.reduce_whole(*pair)
            for pair in ((keep_outer, send_outer), (keep_output, send_output), (keep_inner, send_inner))
        ]
        reduced[0] = reduced[0].reshape(seq, per, small, width).swapaxes(1, 2)
        reduced[0] = reduced[0].reshape(seq, small, per * width)
        feed_total = jnp.concatenate(reduced, axis=2)
        attention_total = links.reduce_whole(keep, send)
    feed_total = links.turn(feed_total)
    attention_total = links.turn(after(attention_total, feed_total))
    (
        outer_grad, output_grad, inner_grad,
        outer_bias_grad, second_gain_grad, second_shift_grad, inner_bias_grad,
    ) = finish(
        "finish_feed",
        feed_total,
        [(per, width), (1, width), (1, wide)],
        [(0, 1), (1, 1), (2, 1), (3, per)],
    )
    (
        packed_weight_grad,
        query_bias_grad, value_bias_grad, output_bias_grad, first_gain_grad, first_shift_grad,
    ) = finish(
        "finish_attention", attention_total, [(1, 3 * width)], [(i, 1) for i in range(5)]
    )
    tokens_grad = widen(tokens_grad)
    return (
        output.reshape(tokens.shape),
        tokens_grad.reshape(tokens.shape),
        packed_weight_grad,
        query_bias_grad.reshape(-1),
        value_bias_grad.reshape(-1),
        output_grad,
        output_bias_grad.reshape(-1),
        first_gain_grad.reshape(-1),
        first_shift_grad.reshape(-1),
        inner_grad,
        inner_bias_grad.reshape(-1),
        outer_grad,
        outer_bias_grad.reshape(-1),
        second_gain_grad.reshape(-1),
        second_shift_grad.reshape(-1),
    )


def solution(mesh):
    split = P(AXES)
    split_rows = P(AXES, None)
    packed_rows = P("dp", "seq", None)
    return jax.shard_map(
        partial(shards, Links(mesh)),
        mesh=mesh,
        in_specs=(
            packed_rows,
            packed_rows,
            P("dp", None),
            split_rows,
            split,
            split,
            split_rows,
            split,
            split,
            split,
            split_rows,
            split,
            split_rows,
            split,
            split,
            split,
        ),
        out_specs=(
            packed_rows,
            packed_rows,
            split_rows,
            split,
            split,
            split_rows,
            split,
            split,
            split,
            split_rows,
            split,
            split_rows,
            split,
            split,
            split,
        ),
        check_vma=False,
    )
```

```python
from functools import partial
import math

import jax
import jax.numpy as jnp
from jax import lax
from jax.experimental import pallas as pl
from jax.experimental.pallas import tpu as pltpu
from jax.sharding import PartitionSpec as P

HEAD_DIM = 64
LANES = 128
CHUNK = 64
PARTS = 4
EPSILON = 1e-06
AXES = ("dp", "seq")
BF16, F32 = jnp.bfloat16, jnp.float32

NN = (((1,), (0,)), ((), ()))
NT = (((1,), (1,)), ((), ()))
TN = (((0,), (0,)), ((), ()))


def narrow(value):
    return value.astype(BF16)


def widen(value):
    return value.astype(F32)


def after(value, *others):
    return lax.optimization_barrier((value,) + others)[0]


def dot(left, right, dims=NN):
    return lax.dot_general(left, right, dims, preferred_element_type=F32)


def shape(dims, dtype=BF16):
    return jax.ShapeDtypeStruct(dims, dtype)


def like(value):
    return jax.ShapeDtypeStruct(value.shape, value.dtype)


def fixed(dims, *index):
    at = tuple(index) or (0,) * len(dims)
    return pl.BlockSpec(dims, lambda *_: at)


SCALARS = pl.BlockSpec(memory_space=pltpu.SMEM)
ANYWHERE = pl.BlockSpec(memory_space=pl.ANY)


def row_sum(value):
    return jnp.sum(value, axis=0, keepdims=True)


def kernel(body, name, flops, touched, **options):
    return pl.pallas_call(
        body,
        name=name,
        compiler_params=pltpu.CompilerParams(vmem_limit_bytes=60 << 20),
        cost_estimate=pl.CostEstimate(flops=flops, bytes_accessed=touched, transcendentals=0),
        **options,
    )


def unite(target, own, other, spots):
    side, chip = spots[1], spots[2]
    rows = own[0].shape[0]
    for index in range(PARTS):
        for half, value in ((side, own[index]), (1 - side, other[index])):
            start = pl.multiple_of((2 * (chip ^ index) + half) * rows, rows)
            target[pl.ds(start, rows), :] = value[...]


def divide(source, keep, send, side, columns):
    count, rows = keep.shape[:2]
    for index in range(count):
        for half, target in ((side, keep), (1 - side, send)):
            start = pl.multiple_of((2 * index + half) * rows, rows)
            target[index, :, columns] = source[pl.ds(start, rows), :]


def gathered_specs(gathered, columns, index):
    block = (gathered[0].shape[0], columns)
    return [pl.BlockSpec(block, lambda *at: (0, index(*at)))] * len(gathered)


def as_columns(rows):
    width = rows[0].shape[1]
    padding = jnp.zeros((LANES - len(rows), width), F32)
    return jnp.concatenate(list(rows) + [padding], axis=0).T


def prepare_attention_body(packed_weight, output_weight, *rest):
    *vectors, out = rest
    seq, small, _ = out.shape
    lane = lax.broadcasted_iota(jnp.int32, (1, LANES), 1)
    block, column = 0.0, 0
    for vector in vectors:
        per = vector.shape[1] // small
        for part in range(per):
            value = jnp.where(spread_mask(small, per, part), vector[...], 0.0)
            value = jnp.sum(value, axis=1, keepdims=True)
            block = block + jnp.where(lane == column, value, 0.0)
            column += 1
    shard = jnp.concatenate(
        [narrow(packed_weight[...]), narrow(output_weight[...]), narrow(block)], axis=1
    )
    for index in range(seq):
        out[index] = shard


def prepare_attention(seq, packed_weight, output_weight, vectors):
    small, wide = packed_weight.shape
    vectors = [vector.reshape(1, -1) for vector in vectors]
    return kernel(
        prepare_attention_body,
        "prepare_attention",
        0,
        16 * small * wide,
        out_shape=shape((seq, small, wide + LANES + output_weight.shape[1])),
    )(packed_weight, output_weight, *vectors)


def prepare_feed_body(inner_weight, outer_weight, out):
    seq, small, _ = out.shape
    wide, width = inner_weight.shape[1], outer_weight.shape[1]
    out[0, :, :wide] = narrow(inner_weight[...])
    for index in range(outer_weight.shape[0] // small):
        start = wide + index * width
        block = outer_weight[index * small : (index + 1) * small]
        out[0, :, start : start + width] = narrow(block)
    for index in range(1, seq):
        out[index] = out[0]


def prepare_feed(seq, inner_weight, outer_weight):
    small, wide = inner_weight.shape
    return kernel(
        prepare_feed_body,
        "prepare_feed",
        0,
        16 * small * wide,
        out_shape=shape((seq, small, 2 * wide)),
    )(inner_weight, outer_weight)


def unite_attention_body(spots, *refs):
    parts, (packed, output, rows, bias, vectors) = refs[: 2 * PARTS], refs[2 * PARTS :]
    width, wide = packed.shape
    for target, start in ((packed, 0), (output, wide), (vectors, wide + width)):
        views = [part.at[:, start : start + target.shape[1]] for part in parts]
        unite(target, views[:PARTS], views[PARTS:], spots)
    rows[...] = widen(vectors[...]).T[:8]
    share, block = width // PARTS, bias.shape[1] // PARTS
    per = block // share
    for index in range(PARTS):
        line = 0.0
        for column in range(per):
            value = widen(vectors[index * share : (index + 1) * share, 8 + column : 9 + column])
            line = line + jnp.where(spread_mask(share, per, column), value, 0.0)
        bias[:, index * block : (index + 1) * block] = row_sum(line)


def unite_attention(spots, gathered, wide):
    rows, columns = gathered[0].shape
    width = 2 * PARTS * rows
    whole = pl.BlockSpec(memory_space=pltpu.VMEM)
    return kernel(
        unite_attention_body,
        "unite_attention",
        0,
        4 * width * columns,
        in_specs=[SCALARS] + [whole] * len(gathered),
        out_specs=[whole] * 4,
        out_shape=[
            shape((width, 3 * width)),
            shape((width, width)),
            shape((8, width), F32),
            shape((1, wide), F32),
        ],
        scratch_shapes=[pltpu.VMEM((width, LANES), BF16)],
    )(spots, *gathered)


def project_body(tokens, weight, rows, packed, flat):
    part = pl.program_id(0)
    seq, count, places, width = tokens.shape
    length = seq * places

    @pl.when(part == 0)
    def _():
        for row in range(count):
            flat[row * length : (row + 1) * length] = tokens[:, row].reshape(length, width)

    query, value = rows[0:1], rows[1:2]
    bias = jnp.where(part == 0, query, jnp.where(part == 2, value, jnp.zeros_like(query)))
    result = narrow(dot(flat[...], weight[...]) + bias)
    packed[...] = result.reshape(packed.shape)


def project(tokens, weight, rows):
    seq, count, places, width = tokens.shape
    length = seq * places
    return kernel(
        project_body,
        "project",
        6 * count * length * width * width,
        8 * count * length * width,
        grid=(3,),
        in_specs=[
            fixed(tokens.shape),
            pl.BlockSpec((width, width), lambda i: (0, i)),
            fixed(rows.shape),
        ],
        out_specs=[
            pl.BlockSpec((count, length, width), lambda i: (0, 0, i)),
            fixed((count * length, width)),
        ],
        out_shape=[shape((count, length, 3 * width)), shape((count * length, width))],
    )(tokens, weight, rows)


def pair_labels(places, lengths, row):
    label, bound = jnp.zeros_like(places), 0
    for pair in range(lengths.shape[1] - 1):
        bound = bound + lengths[row, pair]
        label = label + (places >= bound).astype(jnp.int32)
    return label


def attend_body(spots, lengths, query, key, value, context, probs, bias, scores):
    length = bias.shape[0]

    @pl.when(pl.program_id(1) == 0)
    def _():
        at = spots[0] * pl.num_programs(0) + pl.program_id(0)
        down = pair_labels(lax.broadcasted_iota(jnp.int32, (length, 1), 0), lengths, at)
        along = pair_labels(lax.broadcasted_iota(jnp.int32, (1, length), 1), lengths, at)
        bias[...] = jnp.where(down == along, 0.0, -1e30)

    lane = lax.broadcasted_iota(jnp.int32, (1, LANES), 1)
    values = value[0]
    queries = query[0] * BF16(HEAD_DIM**-0.5)
    for head in range(2):
        mine = (lane >= HEAD_DIM) == bool(head)
        scores[head] = dot(jnp.where(mine, queries, BF16(0)), key[0], NT)
    parts = []
    for head in range(2):
        for start in range(0, length, CHUNK):
            rows = slice(start, start + CHUNK)
            masked = scores[head, rows] + bias[rows]
            raised = jnp.exp(masked - jnp.max(masked, axis=-1, keepdims=True))
            total = jnp.sum(raised, axis=-1, keepdims=True)
            probs[0, head, rows] = narrow(raised * (1.0 / total))
        parts.append(dot(probs[0, head], values))
    context[0] = narrow(jnp.where(lane < HEAD_DIM, parts[0], parts[1]))


def head_pair(length, offset):
    return pl.BlockSpec((1, length, LANES), lambda r, p: (r, 0, offset + p))


def attend(spots, lengths, packed):
    rows, length, wide = packed.shape
    pairs = wide // 3 // LANES
    return kernel(
        attend_body,
        "attend",
        rows * pairs * 16 * length * length * LANES,
        rows * pairs * 8 * length * length,
        grid=(rows, pairs),
        in_specs=[SCALARS, SCALARS] + [head_pair(length, part * pairs) for part in range(3)],
        out_specs=[
            head_pair(length, 0),
            pl.BlockSpec((1, 2, length, length), lambda r, p: (r, p, 0, 0)),
        ],
        out_shape=[shape((rows, length, wide // 3)), shape((rows, 2 * pairs, length, length))],
        scratch_shapes=[pltpu.VMEM((length, length), F32), pltpu.VMEM((2, length, length), F32)],
    )(spots, lengths, packed, packed, packed)


def attend_back_body(query, key, value, upstream, probs, grads, sums, prob_grad, score_grad):
    pair, pairs = pl.program_id(1), pl.num_programs(1)
    lane = lax.broadcasted_iota(jnp.int32, (1, LANES), 1)
    scale = BF16(HEAD_DIM**-0.5)
    queries, keys, values, up = query[0] * scale, key[0], value[0], upstream[0]
    scaled_keys = keys * scale
    length = keys.shape[0]
    query_parts, key_grad, value_grad = [], 0.0, 0.0
    mine = [(lane >= HEAD_DIM) == bool(head) for head in range(2)]
    ups = [jnp.where(lanes, up, BF16(0)) for lanes in mine]
    for head in range(2):
        prob_grad[head] = dot(ups[head], values, NT)
    for head in range(2):
        for start in range(0, length, CHUNK):
            rows = slice(start, start + CHUNK)
            softmaxed = widen(probs[0, head, rows])
            product = softmaxed * prob_grad[head, rows]
            weighted = jnp.sum(product, axis=-1, keepdims=True)
            score_grad[head, rows] = narrow(product - softmaxed * weighted)
    for head in range(2):
        queries_mine = jnp.where(mine[head], queries, BF16(0))
        query_parts.append(dot(score_grad[head], scaled_keys))
        key_grad = key_grad + dot(queries_mine, score_grad[head], TN)
        value_grad = value_grad + dot(ups[head], probs[0, head], TN)
    query_grad = jnp.where(lane < HEAD_DIM, query_parts[0], query_parts[1])
    for part, grad in enumerate((query_grad, key_grad.T, value_grad.T)):
        at = pl.ds(pl.multiple_of((part * pairs + pair) * LANES, LANES), LANES)
        rounded = narrow(grad)
        grads[0, :, at] = rounded
        sums[0, :, at] = row_sum(widen(rounded))


def attend_back(packed, probs, upstream):
    rows, length, wide = packed.shape
    pairs = wide // 3 // LANES
    return kernel(
        attend_back_body,
        "attend_back",
        rows * pairs * 16 * length * length * LANES,
        rows * pairs * 8 * length * length,
        grid=(rows, pairs),
        in_specs=[head_pair(length, part * pairs) for part in range(3)]
        + [
            head_pair(length, 0),
            pl.BlockSpec((1, 2, length, length), lambda r, p: (r, p, 0, 0)),
        ],
        out_specs=[
            pl.BlockSpec((1, length, wide), lambda r, p: (r, 0, 0)),
            pl.BlockSpec((1, 1, wide), lambda r, p: (r, 0, 0)),
        ],
        out_shape=[shape(packed.shape), shape((rows, 1, wide), F32)],
        scratch_shapes=[
            pltpu.VMEM((2, length, length), F32),
            pltpu.VMEM((2, length, length), BF16),
        ],
    )(packed, packed, packed, upstream, probs)


def normed_of(summed):
    centred = summed - jnp.mean(summed, axis=-1, keepdims=True)
    variance = jnp.mean(centred * centred, axis=-1, keepdims=True)
    inverse = lax.rsqrt(variance + EPSILON)
    return centred * inverse, inverse


def norm_back(upstream, normed, inverse, gain):
    scaled = upstream * gain
    first_mean = jnp.mean(scaled, axis=-1, keepdims=True)
    second_mean = jnp.mean(scaled * normed, axis=-1, keepdims=True)
    return inverse * (scaled - first_mean - normed * second_mean)


def settle_body(context, tokens, rows, weight, normed, inverse, low):
    summed = widen(tokens[...]) + dot(context[...], weight[...]) + rows[2:3]
    normed[...], inverse[...] = normed_of(summed)
    low[...] = narrow(normed[...] * rows[3:4] + rows[4:5])


def settle(context, tokens, rows, weight):
    count, width = context.shape
    block = count // 2
    tall = pl.BlockSpec((block, width), lambda i: (i, 0))
    return kernel(
        settle_body,
        "settle",
        2 * count * width * width,
        10 * count * width,
        grid=(2,),
        in_specs=[tall, tall, fixed(rows.shape), fixed(weight.shape)],
        out_specs=[tall, pl.BlockSpec((block, 1), lambda i: (i, 0)), tall],
        out_shape=[shape((count, width), F32), shape((count, 1), F32), shape((count, width))],
    )(context, tokens, rows, weight)


def spread_mask(rows, per, column):
    down = lax.broadcasted_iota(jnp.int32, (rows, rows * per), 0)
    along = lax.broadcasted_iota(jnp.int32, (rows, rows * per), 1)
    return along == down * per + column


def stack_blocks(part):
    seq, rows, wide = part.shape
    width = wide // PARTS
    blocks = [
        widen(part[place, :, index * width : (index + 1) * width])
        for place in range(seq)
        for index in range(PARTS)
    ]
    return narrow(jnp.concatenate(blocks, axis=0))


def feed_body(spots, low, bias, normed_one, rows, *refs):
    inners, outers = refs[: 2 * PARTS], refs[2 * PARTS : 4 * PARTS]
    (
        active, slope, normed_two, inverse_two, output, inner_weight, outer_weight,
        branch, staged, sems,
    ) = refs[4 * PARTS :]
    step, steps = pl.program_id(0), pl.num_programs(0)
    wide = staged.shape[-1]
    copies = [
        pltpu.make_async_copy(
            outer.at[:, :, pl.ds(wide, wide)], staged.at[index], sems.at[index]
        )
        for index, outer in enumerate(outers)
    ]

    @pl.when(step == 0)
    def _():
        for copy in copies:
            copy.start()

    unite(inner_weight, inners[:PARTS], inners[PARTS:], spots)
    inner = dot(low[...], inner_weight[...]) + bias[...]
    share = 0.5 * (1.0 + lax.erf(inner * math.sqrt(0.5)))
    raised = jnp.exp(-0.5 * inner * inner) * (1.0 / math.sqrt(2.0 * math.pi))
    acted = narrow(inner * share)
    active[...] = acted
    slope[...] = narrow(share + inner * raised)
    for index in range(PARTS):

        @pl.when(step == spots[2] ^ index)
        def _():
            copies[index].wait()
            copies[PARTS + index].wait()
            half = outer_weight.shape[0] // 2
            for side, at in ((spots[1], index), (1 - spots[1], PARTS + index)):
                start = pl.multiple_of(side * half, half)
                outer_weight[pl.ds(start, half), :] = stack_blocks(staged.at[at])

    part = dot(acted, outer_weight[...])

    @pl.when(step == 0)
    def _():
        branch[...] = part

    @pl.when(step > 0)
    def _():
        branch[...] += part

    height = normed_one.shape[0]
    at = pl.ds(pl.multiple_of(step * height, height), height)
    branch[at, :] += normed_one[...] * rows[3:4] + (rows[4:5] + rows[5:6])

    @pl.when(step == steps - 1)
    def _():
        normed_two[...], inverse_two[...] = normed_of(branch[...])
        result = narrow(normed_two[...] * rows[6:7] + rows[7:8])
        seq, count, places, width = output.shape
        result = result.reshape(count, seq, places, width)
        for row in range(count):
            output[:, row] = result[row]


def feed(spots, low, bias, normed_one, rows, gathered, dims):
    count, width = low.shape
    wide = gathered[0].shape[1] // 2
    block = wide // PARTS
    deep = [part.reshape(dims[0], -1, 2 * wide) for part in gathered]
    all_of = fixed((count, width))
    across = pl.BlockSpec((count, block), lambda f: (0, f))
    return kernel(
        feed_body,
        "feed",
        4 * count * width * wide,
        12 * count * wide,
        grid=(PARTS,),
        in_specs=[
            SCALARS,
            all_of,
            pl.BlockSpec((1, block), lambda f: (0, f)),
            pl.BlockSpec((count // PARTS, width), lambda f: (f, 0)),
            fixed(rows.shape),
        ]
        + gathered_specs(gathered, block, lambda f: f)
        + [ANYWHERE] * len(deep),
        out_specs=[
            across,
            across,
            all_of,
            fixed((count, 1)),
            fixed(dims),
            pl.BlockSpec((width, block), lambda f: (0, f)),
            pl.BlockSpec((block, width), lambda f: (f, 0)),
        ],
        out_shape=[
            shape((count, wide)),
            shape((count, wide)),
            shape((count, width), F32),
            shape((count, 1), F32),
            shape(dims),
            shape((width, wide)),
            shape((wide, width)),
        ],
        scratch_shapes=[
            pltpu.VMEM((count, width), F32),
            pltpu.VMEM((len(deep),) + deep[0].shape[:2] + (wide,), BF16),
            pltpu.SemaphoreType.DMA((len(deep),)),
        ],
    )(spots, low, bias, normed_one, rows, *gathered, *deep)


def feed_back_body(
    spots, cotangent, normed_two, inverse_two, rows_one, low, inner_weight, outer_weight, active, slope,
    keep_inner, send_inner, keep_outer, send_outer, keep_vectors, send_vectors, hidden_grad,
    up, made, columns,
):
    step, steps, side = pl.program_id(0), pl.num_programs(0), spots[1]
    block = inner_weight.shape[-1]

    @pl.when(step == 0)
    def _():
        rows, width = cotangent.shape[1], cotangent.shape[-1]
        upstream = jnp.concatenate(
            [widen(cotangent[:, row]).reshape(-1, width) for row in range(rows)], axis=0
        )
        normed = normed_two[...]
        hidden_grad[...] = norm_back(upstream, normed, inverse_two[...], rows_one[6:7])
        up[...] = narrow(hidden_grad[...])
        columns[...] = as_columns(
            (row_sum(widen(up[...])), row_sum(upstream * normed), row_sum(upstream))
        )

    inner_grad = narrow(dot(up[...], outer_weight[...], NT) * widen(slope[...]))
    made[...] = narrow(dot(low[...], inner_grad, TN))
    divide(made, keep_inner, send_inner, side, slice(None))
    hidden_grad[...] += dot(inner_grad, inner_weight[...], NT)
    made[...] = narrow(dot(active[...], up[...], TN))
    divide(made, keep_outer, send_outer, side, slice(None))

    bias = row_sum(widen(inner_grad))
    share_rows = columns.shape[0] // PARTS
    per = block // share_rows
    lane = lax.broadcasted_iota(jnp.int32, (1, LANES), 1)
    total = 0.0
    for column in range(per):
        value = jnp.sum(
            jnp.where(spread_mask(share_rows, per, column), bias, 0.0), axis=1, keepdims=True
        )
        total = total + jnp.where(lane == 3 + column, value, 0.0)
    columns[pl.ds(pl.multiple_of(step * share_rows, share_rows), share_rows), :] += total

    @pl.when(step == steps - 1)
    def _():
        made[:, :LANES] = narrow(columns[...])
        divide(made.at[:, :LANES], keep_vectors, send_vectors, side, slice(None))


def feed_back(spots, cotangent, normed_two, inverse_two, rows, low, inner, outer, active, slope):
    count, width = low.shape
    wide = inner.shape[1]
    block = wide // PARTS
    all_of = fixed((count, width))
    across = pl.BlockSpec((count, block), lambda f: (0, f))
    first, second = (PARTS, width // PARTS // 2, wide), (PARTS, block // 2, width)
    third = first[:2] + (LANES,)
    right = pl.BlockSpec(first[:2] + (block,), lambda f: (0, 0, f))
    down = pl.BlockSpec((1,) + second[1:], lambda f: (f, 0, 0))
    return kernel(
        feed_back_body,
        "feed_back",
        8 * count * width * wide,
        12 * count * wide,
        grid=(PARTS,),
        in_specs=[SCALARS, fixed(cotangent.shape), all_of, fixed((count, 1)), fixed(rows.shape), all_of]
        + [
            pl.BlockSpec((width, block), lambda f: (0, f)),
            pl.BlockSpec((block, width), lambda f: (f, 0)),
            across,
            across,
        ],
        out_specs=[right, right, down, down, fixed(third), fixed(third), all_of],
        out_shape=[shape(dims) for dims in (first, first, second, second, third, third)]
        + [shape((count, width), F32)],
        scratch_shapes=[
            pltpu.VMEM((count, width), BF16),
            pltpu.VMEM((width, block), BF16),
            pltpu.VMEM((width, LANES), F32),
        ],
    )(spots, cotangent, normed_two, inverse_two, rows, low, inner, outer, active, slope)


def settle_back_body(
    spots, hidden_grad, normed, inverse, rows, context, weight,
    first_up, context_grad, keep, send, sums, total, made,
):
    step, steps = pl.program_id(0), pl.num_programs(0)

    @pl.when(step == 0)
    def _():
        sums[...] = jnp.zeros_like(sums)
        total[...] = jnp.zeros_like(total)

    upstream = hidden_grad[...]
    up = norm_back(upstream, normed[...], inverse[...], rows[3:4])
    first_up[...] = up
    low = narrow(up)
    context_grad[...] = narrow(dot(low, weight[...], NT))
    total[...] += dot(context[...], low, TN)
    sums[0:1] += row_sum(widen(low))
    sums[1:2] += row_sum(upstream * normed[...])
    sums[2:3] += row_sum(upstream)

    @pl.when(step == steps - 1)
    def _():
        made[...] = narrow(total[...])
        divide(made, keep, send, spots[1], slice(None))


def settle_back(spots, hidden_grad, normed, inverse, rows, context, weight):
    count, width = context.shape
    block = count // 2
    tall = pl.BlockSpec((block, width), lambda i: (i, 0))
    dims = (PARTS, width // PARTS // 2, width)
    return kernel(
        settle_back_body,
        "settle_back",
        10**12,
        16 * count * width,
        grid=(2,),
        in_specs=[SCALARS, tall, tall, pl.BlockSpec((block, 1), lambda i: (i, 0))]
        + [fixed(rows.shape), tall, fixed((width, width))],
        out_specs=[tall, tall, fixed(dims), fixed(dims), fixed((8, width))],
        out_shape=[
            shape((count, width), F32),
            shape((count, width)),
            shape(dims),
            shape(dims),
            shape((8, width), F32),
        ],
        scratch_shapes=[pltpu.VMEM((width, width), F32), pltpu.VMEM((width, width), BF16)],
    )(spots, hidden_grad, normed, inverse, rows, context, weight)


def tokens_back_body(packed_grad, weight, first_up, grad):
    total = first_up[...] + dot(packed_grad[...], weight[...], NT)
    seq, _, places, width = grad.shape
    grad[:, 0] = narrow(total).reshape(seq, places, width)


def tokens_back(packed_grad, weight, first_up, dims):
    count, width = first_up.shape
    seq, rows, places, _ = dims
    length = seq * places
    return kernel(
        tokens_back_body,
        "tokens_back",
        6 * count * width * width,
        8 * count * width,
        grid=(rows,),
        in_specs=[
            pl.BlockSpec((length, 3 * width), lambda r: (r, 0)),
            fixed((width, 3 * width)),
            pl.BlockSpec((length, width), lambda r: (r, 0)),
        ],
        out_specs=pl.BlockSpec((seq, 1, places, width), lambda r: (0, r, 0, 0)),
        out_shape=shape(dims),
    )(packed_grad, weight, first_up)


def weights_back_body(spots, packed_grad, tokens, packed_sums, sums, keep, send, made):
    part, side = pl.program_id(0), spots[1]
    width = tokens.shape[1]
    made[...] = narrow(dot(tokens[...], packed_grad[...], TN))
    divide(made, keep, send, side, pl.ds(pl.multiple_of(part * width, width), width))

    @pl.when(part == 2)
    def _():
        packed = jnp.sum(packed_sums[...], axis=0)
        made[:, :LANES] = narrow(
            as_columns(
                (packed[:, :width], packed[:, 2 * width :], sums[0:1], sums[1:2], sums[2:3])
            )
        )
        divide(made.at[:, :LANES], keep, send, side, slice(3 * width, 3 * width + LANES))


def weights_back(spots, packed_grad, tokens, packed_sums, sums):
    count, width = tokens.shape
    dims = (PARTS, width // PARTS // 2, 3 * width + LANES)
    return kernel(
        weights_back_body,
        "weights_back",
        6 * count * width * width,
        8 * count * width,
        grid=(3,),
        in_specs=[SCALARS, pl.BlockSpec((count, width), lambda i: (0, i)), fixed(tokens.shape)]
        + [fixed(packed_sums.shape), fixed(sums.shape)],
        out_specs=[fixed(dims), fixed(dims)],
        out_shape=[shape(dims), shape(dims)],
        scratch_shapes=[pltpu.VMEM((width, width), BF16)],
    )(spots, packed_grad, tokens, packed_sums, sums)


def side_by_side(out, start, total):
    small, width = out.shape[0], total.shape[1]
    for height in range(0, total.shape[0], small):
        out[:, start : start + width] = narrow(total[height : height + small])
        start += width
    return start


def chip_sums(name, spots, pairs, seq, small):
    operands, in_specs = [], []
    wide = sum(kept.shape[1] // (seq * small) * kept.shape[2] for kept, _ in pairs)
    for kept, came in pairs:
        height = kept.shape[1] // seq
        for part in range(PARTS):
            block = pl.BlockSpec(
                (None, None, height, kept.shape[2]),
                lambda i, spots, part=part: (spots[2] ^ part, i, 0, 0),
            )
            for value in (kept, came):
                operands.append(value.reshape(PARTS, seq, height, value.shape[2]))
                in_specs.append(block)

    def body(spots, *refs):
        ins, outs = refs[: len(operands)], refs[len(operands) :]
        for part, out in enumerate(outs):
            start = 0
            for pair in range(len(pairs)):
                at = 2 * (pair * PARTS + part)
                start = side_by_side(out, start, widen(ins[at][...]) + widen(ins[at + 1][...]))

    return kernel(
        body,
        name,
        0,
        6 * PARTS * seq * small * wide,
        grid_spec=pltpu.PrefetchScalarGridSpec(
            num_scalar_prefetch=1,
            grid=(seq,),
            in_specs=in_specs,
            out_specs=[pl.BlockSpec((None, small, wide), lambda i, spots: (i, 0, 0))] * PARTS,
        ),
        out_shape=[shape((seq, small, wide))] * PARTS,
    )(spots, *operands)


def total_body(*refs):
    total = widen(refs[0][...])
    for ref in refs[1:-1]:
        total = total + widen(ref[...])
    refs[-1][...] = narrow(total)


def total_of(name, values, flops=0):
    seq, small, wide = values[0].shape
    block = pl.BlockSpec((None, small, wide), lambda i: (i, 0, 0))
    return kernel(
        total_body,
        name,
        flops,
        2 * (len(values) + 1) * seq * small * wide,
        grid=(seq,),
        in_specs=[block] * len(values),
        out_specs=block,
        out_shape=shape(values[0].shape),
    )(*values)


def total_pieces(name, spots, values):
    seq, small, wide = values[0].shape
    blocks = [
        pl.BlockSpec((None, small, wide), lambda i, spots, step=step: (lax.rem(spots[0] + step, seq), 0, 0))
        for step in range(seq)
    ]

    def body(spots, *refs):
        for step in range(seq):
            part = refs[step * len(values) : (step + 1) * len(values)]
            total_body(*part, refs[seq * len(values) + step])

    return kernel(
        body,
        name,
        0,
        2 * (len(values) + 1) * seq * small * wide,
        grid_spec=pltpu.PrefetchScalarGridSpec(
            num_scalar_prefetch=1,
            grid=(1,),
            in_specs=[block for block in blocks for _ in values],
            out_specs=[pl.BlockSpec((small, wide), lambda i, spots: (0, 0))] * seq,
        ),
        out_shape=[shape((small, wide))] * seq,
    )(spots, *(list(values) * seq))


def finish_body(count, vectors, blocks, *refs):
    pieces, outs = refs[:count], refs[count:]
    if count == 1:
        pieces = [pieces[0].at[index] for index in range(pieces[0].shape[0])]
    total = widen(pieces[0][...])
    for piece in pieces[1:]:
        total = total + widen(piece[...])
    small, wide = total.shape
    start = 0
    for out, (count, width) in zip(outs, blocks):
        for index in range(count):
            out[index * small : (index + 1) * small] = total[:, start : start + width]
            start += width
    at = wide - LANES
    for out, (column, per) in zip(outs[len(blocks) :], vectors):
        line = 0.0
        for part in range(per):
            value = total[:, at + column + part : at + column + part + 1]
            line = line + jnp.where(spread_mask(small, per, part), value, 0.0)
        out[...] = row_sum(line)


def finish(name, pieces, blocks, vectors):
    small, wide = pieces[0].shape[-2:]
    return kernel(
        partial(finish_body, len(pieces), vectors, blocks),
        name,
        0,
        8 * small * wide,
        out_shape=[shape((count * small, width), F32) for count, width in blocks]
        + [shape((1, small * per), F32) for _, per in vectors],
    )(*pieces)


def block_at(blocks, index, axis=0):
    return lax.dynamic_index_in_dim(blocks, index, axis, keepdims=False)


class Links:
    def __init__(self, mesh):
        self.dp, self.seq = mesh.shape["dp"], mesh.shape["seq"]
        self.bits = self.dp.bit_length() - 1
        assert self.dp == 1 << self.bits
        self.direct = self.dp == 2 * PARTS

    def across(self, value, flip):
        pairs = [
            (d * self.seq + s, (d ^ flip) * self.seq + s)
            for d in range(self.dp)
            for s in range(self.seq)
        ]
        return lax.ppermute(value, AXES, pairs)

    def along(self, value, step):
        pairs = [
            (d * self.seq + s, d * self.seq + (s + step) % self.seq)
            for d in range(self.dp)
            for s in range(self.seq)
        ]
        return lax.ppermute(value, AXES, pairs)

    def digit(self, bit):
        return (lax.axis_index("dp") >> bit) & 1

    def spots(self):
        place, dp = lax.axis_index("seq"), lax.axis_index("dp")
        side, chip = (dp & 1, dp >> 1) if self.direct else (0 * dp, 0 * dp)
        return jnp.stack([place, side, chip]).astype(jnp.int32)

    def turn(self, blocks):
        return lax.all_to_all(blocks, "seq", split_axis=0, concat_axis=0, tiled=True)

    def spread(self, held):
        return [held] + [self.across(held, 2 * part) for part in range(1, PARTS)]

    def swap(self, parts):
        parts = [part.reshape(-1, part.shape[-1]) for part in parts]
        return parts + [self.across(part, 1) for part in parts]

    def gather_whole(self, held):
        done = []
        for bit in range(self.bits):
            other, mine = self.across(held, 1 << bit), self.digit(bit)
            held = jnp.where(mine == 0, jnp.stack([held, other]), jnp.stack([other, held]))
        return held.reshape(self.dp * self.seq, *held.shape[self.bits + 1 :])

    def cut(self, whole):
        whole = whole.reshape(PARTS, 2, -1, whole.shape[-1])
        return [whole[part, side] for side in range(2) for part in range(PARTS)]

    def reduce_whole(self, keep, send):
        rows = keep.shape[0] * keep.shape[1] * 2 // (self.dp * self.seq)
        whole = jnp.stack([keep, send], axis=1)
        held = whole.reshape((2,) * self.bits + (self.seq, rows, keep.shape[-1]))
        for bit in reversed(range(self.bits)):
            mine = self.digit(bit)
            other = self.across(block_at(held, 1 - mine), 1 << bit)
            held = narrow(widen(block_at(held, mine)) + widen(other))
        return held


def shards(
    links,
    tokens,
    cotangent,
    lengths,
    packed_weight,
    query_bias,
    value_bias,
    output_weight,
    output_bias,
    first_gain,
    first_shift,
    inner_weight,
    inner_bias,
    outer_weight,
    outer_bias,
    second_gain,
    second_shift,
):
    row_count, places, width = tokens.shape
    seq, direct = links.seq, links.direct
    rows = row_count // seq
    dims = (seq, rows, places, width)
    small, tall = packed_weight.shape[0], outer_weight.shape[0]
    wide = inner_weight.shape[1]
    per = wide // width
    spots = links.spots()

    vectors = (
        query_bias, value_bias, output_bias, first_gain, first_shift,
        outer_bias, second_gain, second_shift, inner_bias,
    )
    held = links.turn(prepare_attention(seq, packed_weight, output_weight, vectors))
    feed_held = links.turn(after(prepare_feed(seq, inner_weight, outer_weight), held))
    if direct:
        held = links.spread(held)
        came = links.turn(after(tokens.reshape(dims), feed_held, *held))
        gathered = links.swap(held)
        feed_held = links.spread(feed_held)
    else:
        came = links.turn(after(tokens.reshape(dims), feed_held))
        gathered = links.cut(links.gather_whole(held))
        whole = links.gather_whole(feed_held)
        inner, outer = whole[..., :wide], whole[..., wide:]
        outer = outer.reshape(-1, small, per, width).swapaxes(1, 2)
        outer = outer.reshape(2 * PARTS * seq, per, -1, width).swapaxes(1, 2)
        inner, outer = inner.reshape(width, wide), outer.reshape(width, wide)
        feed_gathered = links.cut(jnp.concatenate([inner, outer], axis=1))
    cotangent_mine = links.turn(after(cotangent.reshape(dims), came))
    packed_whole, output_whole, rows_one, inner_bias_row = unite_attention(spots, gathered, wide)
    packed, flat = project(came, packed_whole, rows_one)
    context, probs = attend(spots, lengths, packed)
    context = context.reshape(-1, width)
    if direct:
        feed_held = [feed_held[0]] + [after(value, context) for value in feed_held[1:]]
        context = after(context, *feed_held)
        feed_gathered = links.swap(feed_held)
    normed_one, inverse_one, low = settle(context, flat, rows_one, output_whole)
    active, slope, normed_two, inverse_two, output, inner_whole, outer_whole = feed(
        spots, low, inner_bias_row, normed_one, rows_one, feed_gathered, dims
    )
    cotangent_mine = after(cotangent_mine, slope)
    output = after(output, cotangent_mine)
    cotangent_mine = after(cotangent_mine, output)
    (
        keep_inner, send_inner, keep_outer, send_outer, keep_vectors, send_vectors, hidden_grad,
    ) = feed_back(
        spots,
        cotangent_mine,
        normed_two,
        inverse_two,
        rows_one,
        low,
        inner_whole,
        outer_whole,
        active,
        slope,
    )
    hidden_grad = after(hidden_grad, send_inner, send_outer, send_vectors)
    first_up, context_grad, keep_output, send_output, sums = settle_back(
        spots, hidden_grad, normed_one, inverse_one, rows_one, context, output_whole
    )
    output = after(links.turn(output), sums)
    context_grad = after(context_grad, output)
    if direct:
        inner_came = after(links.across(send_inner, 1), sums)
        outer_came = after(links.across(send_outer, 1), sums)
        output_came = links.across(send_output, 1)
        vectors_came = after(links.across(send_vectors, 1), sums)
        pairs = [
            (keep_outer, outer_came),
            (keep_output, output_came),
            (keep_inner, inner_came),
            (keep_vectors, vectors_came),
        ]
        feed_sums = list(chip_sums("feed_chip_sums", spots, pairs, seq, small))
        context_grad = after(context_grad, *feed_sums[1:])
        feed_sums[1:] = [links.across(feed_sums[part], 2 * part) for part in range(1, PARTS)]
    packed_grad, packed_sums = attend_back(
        packed, probs, context_grad.reshape(rows, seq * places, width)
    )
    packed_grad = packed_grad.reshape(-1, 3 * width)
    grad = tokens_back(packed_grad, packed_whole, first_up, dims)
    tokens_grad = links.turn(grad)
    packed_grad = after(packed_grad, grad)
    keep, send = weights_back(spots, packed_grad, flat, packed_sums, sums)
    if direct:
        feed_sums[1:] = [after(value, keep) for value in feed_sums[1:]]
        feed_total = total_of("feed_total", feed_sums, 10**12)
        came = after(links.across(send, 1), feed_total)
        attention_sums = list(
            chip_sums("attention_chip_sums", spots, [(keep, came)], seq, small)
        )
        feed_total = after(feed_total, tokens_grad, *attention_sums[1:])
        attention_sums[1:] = [
            links.across(attention_sums[part], 2 * part) for part in range(1, PARTS)
        ]
        attention_total = total_pieces("attention_total", spots, attention_sums)
    else:
        reduced = [
            links.reduce_whole(*pair)
            for pair in (
                (keep_outer, send_outer),
                (keep_output, send_output),
                (keep_inner, send_inner),
                (keep_vectors, send_vectors),
            )
        ]
        reduced[0] = reduced[0].reshape(seq, per, small, width).swapaxes(1, 2)
        reduced[0] = reduced[0].reshape(seq, small, per * width)
        feed_total = jnp.concatenate(reduced, axis=2)
        attention_total = links.reduce_whole(keep, send)
        attention_total = [block_at(attention_total, (spots[0] + i) % seq) for i in range(seq)]
    feed_total = links.turn(feed_total)
    attention_total = [
        links.along(piece, step) if step else piece for step, piece in enumerate(attention_total)
    ]
    (
        outer_grad, output_grad, inner_grad,
        outer_bias_grad, second_gain_grad, second_shift_grad, inner_bias_grad,
    ) = finish(
        "finish_feed",
        [feed_total],
        [(per, width), (1, width), (1, wide)],
        [(0, 1), (1, 1), (2, 1), (3, per)],
    )
    tokens_grad = widen(tokens_grad)
    attention_total[1:] = [after(piece, inner_grad, tokens_grad) for piece in attention_total[1:]]
    (
        packed_weight_grad,
        query_bias_grad, value_bias_grad, output_bias_grad, first_gain_grad, first_shift_grad,
    ) = finish(
        "finish_attention", attention_total, [(1, 3 * width)], [(i, 1) for i in range(5)]
    )
    return (
        output.reshape(tokens.shape),
        tokens_grad.reshape(tokens.shape),
        packed_weight_grad,
        query_bias_grad.reshape(-1),
        value_bias_grad.reshape(-1),
        output_grad,
        output_bias_grad.reshape(-1),
        first_gain_grad.reshape(-1),
        first_shift_grad.reshape(-1),
        inner_grad,
        inner_bias_grad.reshape(-1),
        outer_grad,
        outer_bias_grad.reshape(-1),
        second_gain_grad.reshape(-1),
        second_shift_grad.reshape(-1),
    )


def solution(mesh):
    split = P(AXES)
    split_rows = P(AXES, None)
    packed_rows = P("dp", "seq", None)
    return jax.shard_map(
        partial(shards, Links(mesh)),
        mesh=mesh,
        in_specs=(
            packed_rows,
            packed_rows,
            P("dp", None),
            split_rows,
            split,
            split,
            split_rows,
            split,
            split,
            split,
            split_rows,
            split,
            split_rows,
            split,
            split,
            split,
        ),
        out_specs=(
            packed_rows,
            packed_rows,
            split_rows,
            split,
            split,
            split_rows,
            split,
            split,
            split,
            split_rows,
            split,
            split_rows,
            split,
            split,
            split,
        ),
        check_vma=False,
    )
```

```python
from functools import partial
import math

import jax
import jax.numpy as jnp
from jax import lax
from jax.experimental import pallas as pl
from jax.experimental.pallas import tpu as pltpu
from jax.sharding import PartitionSpec as P

HEAD_DIM = 64
LANES = 128
CHUNK = 64
PARTS = 4
EPSILON = 1e-06
AXES = ("dp", "seq")
BF16, F32 = jnp.bfloat16, jnp.float32

NN = (((1,), (0,)), ((), ()))
NT = (((1,), (1,)), ((), ()))
TN = (((0,), (0,)), ((), ()))


def narrow(value):
    return value.astype(BF16)


def widen(value):
    return value.astype(F32)


def after(value, *others):
    return lax.optimization_barrier((value,) + others)[0]


def dot(left, right, dims=NN):
    return lax.dot_general(left, right, dims, preferred_element_type=F32)


def shape(dims, dtype=BF16):
    return jax.ShapeDtypeStruct(dims, dtype)


def like(value):
    return jax.ShapeDtypeStruct(value.shape, value.dtype)


def fixed(dims, *index):
    at = tuple(index) or (0,) * len(dims)
    return pl.BlockSpec(dims, lambda *_: at)


SCALARS = pl.BlockSpec(memory_space=pltpu.SMEM)
ANYWHERE = pl.BlockSpec(memory_space=pl.ANY)


def row_sum(value):
    return jnp.sum(value, axis=0, keepdims=True)


def kernel(body, name, flops, touched, **options):
    return pl.pallas_call(
        body,
        name=name,
        compiler_params=pltpu.CompilerParams(vmem_limit_bytes=60 << 20),
        cost_estimate=pl.CostEstimate(flops=flops, bytes_accessed=touched, transcendentals=0),
        **options,
    )


def unite(target, own, other, spots):
    side, chip = spots[1], spots[2]
    rows = own[0].shape[0]
    for index in range(PARTS):
        for half, value in ((side, own[index]), (1 - side, other[index])):
            start = pl.multiple_of((2 * (chip ^ index) + half) * rows, rows)
            target[pl.ds(start, rows), :] = value[...]


def divide(source, keep, send, side, columns):
    count, rows = keep.shape[:2]
    for index in range(count):
        for half, target in ((side, keep), (1 - side, send)):
            start = pl.multiple_of((2 * index + half) * rows, rows)
            target[index, :, columns] = source[pl.ds(start, rows), :]


def gathered_specs(gathered, columns, index):
    block = (gathered[0].shape[0], columns)
    return [pl.BlockSpec(block, lambda *at: (0, index(*at)))] * len(gathered)


def as_columns(rows):
    width = rows[0].shape[1]
    padding = jnp.zeros((LANES - len(rows), width), F32)
    return jnp.concatenate(list(rows) + [padding], axis=0).T


def prepare_attention_body(packed_weight, output_weight, *rest):
    *vectors, out = rest
    seq, small, _ = out.shape
    lane = lax.broadcasted_iota(jnp.int32, (1, LANES), 1)
    block, column = 0.0, 0
    for vector in vectors:
        per = vector.shape[1] // small
        for part in range(per):
            value = jnp.where(spread_mask(small, per, part), vector[...], 0.0)
            value = jnp.sum(value, axis=1, keepdims=True)
            block = block + jnp.where(lane == column, value, 0.0)
            column += 1
    shard = jnp.concatenate(
        [narrow(packed_weight[...]), narrow(output_weight[...]), narrow(block)], axis=1
    )
    for index in range(seq):
        out[index] = shard


def prepare_attention(seq, packed_weight, output_weight, vectors):
    small, wide = packed_weight.shape
    vectors = [vector.reshape(1, -1) for vector in vectors]
    return kernel(
        prepare_attention_body,
        "prepare_attention",
        0,
        16 * small * wide,
        out_shape=shape((seq, small, wide + LANES + output_weight.shape[1])),
    )(packed_weight, output_weight, *vectors)


def prepare_feed_body(inner_weight, outer_weight, out):
    seq, small, _ = out.shape
    wide, width = inner_weight.shape[1], outer_weight.shape[1]
    out[0, :, :wide] = narrow(inner_weight[...])
    for index in range(outer_weight.shape[0] // small):
        start = wide + index * width
        block = outer_weight[index * small : (index + 1) * small]
        out[0, :, start : start + width] = narrow(block)
    for index in range(1, seq):
        out[index] = out[0]


def prepare_feed(seq, inner_weight, outer_weight):
    small, wide = inner_weight.shape
    return kernel(
        prepare_feed_body,
        "prepare_feed",
        0,
        16 * small * wide,
        out_shape=shape((seq, small, 2 * wide)),
    )(inner_weight, outer_weight)


def unite_attention_body(spots, *refs):
    parts, (packed, output, rows, bias, vectors) = refs[: 2 * PARTS], refs[2 * PARTS :]
    width, wide = packed.shape
    for target, start in ((packed, 0), (output, wide), (vectors, wide + width)):
        views = [part.at[:, start : start + target.shape[1]] for part in parts]
        unite(target, views[:PARTS], views[PARTS:], spots)
    rows[...] = widen(vectors[...]).T[:8]
    share, block = width // PARTS, bias.shape[1] // PARTS
    per = block // share
    for index in range(PARTS):
        line = 0.0
        for column in range(per):
            value = widen(vectors[index * share : (index + 1) * share, 8 + column : 9 + column])
            line = line + jnp.where(spread_mask(share, per, column), value, 0.0)
        bias[:, index * block : (index + 1) * block] = row_sum(line)


def unite_attention(spots, gathered, wide):
    rows, columns = gathered[0].shape
    width = 2 * PARTS * rows
    whole = pl.BlockSpec(memory_space=pltpu.VMEM)
    return kernel(
        unite_attention_body,
        "unite_attention",
        0,
        4 * width * columns,
        in_specs=[SCALARS] + [whole] * len(gathered),
        out_specs=[whole] * 4,
        out_shape=[
            shape((width, 3 * width)),
            shape((width, width)),
            shape((8, width), F32),
            shape((1, wide), F32),
        ],
        scratch_shapes=[pltpu.VMEM((width, LANES), BF16)],
    )(spots, *gathered)


def project_body(tokens, weight, rows, packed, flat):
    part = pl.program_id(0)
    seq, count, places, width = tokens.shape
    length = seq * places

    @pl.when(part == 0)
    def _():
        for row in range(count):
            flat[row * length : (row + 1) * length] = tokens[:, row].reshape(length, width)

    query, value = rows[0:1], rows[1:2]
    bias = jnp.where(part == 0, query, jnp.where(part == 2, value, jnp.zeros_like(query)))
    result = narrow(dot(flat[...], weight[...]) + bias)
    packed[...] = result.reshape(packed.shape)


def project(tokens, weight, rows):
    seq, count, places, width = tokens.shape
    length = seq * places
    return kernel(
        project_body,
        "project",
        6 * count * length * width * width,
        8 * count * length * width,
        grid=(3,),
        in_specs=[
            fixed(tokens.shape),
            pl.BlockSpec((width, width), lambda i: (0, i)),
            fixed(rows.shape),
        ],
        out_specs=[
            pl.BlockSpec((count, length, width), lambda i: (0, 0, i)),
            fixed((count * length, width)),
        ],
        out_shape=[shape((count, length, 3 * width)), shape((count * length, width))],
    )(tokens, weight, rows)


def pair_labels(places, lengths, row):
    label, bound = jnp.zeros_like(places), 0
    for pair in range(lengths.shape[1] - 1):
        bound = bound + lengths[row, pair]
        label = label + (places >= bound).astype(jnp.int32)
    return label


def attend_body(spots, lengths, query, key, value, context, probs, bias, scores):
    length = bias.shape[0]

    @pl.when(pl.program_id(1) == 0)
    def _():
        at = spots[0] * pl.num_programs(0) + pl.program_id(0)
        down = pair_labels(lax.broadcasted_iota(jnp.int32, (length, 1), 0), lengths, at)
        along = pair_labels(lax.broadcasted_iota(jnp.int32, (1, length), 1), lengths, at)
        bias[...] = jnp.where(down == along, 0.0, -1e30)

    lane = lax.broadcasted_iota(jnp.int32, (1, LANES), 1)
    values = value[0]
    queries = query[0] * BF16(HEAD_DIM**-0.5)
    for head in range(2):
        mine = (lane >= HEAD_DIM) == bool(head)
        scores[head] = dot(jnp.where(mine, queries, BF16(0)), key[0], NT)
    parts = []
    for head in range(2):
        for start in range(0, length, CHUNK):
            rows = slice(start, start + CHUNK)
            masked = scores[head, rows] + bias[rows]
            raised = jnp.exp(masked - jnp.max(masked, axis=-1, keepdims=True))
            total = jnp.sum(raised, axis=-1, keepdims=True)
            probs[0, head, rows] = narrow(raised * (1.0 / total))
        parts.append(dot(probs[0, head], values))
    context[0] = narrow(jnp.where(lane < HEAD_DIM, parts[0], parts[1]))


def head_pair(length, offset):
    return pl.BlockSpec((1, length, LANES), lambda r, p: (r, 0, offset + p))


def attend(spots, lengths, packed):
    rows, length, wide = packed.shape
    pairs = wide // 3 // LANES
    return kernel(
        attend_body,
        "attend",
        rows * pairs * 16 * length * length * LANES,
        rows * pairs * 8 * length * length,
        grid=(rows, pairs),
        in_specs=[SCALARS, SCALARS] + [head_pair(length, part * pairs) for part in range(3)],
        out_specs=[
            head_pair(length, 0),
            pl.BlockSpec((1, 2, length, length), lambda r, p: (r, p, 0, 0)),
        ],
        out_shape=[shape((rows, length, wide // 3)), shape((rows, 2 * pairs, length, length))],
        scratch_shapes=[pltpu.VMEM((length, length), F32), pltpu.VMEM((2, length, length), F32)],
    )(spots, lengths, packed, packed, packed)


def attend_back_body(query, key, value, upstream, probs, grads, sums, prob_grad, score_grad):
    pair, pairs = pl.program_id(1), pl.num_programs(1)
    lane = lax.broadcasted_iota(jnp.int32, (1, LANES), 1)
    scale = BF16(HEAD_DIM**-0.5)
    queries, keys, values, up = query[0] * scale, key[0], value[0], upstream[0]
    scaled_keys = keys * scale
    length = keys.shape[0]
    query_parts, key_grad, value_grad = [], 0.0, 0.0
    mine = [(lane >= HEAD_DIM) == bool(head) for head in range(2)]
    ups = [jnp.where(lanes, up, BF16(0)) for lanes in mine]
    for head in range(2):
        prob_grad[head] = dot(ups[head], values, NT)
    for head in range(2):
        for start in range(0, length, CHUNK):
            rows = slice(start, start + CHUNK)
            softmaxed = widen(probs[0, head, rows])
            product = softmaxed * prob_grad[head, rows]
            weighted = jnp.sum(product, axis=-1, keepdims=True)
            score_grad[head, rows] = narrow(product - softmaxed * weighted)
    for head in range(2):
        queries_mine = jnp.where(mine[head], queries, BF16(0))
        query_parts.append(dot(score_grad[head], scaled_keys))
        key_grad = key_grad + dot(queries_mine, score_grad[head], TN)
        value_grad = value_grad + dot(ups[head], probs[0, head], TN)
    query_grad = jnp.where(lane < HEAD_DIM, query_parts[0], query_parts[1])
    for part, grad in enumerate((query_grad, key_grad.T, value_grad.T)):
        at = pl.ds(pl.multiple_of((part * pairs + pair) * LANES, LANES), LANES)
        rounded = narrow(grad)
        grads[0, :, at] = rounded
        sums[0, :, at] = row_sum(widen(rounded))


def attend_back(packed, probs, upstream):
    rows, length, wide = packed.shape
    pairs = wide // 3 // LANES
    return kernel(
        attend_back_body,
        "attend_back",
        rows * pairs * 16 * length * length * LANES,
        rows * pairs * 8 * length * length,
        grid=(rows, pairs),
        in_specs=[head_pair(length, part * pairs) for part in range(3)]
        + [
            head_pair(length, 0),
            pl.BlockSpec((1, 2, length, length), lambda r, p: (r, p, 0, 0)),
        ],
        out_specs=[
            pl.BlockSpec((1, length, wide), lambda r, p: (r, 0, 0)),
            pl.BlockSpec((1, 1, wide), lambda r, p: (r, 0, 0)),
        ],
        out_shape=[shape(packed.shape), shape((rows, 1, wide), F32)],
        scratch_shapes=[
            pltpu.VMEM((2, length, length), F32),
            pltpu.VMEM((2, length, length), BF16),
        ],
    )(packed, packed, packed, upstream, probs)


def normed_of(summed):
    centred = summed - jnp.mean(summed, axis=-1, keepdims=True)
    variance = jnp.mean(centred * centred, axis=-1, keepdims=True)
    inverse = lax.rsqrt(variance + EPSILON)
    return centred * inverse, inverse


def norm_back(upstream, normed, inverse, gain):
    scaled = upstream * gain
    first_mean = jnp.mean(scaled, axis=-1, keepdims=True)
    second_mean = jnp.mean(scaled * normed, axis=-1, keepdims=True)
    return inverse * (scaled - first_mean - normed * second_mean)


def settle_body(context, tokens, rows, weight, normed, inverse, low):
    summed = widen(tokens[...]) + dot(context[...], weight[...]) + rows[2:3]
    normed[...], inverse[...] = normed_of(summed)
    low[...] = narrow(normed[...] * rows[3:4] + rows[4:5])


def settle(context, tokens, rows, weight):
    count, width = context.shape
    block = count // 2
    tall = pl.BlockSpec((block, width), lambda i: (i, 0))
    return kernel(
        settle_body,
        "settle",
        2 * count * width * width,
        10 * count * width,
        grid=(2,),
        in_specs=[tall, tall, fixed(rows.shape), fixed(weight.shape)],
        out_specs=[tall, pl.BlockSpec((block, 1), lambda i: (i, 0)), tall],
        out_shape=[shape((count, width), F32), shape((count, 1), F32), shape((count, width))],
    )(context, tokens, rows, weight)


def spread_mask(rows, per, column):
    down = lax.broadcasted_iota(jnp.int32, (rows, rows * per), 0)
    along = lax.broadcasted_iota(jnp.int32, (rows, rows * per), 1)
    return along == down * per + column


def stack_blocks(part):
    seq, rows, wide = part.shape
    width = wide // PARTS
    blocks = [
        widen(part[place, :, index * width : (index + 1) * width])
        for place in range(seq)
        for index in range(PARTS)
    ]
    return narrow(jnp.concatenate(blocks, axis=0))


def feed_body(spots, low, bias, normed_one, rows, *refs):
    inners, outers = refs[: 2 * PARTS], refs[2 * PARTS : 4 * PARTS]
    (
        active, slope, normed_two, inverse_two, output, inner_weight, outer_weight,
        branch, staged, sems,
    ) = refs[4 * PARTS :]
    step, steps = pl.program_id(0), pl.num_programs(0)
    wide = staged.shape[-1]
    copies = [
        pltpu.make_async_copy(
            outer.at[:, :, pl.ds(wide, wide)], staged.at[index], sems.at[index]
        )
        for index, outer in enumerate(outers)
    ]

    @pl.when(step == 0)
    def _():
        for copy in copies:
            copy.start()

    unite(inner_weight, inners[:PARTS], inners[PARTS:], spots)
    inner = dot(low[...], inner_weight[...]) + bias[...]
    share = 0.5 * (1.0 + lax.erf(inner * math.sqrt(0.5)))
    raised = jnp.exp(-0.5 * inner * inner) * (1.0 / math.sqrt(2.0 * math.pi))
    acted = narrow(inner * share)
    active[...] = acted
    slope[...] = narrow(share + inner * raised)
    for index in range(PARTS):

        @pl.when(step == spots[2] ^ index)
        def _():
            copies[index].wait()
            copies[PARTS + index].wait()
            half = outer_weight.shape[0] // 2
            for side, at in ((spots[1], index), (1 - spots[1], PARTS + index)):
                start = pl.multiple_of(side * half, half)
                outer_weight[pl.ds(start, half), :] = stack_blocks(staged.at[at])

    part = dot(acted, outer_weight[...])

    @pl.when(step == 0)
    def _():
        branch[...] = part

    @pl.when(step > 0)
    def _():
        branch[...] += part

    height = normed_one.shape[0]
    at = pl.ds(pl.multiple_of(step * height, height), height)
    branch[at, :] += normed_one[...] * rows[3:4] + (rows[4:5] + rows[5:6])

    @pl.when(step == steps - 1)
    def _():
        normed_two[...], inverse_two[...] = normed_of(branch[...])
        result = narrow(normed_two[...] * rows[6:7] + rows[7:8])
        seq, count, places, width = output.shape
        result = result.reshape(count, seq, places, width)
        for row in range(count):
            output[:, row] = result[row]


def feed(spots, low, bias, normed_one, rows, gathered, dims):
    count, width = low.shape
    wide = gathered[0].shape[1] // 2
    block = wide // PARTS
    deep = [part.reshape(dims[0], -1, 2 * wide) for part in gathered]
    all_of = fixed((count, width))
    across = pl.BlockSpec((count, block), lambda f: (0, f))
    return kernel(
        feed_body,
        "feed",
        4 * count * width * wide,
        12 * count * wide,
        grid=(PARTS,),
        in_specs=[
            SCALARS,
            all_of,
            pl.BlockSpec((1, block), lambda f: (0, f)),
            pl.BlockSpec((count // PARTS, width), lambda f: (f, 0)),
            fixed(rows.shape),
        ]
        + gathered_specs(gathered, block, lambda f: f)
        + [ANYWHERE] * len(deep),
        out_specs=[
            across,
            across,
            all_of,
            fixed((count, 1)),
            fixed(dims),
            pl.BlockSpec((width, block), lambda f: (0, f)),
            pl.BlockSpec((block, width), lambda f: (f, 0)),
        ],
        out_shape=[
            shape((count, wide)),
            shape((count, wide)),
            shape((count, width), F32),
            shape((count, 1), F32),
            shape(dims),
            shape((width, wide)),
            shape((wide, width)),
        ],
        scratch_shapes=[
            pltpu.VMEM((count, width), F32),
            pltpu.VMEM((len(deep),) + deep[0].shape[:2] + (wide,), BF16),
            pltpu.SemaphoreType.DMA((len(deep),)),
        ],
    )(spots, low, bias, normed_one, rows, *gathered, *deep)


def feed_back_body(
    spots, cotangent, normed_two, inverse_two, rows_one, low, inner_weight, outer_weight, active, slope,
    keep_inner, send_inner, keep_outer, send_outer, keep_vectors, send_vectors, hidden_grad,
    up, made, columns, pre, grads,
):
    step, steps, side = pl.program_id(0), pl.num_programs(0), spots[1]
    block = inner_weight.shape[-1]

    @pl.when(step == 0)
    def _():
        rows, width = cotangent.shape[1], cotangent.shape[-1]
        upstream = jnp.concatenate(
            [widen(cotangent[:, row]).reshape(-1, width) for row in range(rows)], axis=0
        )
        normed = normed_two[...]
        hidden_grad[...] = norm_back(upstream, normed, inverse_two[...], rows_one[6:7])
        up[...] = narrow(hidden_grad[...])
        columns[...] = as_columns(
            (row_sum(widen(up[...])), row_sum(upstream * normed), row_sum(upstream))
        )

    pre[...] = dot(up[...], outer_weight[...], NT)
    for start in range(0, pre.shape[0], 4 * CHUNK):
        down = slice(start, start + 4 * CHUNK)
        grads[down] = narrow(pre[down] * widen(slope[down]))
    inner_grad = grads[...]
    made[...] = narrow(dot(low[...], inner_grad, TN))
    divide(made, keep_inner, send_inner, side, slice(None))
    hidden_grad[...] += dot(inner_grad, inner_weight[...], NT)
    made[...] = narrow(dot(active[...], up[...], TN))
    divide(made, keep_outer, send_outer, side, slice(None))

    bias = row_sum(widen(inner_grad))
    share_rows = columns.shape[0] // PARTS
    per = block // share_rows
    lane = lax.broadcasted_iota(jnp.int32, (1, LANES), 1)
    total = 0.0
    for column in range(per):
        value = jnp.sum(
            jnp.where(spread_mask(share_rows, per, column), bias, 0.0), axis=1, keepdims=True
        )
        total = total + jnp.where(lane == 3 + column, value, 0.0)
    columns[pl.ds(pl.multiple_of(step * share_rows, share_rows), share_rows), :] += total

    @pl.when(step == steps - 1)
    def _():
        made[:, :LANES] = narrow(columns[...])
        divide(made.at[:, :LANES], keep_vectors, send_vectors, side, slice(None))


def feed_back(spots, cotangent, normed_two, inverse_two, rows, low, inner, outer, active, slope):
    count, width = low.shape
    wide = inner.shape[1]
    block = wide // PARTS
    all_of = fixed((count, width))
    across = pl.BlockSpec((count, block), lambda f: (0, f))
    first, second = (PARTS, width // PARTS // 2, wide), (PARTS, block // 2, width)
    third = first[:2] + (LANES,)
    right = pl.BlockSpec(first[:2] + (block,), lambda f: (0, 0, f))
    down = pl.BlockSpec((1,) + second[1:], lambda f: (f, 0, 0))
    return kernel(
        feed_back_body,
        "feed_back",
        8 * count * width * wide,
        12 * count * wide,
        grid=(PARTS,),
        in_specs=[SCALARS, fixed(cotangent.shape), all_of, fixed((count, 1)), fixed(rows.shape), all_of]
        + [
            pl.BlockSpec((width, block), lambda f: (0, f)),
            pl.BlockSpec((block, width), lambda f: (f, 0)),
            across,
            across,
        ],
        out_specs=[right, right, down, down, fixed(third), fixed(third), all_of],
        out_shape=[shape(dims) for dims in (first, first, second, second, third, third)]
        + [shape((count, width), F32)],
        scratch_shapes=[
            pltpu.VMEM((count, width), BF16),
            pltpu.VMEM((width, block), BF16),
            pltpu.VMEM((width, LANES), F32),
            pltpu.VMEM((count, block), F32),
            pltpu.VMEM((count, block), BF16),
        ],
    )(spots, cotangent, normed_two, inverse_two, rows, low, inner, outer, active, slope)


def settle_back_body(
    spots, hidden_grad, normed, inverse, rows, context, weight,
    first_up, context_grad, keep, send, sums, total, made,
):
    step, steps = pl.program_id(0), pl.num_programs(0)

    @pl.when(step == 0)
    def _():
        sums[...] = jnp.zeros_like(sums)
        total[...] = jnp.zeros_like(total)

    upstream = hidden_grad[...]
    up = norm_back(upstream, normed[...], inverse[...], rows[3:4])
    first_up[...] = up
    low = narrow(up)
    context_grad[...] = narrow(dot(low, weight[...], NT))
    total[...] += dot(context[...], low, TN)
    sums[0:1] += row_sum(widen(low))
    sums[1:2] += row_sum(upstream * normed[...])
    sums[2:3] += row_sum(upstream)

    @pl.when(step == steps - 1)
    def _():
        made[...] = narrow(total[...])
        divide(made, keep, send, spots[1], slice(None))


def settle_back(spots, hidden_grad, normed, inverse, rows, context, weight):
    count, width = context.shape
    block = count // 2
    tall = pl.BlockSpec((block, width), lambda i: (i, 0))
    dims = (PARTS, width // PARTS // 2, width)
    return kernel(
        settle_back_body,
        "settle_back",
        10**12,
        16 * count * width,
        grid=(2,),
        in_specs=[SCALARS, tall, tall, pl.BlockSpec((block, 1), lambda i: (i, 0))]
        + [fixed(rows.shape), tall, fixed((width, width))],
        out_specs=[tall, tall, fixed(dims), fixed(dims), fixed((8, width))],
        out_shape=[
            shape((count, width), F32),
            shape((count, width)),
            shape(dims),
            shape(dims),
            shape((8, width), F32),
        ],
        scratch_shapes=[pltpu.VMEM((width, width), F32), pltpu.VMEM((width, width), BF16)],
    )(spots, hidden_grad, normed, inverse, rows, context, weight)


def tokens_back_body(packed_grad, weight, first_up, grad):
    total = first_up[...] + dot(packed_grad[...], weight[...], NT)
    seq, _, places, width = grad.shape
    grad[:, 0] = narrow(total).reshape(seq, places, width)


def tokens_back(packed_grad, weight, first_up, dims):
    count, width = first_up.shape
    seq, rows, places, _ = dims
    length = seq * places
    return kernel(
        tokens_back_body,
        "tokens_back",
        6 * count * width * width,
        8 * count * width,
        grid=(rows,),
        in_specs=[
            pl.BlockSpec((length, 3 * width), lambda r: (r, 0)),
            fixed((width, 3 * width)),
            pl.BlockSpec((length, width), lambda r: (r, 0)),
        ],
        out_specs=pl.BlockSpec((seq, 1, places, width), lambda r: (0, r, 0, 0)),
        out_shape=shape(dims),
    )(packed_grad, weight, first_up)


def weights_back_body(spots, packed_grad, tokens, packed_sums, sums, keep, send, made):
    part, side = pl.program_id(0), spots[1]
    width = tokens.shape[1]
    made[...] = narrow(dot(tokens[...], packed_grad[...], TN))
    divide(made, keep, send, side, pl.ds(pl.multiple_of(part * width, width), width))

    @pl.when(part == 2)
    def _():
        packed = jnp.sum(packed_sums[...], axis=0)
        made[:, :LANES] = narrow(
            as_columns(
                (packed[:, :width], packed[:, 2 * width :], sums[0:1], sums[1:2], sums[2:3])
            )
        )
        divide(made.at[:, :LANES], keep, send, side, slice(3 * width, 3 * width + LANES))


def weights_back(spots, packed_grad, tokens, packed_sums, sums):
    count, width = tokens.shape
    dims = (PARTS, width // PARTS // 2, 3 * width + LANES)
    return kernel(
        weights_back_body,
        "weights_back",
        6 * count * width * width,
        8 * count * width,
        grid=(3,),
        in_specs=[SCALARS, pl.BlockSpec((count, width), lambda i: (0, i)), fixed(tokens.shape)]
        + [fixed(packed_sums.shape), fixed(sums.shape)],
        out_specs=[fixed(dims), fixed(dims)],
        out_shape=[shape(dims), shape(dims)],
        scratch_shapes=[pltpu.VMEM((width, width), BF16)],
    )(spots, packed_grad, tokens, packed_sums, sums)


def side_by_side(out, start, total):
    small, width = out.shape[0], total.shape[1]
    for height in range(0, total.shape[0], small):
        out[:, start : start + width] = narrow(total[height : height + small])
        start += width
    return start


def chip_sums(name, spots, pairs, seq, small):
    operands, in_specs = [], []
    wide = sum(kept.shape[1] // (seq * small) * kept.shape[2] for kept, _ in pairs)
    for kept, came in pairs:
        height = kept.shape[1] // seq
        for part in range(PARTS):
            block = pl.BlockSpec(
                (None, None, height, kept.shape[2]),
                lambda i, spots, part=part: (spots[2] ^ part, i, 0, 0),
            )
            for value in (kept, came):
                operands.append(value.reshape(PARTS, seq, height, value.shape[2]))
                in_specs.append(block)

    def body(spots, *refs):
        ins, outs = refs[: len(operands)], refs[len(operands) :]
        for part, out in enumerate(outs):
            start = 0
            for pair in range(len(pairs)):
                at = 2 * (pair * PARTS + part)
                start = side_by_side(out, start, widen(ins[at][...]) + widen(ins[at + 1][...]))

    return kernel(
        body,
        name,
        0,
        6 * PARTS * seq * small * wide,
        grid_spec=pltpu.PrefetchScalarGridSpec(
            num_scalar_prefetch=1,
            grid=(seq,),
            in_specs=in_specs,
            out_specs=[pl.BlockSpec((None, small, wide), lambda i, spots: (i, 0, 0))] * PARTS,
        ),
        out_shape=[shape((seq, small, wide))] * PARTS,
    )(spots, *operands)


def total_body(*refs):
    total = widen(refs[0][...])
    for ref in refs[1:-1]:
        total = total + widen(ref[...])
    refs[-1][...] = narrow(total)


def total_of(name, values, flops=0):
    seq, small, wide = values[0].shape
    block = pl.BlockSpec((None, small, wide), lambda i: (i, 0, 0))
    return kernel(
        total_body,
        name,
        flops,
        2 * (len(values) + 1) * seq * small * wide,
        grid=(seq,),
        in_specs=[block] * len(values),
        out_specs=block,
        out_shape=shape(values[0].shape),
    )(*values)


def total_pieces(name, spots, values):
    seq, small, wide = values[0].shape
    blocks = [
        pl.BlockSpec((None, small, wide), lambda i, spots, step=step: (lax.rem(spots[0] + step, seq), 0, 0))
        for step in range(seq)
    ]

    def body(spots, *refs):
        for step in range(seq):
            part = refs[step * len(values) : (step + 1) * len(values)]
            total_body(*part, refs[seq * len(values) + step])

    return kernel(
        body,
        name,
        0,
        2 * (len(values) + 1) * seq * small * wide,
        grid_spec=pltpu.PrefetchScalarGridSpec(
            num_scalar_prefetch=1,
            grid=(1,),
            in_specs=[block for block in blocks for _ in values],
            out_specs=[pl.BlockSpec((small, wide), lambda i, spots: (0, 0))] * seq,
        ),
        out_shape=[shape((small, wide))] * seq,
    )(spots, *(list(values) * seq))


def copied(value, *others):
    def body(source, target):
        target[...] = source[...]

    block = pl.BlockSpec((1,) + value.shape[1:], lambda i: (i,) + (0,) * (value.ndim - 1))
    return kernel(
        body,
        "copied",
        0,
        4 * math.prod(value.shape),
        grid=value.shape[:1],
        in_specs=[block],
        out_specs=block,
        out_shape=like(value),
    )(after(value, *others))


def finish_body(count, vectors, blocks, *refs):
    pieces, outs = refs[:count], refs[count:]
    if count == 1:
        pieces = [pieces[0].at[index] for index in range(pieces[0].shape[0])]
    total = widen(pieces[0][...])
    for piece in pieces[1:]:
        total = total + widen(piece[...])
    small, wide = total.shape
    start = 0
    for out, (count, width) in zip(outs, blocks):
        for index in range(count):
            out[index * small : (index + 1) * small] = total[:, start : start + width]
            start += width
    at = wide - LANES
    for out, (column, per) in zip(outs[len(blocks) :], vectors):
        line = 0.0
        for part in range(per):
            value = total[:, at + column + part : at + column + part + 1]
            line = line + jnp.where(spread_mask(small, per, part), value, 0.0)
        out[...] = row_sum(line)


def finish(name, pieces, blocks, vectors):
    small, wide = pieces[0].shape[-2:]
    return kernel(
        partial(finish_body, len(pieces), vectors, blocks),
        name,
        0,
        8 * small * wide,
        out_shape=[shape((count * small, width), F32) for count, width in blocks]
        + [shape((1, small * per), F32) for _, per in vectors],
    )(*pieces)


def block_at(blocks, index, axis=0):
    return lax.dynamic_index_in_dim(blocks, index, axis, keepdims=False)


class Links:
    def __init__(self, mesh):
        self.dp, self.seq = mesh.shape["dp"], mesh.shape["seq"]
        self.bits = self.dp.bit_length() - 1
        assert self.dp == 1 << self.bits
        self.direct = self.dp == 2 * PARTS

    def across(self, value, flip):
        pairs = [
            (d * self.seq + s, (d ^ flip) * self.seq + s)
            for d in range(self.dp)
            for s in range(self.seq)
        ]
        return lax.ppermute(value, AXES, pairs)

    def along(self, value, step):
        pairs = [
            (d * self.seq + s, d * self.seq + (s + step) % self.seq)
            for d in range(self.dp)
            for s in range(self.seq)
        ]
        return lax.ppermute(value, AXES, pairs)

    def digit(self, bit):
        return (lax.axis_index("dp") >> bit) & 1

    def spots(self):
        place, dp = lax.axis_index("seq"), lax.axis_index("dp")
        side, chip = (dp & 1, dp >> 1) if self.direct else (0 * dp, 0 * dp)
        return jnp.stack([place, side, chip]).astype(jnp.int32)

    def turn(self, blocks):
        return lax.all_to_all(blocks, "seq", split_axis=0, concat_axis=0, tiled=True)

    def spread(self, held):
        return [held] + [self.across(held, 2 * part) for part in range(1, PARTS)]

    def swap(self, parts):
        parts = [part.reshape(-1, part.shape[-1]) for part in parts]
        return parts + [self.across(part, 1) for part in parts]

    def gather_whole(self, held):
        done = []
        for bit in range(self.bits):
            other, mine = self.across(held, 1 << bit), self.digit(bit)
            held = jnp.where(mine == 0, jnp.stack([held, other]), jnp.stack([other, held]))
        return held.reshape(self.dp * self.seq, *held.shape[self.bits + 1 :])

    def cut(self, whole):
        whole = whole.reshape(PARTS, 2, -1, whole.shape[-1])
        return [whole[part, side] for side in range(2) for part in range(PARTS)]

    def reduce_whole(self, keep, send):
        rows = keep.shape[0] * keep.shape[1] * 2 // (self.dp * self.seq)
        whole = jnp.stack([keep, send], axis=1)
        held = whole.reshape((2,) * self.bits + (self.seq, rows, keep.shape[-1]))
        for bit in reversed(range(self.bits)):
            mine = self.digit(bit)
            other = self.across(block_at(held, 1 - mine), 1 << bit)
            held = narrow(widen(block_at(held, mine)) + widen(other))
        return held


def shards(
    links,
    tokens,
    cotangent,
    lengths,
    packed_weight,
    query_bias,
    value_bias,
    output_weight,
    output_bias,
    first_gain,
    first_shift,
    inner_weight,
    inner_bias,
    outer_weight,
    outer_bias,
    second_gain,
    second_shift,
):
    row_count, places, width = tokens.shape
    seq, direct = links.seq, links.direct
    rows = row_count // seq
    dims = (seq, rows, places, width)
    small, tall = packed_weight.shape[0], outer_weight.shape[0]
    wide = inner_weight.shape[1]
    per = wide // width
    spots = links.spots()

    vectors = (
        query_bias, value_bias, output_bias, first_gain, first_shift,
        outer_bias, second_gain, second_shift, inner_bias,
    )
    held = links.turn(prepare_attention(seq, packed_weight, output_weight, vectors))
    feed_held = links.turn(after(prepare_feed(seq, inner_weight, outer_weight), held))
    if direct:
        held = links.spread(held)
        came = links.turn(after(tokens.reshape(dims), feed_held, *held))
        gathered = links.swap(held)
        feed_held = links.spread(feed_held)
    else:
        came = links.turn(after(tokens.reshape(dims), feed_held))
        gathered = links.cut(links.gather_whole(held))
        whole = links.gather_whole(feed_held)
        inner, outer = whole[..., :wide], whole[..., wide:]
        outer = outer.reshape(-1, small, per, width).swapaxes(1, 2)
        outer = outer.reshape(2 * PARTS * seq, per, -1, width).swapaxes(1, 2)
        inner, outer = inner.reshape(width, wide), outer.reshape(width, wide)
        feed_gathered = links.cut(jnp.concatenate([inner, outer], axis=1))
    cotangent_mine = links.turn(after(cotangent.reshape(dims), came))
    packed_whole, output_whole, rows_one, inner_bias_row = unite_attention(spots, gathered, wide)
    packed, flat = project(came, packed_whole, rows_one)
    context, probs = attend(spots, lengths, packed)
    context = context.reshape(-1, width)
    if direct:
        feed_held = [feed_held[0]] + [after(value, context) for value in feed_held[1:]]
        context = after(context, *feed_held)
        feed_gathered = links.swap(feed_held)
    normed_one, inverse_one, low = settle(context, flat, rows_one, output_whole)
    active, slope, normed_two, inverse_two, output, inner_whole, outer_whole = feed(
        spots, low, inner_bias_row, normed_one, rows_one, feed_gathered, dims
    )
    cotangent_mine = after(cotangent_mine, slope)
    output = after(output, cotangent_mine)
    cotangent_mine = after(cotangent_mine, output)
    (
        keep_inner, send_inner, keep_outer, send_outer, keep_vectors, send_vectors, hidden_grad,
    ) = feed_back(
        spots,
        cotangent_mine,
        normed_two,
        inverse_two,
        rows_one,
        low,
        inner_whole,
        outer_whole,
        active,
        slope,
    )
    hidden_grad = after(hidden_grad, send_inner, send_outer, send_vectors)
    first_up, context_grad, keep_output, send_output, sums = settle_back(
        spots, hidden_grad, normed_one, inverse_one, rows_one, context, output_whole
    )
    output = after(links.turn(output), sums)
    context_grad = after(context_grad, output)
    if direct:
        inner_came = after(links.across(send_inner, 1), sums)
        outer_came = after(links.across(send_outer, 1), sums)
        output_came = links.across(send_output, 1)
        vectors_came = after(links.across(send_vectors, 1), sums)
        pairs = [
            (keep_outer, outer_came),
            (keep_output, output_came),
            (keep_inner, inner_came),
            (keep_vectors, vectors_came),
        ]
        feed_sums = list(chip_sums("feed_chip_sums", spots, pairs, seq, small))
        context_grad = after(context_grad, *feed_sums[1:])
        feed_sums[1:] = [links.across(feed_sums[part], 2 * part) for part in range(1, PARTS)]
    packed_grad, packed_sums = attend_back(
        packed, probs, context_grad.reshape(rows, seq * places, width)
    )
    packed_grad = packed_grad.reshape(-1, 3 * width)
    grad = tokens_back(packed_grad, packed_whole, first_up, dims)
    tokens_grad = links.turn(grad)
    packed_grad = after(packed_grad, grad)
    keep, send = weights_back(spots, packed_grad, flat, packed_sums, sums)
    output = copied(output, keep)
    if direct:
        feed_sums[1:] = [after(value, keep, output) for value in feed_sums[1:]]
        feed_total = total_of("feed_total", feed_sums, 10**12)
        came = after(links.across(send, 1), feed_total)
        attention_sums = list(
            chip_sums("attention_chip_sums", spots, [(keep, came)], seq, small)
        )
        feed_total = after(feed_total, tokens_grad, *attention_sums[1:])
        attention_sums[1:] = [
            links.across(attention_sums[part], 2 * part) for part in range(1, PARTS)
        ]
        attention_total = total_pieces("attention_total", spots, attention_sums)
    else:
        reduced = [
            links.reduce_whole(*pair)
            for pair in (
                (keep_outer, send_outer),
                (keep_output, send_output),
                (keep_inner, send_inner),
                (keep_vectors, send_vectors),
            )
        ]
        reduced[0] = reduced[0].reshape(seq, per, small, width).swapaxes(1, 2)
        reduced[0] = reduced[0].reshape(seq, small, per * width)
        feed_total = jnp.concatenate(reduced, axis=2)
        attention_total = links.reduce_whole(keep, send)
        attention_total = [block_at(attention_total, (spots[0] + i) % seq) for i in range(seq)]
    feed_total = links.turn(feed_total)
    attention_total = [
        links.along(piece, step) if step else piece for step, piece in enumerate(attention_total)
    ]
    (
        outer_grad, output_grad, inner_grad,
        outer_bias_grad, second_gain_grad, second_shift_grad, inner_bias_grad,
    ) = finish(
        "finish_feed",
        [feed_total],
        [(per, width), (1, width), (1, wide)],
        [(0, 1), (1, 1), (2, 1), (3, per)],
    )
    tokens_grad = widen(tokens_grad)
    attention_total[1:] = [after(piece, inner_grad, tokens_grad) for piece in attention_total[1:]]
    (
        packed_weight_grad,
        query_bias_grad, value_bias_grad, output_bias_grad, first_gain_grad, first_shift_grad,
    ) = finish(
        "finish_attention", attention_total, [(1, 3 * width)], [(i, 1) for i in range(5)]
    )
    return (
        output.reshape(tokens.shape),
        tokens_grad.reshape(tokens.shape),
        packed_weight_grad,
        query_bias_grad.reshape(-1),
        value_bias_grad.reshape(-1),
        output_grad,
        output_bias_grad.reshape(-1),
        first_gain_grad.reshape(-1),
        first_shift_grad.reshape(-1),
        inner_grad,
        inner_bias_grad.reshape(-1),
        outer_grad,
        outer_bias_grad.reshape(-1),
        second_gain_grad.reshape(-1),
        second_shift_grad.reshape(-1),
    )


def solution(mesh):
    split = P(AXES)
    split_rows = P(AXES, None)
    packed_rows = P("dp", "seq", None)
    return jax.shard_map(
        partial(shards, Links(mesh)),
        mesh=mesh,
        in_specs=(
            packed_rows,
            packed_rows,
            P("dp", None),
            split_rows,
            split,
            split,
            split_rows,
            split,
            split,
            split,
            split_rows,
            split,
            split_rows,
            split,
            split,
            split,
        ),
        out_specs=(
            packed_rows,
            packed_rows,
            split_rows,
            split,
            split,
            split_rows,
            split,
            split,
            split,
            split_rows,
            split,
            split_rows,
            split,
            split,
            split,
        ),
        check_vma=False,
    )
```

```python
from functools import partial
import math

import jax
import jax.numpy as jnp
from jax import lax
from jax.experimental import pallas as pl
from jax.experimental.pallas import tpu as pltpu
from jax.sharding import PartitionSpec as P

HEAD_DIM = 64
LANES = 128
CHUNK = 64
PARTS = 4
EPSILON = 1e-06
AXES = ("dp", "seq")
BF16, F32 = jnp.bfloat16, jnp.float32

NN = (((1,), (0,)), ((), ()))
NT = (((1,), (1,)), ((), ()))
TN = (((0,), (0,)), ((), ()))


def narrow(value):
    return value.astype(BF16)


def widen(value):
    return value.astype(F32)


def after(value, *others):
    return lax.optimization_barrier((value,) + others)[0]


def dot(left, right, dims=NN):
    return lax.dot_general(left, right, dims, preferred_element_type=F32)


def shape(dims, dtype=BF16):
    return jax.ShapeDtypeStruct(dims, dtype)


def like(value):
    return jax.ShapeDtypeStruct(value.shape, value.dtype)


def fixed(dims, *index):
    at = tuple(index) or (0,) * len(dims)
    return pl.BlockSpec(dims, lambda *_: at)


SCALARS = pl.BlockSpec(memory_space=pltpu.SMEM)
ANYWHERE = pl.BlockSpec(memory_space=pl.ANY)


def row_sum(value):
    return jnp.sum(value, axis=0, keepdims=True)


def kernel(body, name, flops, touched, **options):
    return pl.pallas_call(
        body,
        name=name,
        compiler_params=pltpu.CompilerParams(vmem_limit_bytes=60 << 20),
        cost_estimate=pl.CostEstimate(flops=flops, bytes_accessed=touched, transcendentals=0),
        **options,
    )


def unite(target, own, other, spots):
    side, chip = spots[1], spots[2]
    rows = own[0].shape[0]
    for index in range(PARTS):
        for half, value in ((side, own[index]), (1 - side, other[index])):
            start = pl.multiple_of((2 * (chip ^ index) + half) * rows, rows)
            target[pl.ds(start, rows), :] = value[...]


def divide(source, keep, send, side, columns):
    count, rows = keep.shape[:2]
    for index in range(count):
        for half, target in ((side, keep), (1 - side, send)):
            start = pl.multiple_of((2 * index + half) * rows, rows)
            target[index, :, columns] = source[pl.ds(start, rows), :]


def gathered_specs(gathered, columns, index):
    block = (gathered[0].shape[0], columns)
    return [pl.BlockSpec(block, lambda *at: (0, index(*at)))] * len(gathered)


def as_columns(rows):
    width = rows[0].shape[1]
    padding = jnp.zeros((LANES - len(rows), width), F32)
    return jnp.concatenate(list(rows) + [padding], axis=0).T


def prepare_attention_body(packed_weight, output_weight, *rest):
    *vectors, out = rest
    seq, small, _ = out.shape
    lane = lax.broadcasted_iota(jnp.int32, (1, LANES), 1)
    block, column = 0.0, 0
    for vector in vectors:
        per = vector.shape[1] // small
        for part in range(per):
            value = jnp.where(spread_mask(small, per, part), vector[...], 0.0)
            value = jnp.sum(value, axis=1, keepdims=True)
            block = block + jnp.where(lane == column, value, 0.0)
            column += 1
    shard = jnp.concatenate(
        [narrow(packed_weight[...]), narrow(output_weight[...]), narrow(block)], axis=1
    )
    for index in range(seq):
        out[index] = shard


def prepare_attention(seq, packed_weight, output_weight, vectors):
    small, wide = packed_weight.shape
    vectors = [vector.reshape(1, -1) for vector in vectors]
    return kernel(
        prepare_attention_body,
        "prepare_attention",
        0,
        16 * small * wide,
        out_shape=shape((seq, small, wide + LANES + output_weight.shape[1])),
    )(packed_weight, output_weight, *vectors)


def prepare_feed_body(inner_weight, outer_weight, out):
    seq, small, _ = out.shape
    wide, width = inner_weight.shape[1], outer_weight.shape[1]
    out[0, :, :wide] = narrow(inner_weight[...])
    for index in range(outer_weight.shape[0] // small):
        start = wide + index * width
        block = outer_weight[index * small : (index + 1) * small]
        out[0, :, start : start + width] = narrow(block)
    for index in range(1, seq):
        out[index] = out[0]


def prepare_feed(seq, inner_weight, outer_weight):
    small, wide = inner_weight.shape
    return kernel(
        prepare_feed_body,
        "prepare_feed",
        0,
        16 * small * wide,
        out_shape=shape((seq, small, 2 * wide)),
    )(inner_weight, outer_weight)


def unite_attention_body(spots, *refs):
    parts, (packed, output, rows, bias, vectors) = refs[: 2 * PARTS], refs[2 * PARTS :]
    width, wide = packed.shape
    for target, start in ((packed, 0), (output, wide), (vectors, wide + width)):
        views = [part.at[:, start : start + target.shape[1]] for part in parts]
        unite(target, views[:PARTS], views[PARTS:], spots)
    rows[...] = widen(vectors[...]).T[:8]
    share, block = width // PARTS, bias.shape[1] // PARTS
    per = block // share
    for index in range(PARTS):
        line = 0.0
        for column in range(per):
            value = widen(vectors[index * share : (index + 1) * share, 8 + column : 9 + column])
            line = line + jnp.where(spread_mask(share, per, column), value, 0.0)
        bias[:, index * block : (index + 1) * block] = row_sum(line)


def unite_attention(spots, gathered, wide):
    rows, columns = gathered[0].shape
    width = 2 * PARTS * rows
    whole = pl.BlockSpec(memory_space=pltpu.VMEM)
    return kernel(
        unite_attention_body,
        "unite_attention",
        0,
        4 * width * columns,
        in_specs=[SCALARS] + [whole] * len(gathered),
        out_specs=[whole] * 4,
        out_shape=[
            shape((width, 3 * width)),
            shape((width, width)),
            shape((8, width), F32),
            shape((1, wide), F32),
        ],
        scratch_shapes=[pltpu.VMEM((width, LANES), BF16)],
    )(spots, *gathered)


def project_body(tokens, weight, rows, packed, flat):
    part = pl.program_id(0)
    seq, count, places, width = tokens.shape
    length = seq * places

    @pl.when(part == 0)
    def _():
        for row in range(count):
            flat[row * length : (row + 1) * length] = tokens[:, row].reshape(length, width)

    query, value = rows[0:1], rows[1:2]
    bias = jnp.where(part == 0, query, jnp.where(part == 2, value, jnp.zeros_like(query)))
    result = narrow(dot(flat[...], weight[...]) + bias)
    packed[...] = result.reshape(packed.shape)


def project(tokens, weight, rows):
    seq, count, places, width = tokens.shape
    length = seq * places
    return kernel(
        project_body,
        "project",
        6 * count * length * width * width,
        8 * count * length * width,
        grid=(3,),
        in_specs=[
            fixed(tokens.shape),
            pl.BlockSpec((width, width), lambda i: (0, i)),
            fixed(rows.shape),
        ],
        out_specs=[
            pl.BlockSpec((count, length, width), lambda i: (0, 0, i)),
            fixed((count * length, width)),
        ],
        out_shape=[shape((count, length, 3 * width)), shape((count * length, width))],
    )(tokens, weight, rows)


def pair_labels(places, lengths, row):
    label, bound = jnp.zeros_like(places), 0
    for pair in range(lengths.shape[1] - 1):
        bound = bound + lengths[row, pair]
        label = label + (places >= bound).astype(jnp.int32)
    return label


def attend_body(spots, lengths, query, key, value, context, probs, bias, scores):
    length = bias.shape[0]

    @pl.when(pl.program_id(1) == 0)
    def _():
        at = spots[0] * pl.num_programs(0) + pl.program_id(0)
        down = pair_labels(lax.broadcasted_iota(jnp.int32, (length, 1), 0), lengths, at)
        along = pair_labels(lax.broadcasted_iota(jnp.int32, (1, length), 1), lengths, at)
        bias[...] = jnp.where(down == along, 0.0, -1e30)

    lane = lax.broadcasted_iota(jnp.int32, (1, LANES), 1)
    values = value[0]
    queries = query[0] * BF16(HEAD_DIM**-0.5)
    for head in range(2):
        mine = (lane >= HEAD_DIM) == bool(head)
        scores[head] = dot(jnp.where(mine, queries, BF16(0)), key[0], NT)
    parts = []
    for head in range(2):
        for start in range(0, length, CHUNK):
            rows = slice(start, start + CHUNK)
            masked = scores[head, rows] + bias[rows]
            raised = jnp.exp(masked - jnp.max(masked, axis=-1, keepdims=True))
            total = jnp.sum(raised, axis=-1, keepdims=True)
            probs[0, head, rows] = narrow(raised * (1.0 / total))
        parts.append(dot(probs[0, head], values))
    context[0] = narrow(jnp.where(lane < HEAD_DIM, parts[0], parts[1]))


def head_pair(length, offset):
    return pl.BlockSpec((1, length, LANES), lambda r, p: (r, 0, offset + p))


def attend(spots, lengths, packed):
    rows, length, wide = packed.shape
    pairs = wide // 3 // LANES
    return kernel(
        attend_body,
        "attend",
        rows * pairs * 16 * length * length * LANES,
        rows * pairs * 8 * length * length,
        grid=(rows, pairs),
        in_specs=[SCALARS, SCALARS] + [head_pair(length, part * pairs) for part in range(3)],
        out_specs=[
            head_pair(length, 0),
            pl.BlockSpec((1, 2, length, length), lambda r, p: (r, p, 0, 0)),
        ],
        out_shape=[shape((rows, length, wide // 3)), shape((rows, 2 * pairs, length, length))],
        scratch_shapes=[pltpu.VMEM((length, length), F32), pltpu.VMEM((2, length, length), F32)],
    )(spots, lengths, packed, packed, packed)


def attend_back_body(query, key, value, upstream, probs, *rest):
    grads, sums, prob_grad, score_grad = rest[-4:]
    pair, pairs = pl.program_id(0), pl.num_programs(0)
    lane = lax.broadcasted_iota(jnp.int32, (1, LANES), 1)
    scale = BF16(HEAD_DIM**-0.5)
    queries, keys, values, up = query[0] * scale, key[0], value[0], upstream[0]
    scaled_keys = keys * scale
    length = keys.shape[0]
    query_parts, key_grad, value_grad = [], 0.0, 0.0
    mine = [(lane >= HEAD_DIM) == bool(head) for head in range(2)]
    ups = [jnp.where(lanes, up, BF16(0)) for lanes in mine]
    for head in range(2):
        prob_grad[head] = dot(ups[head], values, NT)
    for head in range(2):
        for start in range(0, length, CHUNK):
            rows = slice(start, start + CHUNK)
            softmaxed = widen(probs[0, head, rows])
            product = softmaxed * prob_grad[head, rows]
            weighted = jnp.sum(product, axis=-1, keepdims=True)
            score_grad[head, rows] = narrow(product - softmaxed * weighted)
    for head in range(2):
        queries_mine = jnp.where(mine[head], queries, BF16(0))
        query_parts.append(dot(score_grad[head], scaled_keys))
        key_grad = key_grad + dot(queries_mine, score_grad[head], TN)
        value_grad = value_grad + dot(ups[head], probs[0, head], TN)
    query_grad = jnp.where(lane < HEAD_DIM, query_parts[0], query_parts[1])
    for part, grad in enumerate((query_grad, key_grad.T, value_grad.T)):
        at = pl.ds(pl.multiple_of((part * pairs + pair) * LANES, LANES), LANES)
        rounded = narrow(grad)
        grads[0, :, at] = rounded
        sums[0, :, at] = row_sum(widen(rounded))


def attend_back(packed, probs, upstream, row, prior=()):
    rows, length, wide = packed.shape
    pairs = wide // 3 // LANES

    def columns(offset):
        return pl.BlockSpec((1, length, LANES), lambda p: (row, 0, offset + p))

    return kernel(
        attend_back_body,
        "attend_back",
        10**12 if row else 0,
        pairs * 8 * length * length,
        grid=(pairs,),
        in_specs=[columns(part * pairs) for part in range(3)]
        + [columns(0), pl.BlockSpec((1, 2, length, length), lambda p: (row, p, 0, 0))]
        + [ANYWHERE] * len(prior),
        out_specs=[
            pl.BlockSpec((1, length, wide), lambda p: (row, 0, 0)),
            pl.BlockSpec((1, 1, wide), lambda p: (row, 0, 0)),
        ],
        out_shape=[shape(packed.shape), shape((rows, 1, wide), F32)],
        scratch_shapes=[
            pltpu.VMEM((2, length, length), F32),
            pltpu.VMEM((2, length, length), BF16),
        ],
        input_output_aliases={5 + index: index for index in range(len(prior))},
    )(packed, packed, packed, upstream, probs, *prior)


def normed_of(summed):
    centred = summed - jnp.mean(summed, axis=-1, keepdims=True)
    variance = jnp.mean(centred * centred, axis=-1, keepdims=True)
    inverse = lax.rsqrt(variance + EPSILON)
    return centred * inverse, inverse


def norm_back(upstream, normed, inverse, gain):
    scaled = upstream * gain
    first_mean = jnp.mean(scaled, axis=-1, keepdims=True)
    second_mean = jnp.mean(scaled * normed, axis=-1, keepdims=True)
    return inverse * (scaled - first_mean - normed * second_mean)


def settle_body(context, tokens, rows, weight, normed, inverse, low):
    summed = widen(tokens[...]) + dot(context[...], weight[...]) + rows[2:3]
    normed[...], inverse[...] = normed_of(summed)
    low[...] = narrow(normed[...] * rows[3:4] + rows[4:5])


def settle(context, tokens, rows, weight):
    count, width = context.shape
    block = count // 2
    tall = pl.BlockSpec((block, width), lambda i: (i, 0))
    return kernel(
        settle_body,
        "settle",
        2 * count * width * width,
        10 * count * width,
        grid=(2,),
        in_specs=[tall, tall, fixed(rows.shape), fixed(weight.shape)],
        out_specs=[tall, pl.BlockSpec((block, 1), lambda i: (i, 0)), tall],
        out_shape=[shape((count, width), F32), shape((count, 1), F32), shape((count, width))],
    )(context, tokens, rows, weight)


def spread_mask(rows, per, column):
    down = lax.broadcasted_iota(jnp.int32, (rows, rows * per), 0)
    along = lax.broadcasted_iota(jnp.int32, (rows, rows * per), 1)
    return along == down * per + column


def stack_blocks(part):
    seq, rows, wide = part.shape
    width = wide // PARTS
    blocks = [
        widen(part[place, :, index * width : (index + 1) * width])
        for place in range(seq)
        for index in range(PARTS)
    ]
    return narrow(jnp.concatenate(blocks, axis=0))


def feed_body(spots, low, bias, normed_one, rows, *refs):
    inners, outers = refs[: 2 * PARTS], refs[2 * PARTS : 4 * PARTS]
    (
        active, slope, normed_two, inverse_two, output, inner_weight, outer_weight,
        branch, staged, sems,
    ) = refs[4 * PARTS :]
    step, steps = pl.program_id(0), pl.num_programs(0)
    wide = staged.shape[-1]
    copies = [
        pltpu.make_async_copy(
            outer.at[:, :, pl.ds(wide, wide)], staged.at[index], sems.at[index]
        )
        for index, outer in enumerate(outers)
    ]

    @pl.when(step == 0)
    def _():
        for copy in copies:
            copy.start()

    unite(inner_weight, inners[:PARTS], inners[PARTS:], spots)
    inner = dot(low[...], inner_weight[...]) + bias[...]
    share = 0.5 * (1.0 + lax.erf(inner * math.sqrt(0.5)))
    raised = jnp.exp(-0.5 * inner * inner) * (1.0 / math.sqrt(2.0 * math.pi))
    acted = narrow(inner * share)
    active[...] = acted
    slope[...] = narrow(share + inner * raised)
    for index in range(PARTS):

        @pl.when(step == spots[2] ^ index)
        def _():
            copies[index].wait()
            copies[PARTS + index].wait()
            half = outer_weight.shape[0] // 2
            for side, at in ((spots[1], index), (1 - spots[1], PARTS + index)):
                start = pl.multiple_of(side * half, half)
                outer_weight[pl.ds(start, half), :] = stack_blocks(staged.at[at])

    part = dot(acted, outer_weight[...])

    @pl.when(step == 0)
    def _():
        branch[...] = part

    @pl.when(step > 0)
    def _():
        branch[...] += part

    height = normed_one.shape[0]
    at = pl.ds(pl.multiple_of(step * height, height), height)
    branch[at, :] += normed_one[...] * rows[3:4] + (rows[4:5] + rows[5:6])

    @pl.when(step == steps - 1)
    def _():
        normed_two[...], inverse_two[...] = normed_of(branch[...])
        result = narrow(normed_two[...] * rows[6:7] + rows[7:8])
        seq, count, places, width = output.shape
        result = result.reshape(count, seq, places, width)
        for row in range(count):
            output[:, row] = result[row]


def feed(spots, low, bias, normed_one, rows, gathered, dims):
    count, width = low.shape
    wide = gathered[0].shape[1] // 2
    block = wide // PARTS
    deep = [part.reshape(dims[0], -1, 2 * wide) for part in gathered]
    all_of = fixed((count, width))
    across = pl.BlockSpec((count, block), lambda f: (0, f))
    return kernel(
        feed_body,
        "feed",
        4 * count * width * wide,
        12 * count * wide,
        grid=(PARTS,),
        in_specs=[
            SCALARS,
            all_of,
            pl.BlockSpec((1, block), lambda f: (0, f)),
            pl.BlockSpec((count // PARTS, width), lambda f: (f, 0)),
            fixed(rows.shape),
        ]
        + gathered_specs(gathered, block, lambda f: f)
        + [ANYWHERE] * len(deep),
        out_specs=[
            across,
            across,
            all_of,
            fixed((count, 1)),
            fixed(dims),
            pl.BlockSpec((width, block), lambda f: (0, f)),
            pl.BlockSpec((block, width), lambda f: (f, 0)),
        ],
        out_shape=[
            shape((count, wide)),
            shape((count, wide)),
            shape((count, width), F32),
            shape((count, 1), F32),
            shape(dims),
            shape((width, wide)),
            shape((wide, width)),
        ],
        scratch_shapes=[
            pltpu.VMEM((count, width), F32),
            pltpu.VMEM((len(deep),) + deep[0].shape[:2] + (wide,), BF16),
            pltpu.SemaphoreType.DMA((len(deep),)),
        ],
    )(spots, low, bias, normed_one, rows, *gathered, *deep)


def feed_back_body(
    spots, cotangent, normed_two, inverse_two, rows_one, low, inner_weight, outer_weight, active, slope,
    keep_inner, send_inner, keep_outer, send_outer, keep_vectors, send_vectors, hidden_grad,
    up, made, columns, pre, grads,
):
    step, steps, side = pl.program_id(0), pl.num_programs(0), spots[1]
    block = inner_weight.shape[-1]

    @pl.when(step == 0)
    def _():
        rows, width = cotangent.shape[1], cotangent.shape[-1]
        upstream = jnp.concatenate(
            [widen(cotangent[:, row]).reshape(-1, width) for row in range(rows)], axis=0
        )
        normed = normed_two[...]
        hidden_grad[...] = norm_back(upstream, normed, inverse_two[...], rows_one[6:7])
        up[...] = narrow(hidden_grad[...])
        columns[...] = as_columns(
            (row_sum(widen(up[...])), row_sum(upstream * normed), row_sum(upstream))
        )

    pre[...] = dot(up[...], outer_weight[...], NT)
    for start in range(0, pre.shape[0], 4 * CHUNK):
        down = slice(start, start + 4 * CHUNK)
        grads[down] = narrow(pre[down] * widen(slope[down]))
    inner_grad = grads[...]
    made[...] = narrow(dot(low[...], inner_grad, TN))
    divide(made, keep_inner, send_inner, side, slice(None))
    hidden_grad[...] += dot(inner_grad, inner_weight[...], NT)
    made[...] = narrow(dot(active[...], up[...], TN))
    divide(made, keep_outer, send_outer, side, slice(None))

    bias = row_sum(widen(inner_grad))
    share_rows = columns.shape[0] // PARTS
    per = block // share_rows
    lane = lax.broadcasted_iota(jnp.int32, (1, LANES), 1)
    total = 0.0
    for column in range(per):
        value = jnp.sum(
            jnp.where(spread_mask(share_rows, per, column), bias, 0.0), axis=1, keepdims=True
        )
        total = total + jnp.where(lane == 3 + column, value, 0.0)
    columns[pl.ds(pl.multiple_of(step * share_rows, share_rows), share_rows), :] += total

    @pl.when(step == steps - 1)
    def _():
        made[:, :LANES] = narrow(columns[...])
        divide(made.at[:, :LANES], keep_vectors, send_vectors, side, slice(None))


def feed_back(spots, cotangent, normed_two, inverse_two, rows, low, inner, outer, active, slope):
    count, width = low.shape
    wide = inner.shape[1]
    block = wide // PARTS
    all_of = fixed((count, width))
    across = pl.BlockSpec((count, block), lambda f: (0, f))
    first, second = (PARTS, width // PARTS // 2, wide), (PARTS, block // 2, width)
    third = first[:2] + (LANES,)
    right = pl.BlockSpec(first[:2] + (block,), lambda f: (0, 0, f))
    down = pl.BlockSpec((1,) + second[1:], lambda f: (f, 0, 0))
    return kernel(
        feed_back_body,
        "feed_back",
        8 * count * width * wide,
        12 * count * wide,
        grid=(PARTS,),
        in_specs=[SCALARS, fixed(cotangent.shape), all_of, fixed((count, 1)), fixed(rows.shape), all_of]
        + [
            pl.BlockSpec((width, block), lambda f: (0, f)),
            pl.BlockSpec((block, width), lambda f: (f, 0)),
            across,
            across,
        ],
        out_specs=[right, right, down, down, fixed(third), fixed(third), all_of],
        out_shape=[shape(dims) for dims in (first, first, second, second, third, third)]
        + [shape((count, width), F32)],
        scratch_shapes=[
            pltpu.VMEM((count, width), BF16),
            pltpu.VMEM((width, block), BF16),
            pltpu.VMEM((width, LANES), F32),
            pltpu.VMEM((count, block), F32),
            pltpu.VMEM((count, block), BF16),
        ],
    )(spots, cotangent, normed_two, inverse_two, rows, low, inner, outer, active, slope)


def settle_back_body(
    spots, hidden_grad, normed, inverse, rows, context, weight,
    first_up, context_grad, keep, send, sums, total, made,
):
    step, steps = pl.program_id(0), pl.num_programs(0)

    @pl.when(step == 0)
    def _():
        sums[...] = jnp.zeros_like(sums)
        total[...] = jnp.zeros_like(total)

    upstream = hidden_grad[...]
    up = norm_back(upstream, normed[...], inverse[...], rows[3:4])
    first_up[...] = up
    low = narrow(up)
    context_grad[...] = narrow(dot(low, weight[...], NT))
    total[...] += dot(context[...], low, TN)
    sums[0:1] += row_sum(widen(low))
    sums[1:2] += row_sum(upstream * normed[...])
    sums[2:3] += row_sum(upstream)

    @pl.when(step == steps - 1)
    def _():
        made[...] = narrow(total[...])
        divide(made, keep, send, spots[1], slice(None))


def settle_back(spots, hidden_grad, normed, inverse, rows, context, weight):
    count, width = context.shape
    block = count // 2
    tall = pl.BlockSpec((block, width), lambda i: (i, 0))
    dims = (PARTS, width // PARTS // 2, width)
    return kernel(
        settle_back_body,
        "settle_back",
        10**12,
        16 * count * width,
        grid=(2,),
        in_specs=[SCALARS, tall, tall, pl.BlockSpec((block, 1), lambda i: (i, 0))]
        + [fixed(rows.shape), tall, fixed((width, width))],
        out_specs=[tall, tall, fixed(dims), fixed(dims), fixed((8, width))],
        out_shape=[
            shape((count, width), F32),
            shape((count, width)),
            shape(dims),
            shape(dims),
            shape((8, width), F32),
        ],
        scratch_shapes=[pltpu.VMEM((width, width), F32), pltpu.VMEM((width, width), BF16)],
    )(spots, hidden_grad, normed, inverse, rows, context, weight)


def tokens_back_body(packed_grad, weight, first_up, grad):
    grad[...] = narrow(first_up[...] + dot(packed_grad[0], weight[...], NT))


def tokens_back(packed_grad, weight, first_up, row):
    _, length, wide = packed_grad.shape
    width = wide // 3
    half = length // 2
    return kernel(
        tokens_back_body,
        "tokens_back",
        2 * length * width * wide,
        8 * length * width,
        grid=(2,),
        in_specs=[
            pl.BlockSpec((1, half, wide), lambda i: (row, i, 0)),
            fixed((width, wide)),
            pl.BlockSpec((half, width), lambda i: (2 * row + i, 0)),
        ],
        out_specs=pl.BlockSpec((half, width), lambda i: (i, 0)),
        out_shape=shape((length, width)),
    )(packed_grad, weight, first_up)


def weights_back_body(spots, packed_grad, tokens, packed_sums, sums, keep, send, made):
    part, side = pl.program_id(0), spots[1]
    width = tokens.shape[1]
    made[...] = narrow(dot(tokens[...], packed_grad[...], TN))
    divide(made, keep, send, side, pl.ds(pl.multiple_of(part * width, width), width))

    @pl.when(part == 2)
    def _():
        packed = jnp.sum(packed_sums[...], axis=0)
        made[:, :LANES] = narrow(
            as_columns(
                (packed[:, :width], packed[:, 2 * width :], sums[0:1], sums[1:2], sums[2:3])
            )
        )
        divide(made.at[:, :LANES], keep, send, side, slice(3 * width, 3 * width + LANES))


def weights_back(spots, packed_grad, tokens, packed_sums, sums):
    count, width = tokens.shape
    dims = (PARTS, width // PARTS // 2, 3 * width + LANES)
    return kernel(
        weights_back_body,
        "weights_back",
        6 * count * width * width,
        8 * count * width,
        grid=(3,),
        in_specs=[SCALARS, pl.BlockSpec((count, width), lambda i: (0, i)), fixed(tokens.shape)]
        + [fixed(packed_sums.shape), fixed(sums.shape)],
        out_specs=[fixed(dims), fixed(dims)],
        out_shape=[shape(dims), shape(dims)],
        scratch_shapes=[pltpu.VMEM((width, width), BF16)],
    )(spots, packed_grad, tokens, packed_sums, sums)


def side_by_side(out, start, total):
    small, width = out.shape[0], total.shape[1]
    for height in range(0, total.shape[0], small):
        out[:, start : start + width] = narrow(total[height : height + small])
        start += width
    return start


def chip_sums(name, spots, pairs, seq, small):
    operands, in_specs = [], []
    wide = sum(kept.shape[1] // (seq * small) * kept.shape[2] for kept, _ in pairs)
    for kept, came in pairs:
        height = kept.shape[1] // seq
        for value in (kept, came):
            operands.append(value.reshape(PARTS, seq, height, value.shape[2]))
            in_specs.append(
                pl.BlockSpec(
                    (PARTS, None, height, value.shape[2]), lambda i, spots: (0, i, 0, 0)
                )
            )

    def body(spots, *refs):
        ins, outs = refs[: len(operands)], refs[len(operands) :]
        for part, out in enumerate(outs):
            start = 0
            chip = spots[2] ^ part
            for kept, came in zip(ins[::2], ins[1::2]):
                start = side_by_side(out, start, widen(kept[chip]) + widen(came[chip]))

    return kernel(
        body,
        name,
        0,
        6 * PARTS * seq * small * wide,
        grid_spec=pltpu.PrefetchScalarGridSpec(
            num_scalar_prefetch=1,
            grid=(seq,),
            in_specs=in_specs,
            out_specs=[pl.BlockSpec((None, small, wide), lambda i, spots: (i, 0, 0))] * PARTS,
        ),
        out_shape=[shape((seq, small, wide))] * PARTS,
    )(spots, *operands)


def total_body(*refs):
    total = widen(refs[0][...])
    for ref in refs[1:-1]:
        total = total + widen(ref[...])
    refs[-1][...] = narrow(total)


def total_of(name, values, flops=0):
    seq, small, wide = values[0].shape
    block = pl.BlockSpec((None, small, wide), lambda i: (i, 0, 0))
    return kernel(
        total_body,
        name,
        flops,
        2 * (len(values) + 1) * seq * small * wide,
        grid=(seq,),
        in_specs=[block] * len(values),
        out_specs=block,
        out_shape=shape(values[0].shape),
    )(*values)


def total_pieces(name, spots, values):
    seq, small, wide = values[0].shape

    def body(spots, *refs):
        for step in range(seq):
            at = lax.rem(spots[0] + step, seq)
            total_body(*[ref.at[at] for ref in refs[: len(values)]], refs[len(values) + step])

    return kernel(
        body,
        name,
        0,
        2 * (len(values) + 1) * seq * small * wide,
        in_specs=[SCALARS] + [pl.BlockSpec(memory_space=pltpu.VMEM)] * len(values),
        out_specs=[pl.BlockSpec(memory_space=pltpu.VMEM)] * seq,
        out_shape=[shape((small, wide))] * seq,
    )(spots, *values)


def copied(value, *others):
    def body(source, target):
        target[...] = source[...]

    block = pl.BlockSpec((1,) + value.shape[1:], lambda i: (i,) + (0,) * (value.ndim - 1))
    return kernel(
        body,
        "copied",
        0,
        4 * math.prod(value.shape),
        grid=value.shape[:1],
        in_specs=[block],
        out_specs=block,
        out_shape=like(value),
    )(after(value, *others))


def finish_body(count, vectors, blocks, *refs):
    pieces, outs = refs[:count], refs[count:]
    if count == 1:
        pieces = [pieces[0].at[index] for index in range(pieces[0].shape[0])]
    total = widen(pieces[0][...])
    for piece in pieces[1:]:
        total = total + widen(piece[...])
    small, wide = total.shape
    start = 0
    for out, (count, width) in zip(outs, blocks):
        for index in range(count):
            out[index * small : (index + 1) * small] = total[:, start : start + width]
            start += width
    at = wide - LANES
    for out, (column, per) in zip(outs[len(blocks) :], vectors):
        line = 0.0
        for part in range(per):
            value = total[:, at + column + part : at + column + part + 1]
            line = line + jnp.where(spread_mask(small, per, part), value, 0.0)
        out[...] = row_sum(line)


def finish(name, pieces, blocks, vectors):
    small, wide = pieces[0].shape[-2:]
    return kernel(
        partial(finish_body, len(pieces), vectors, blocks),
        name,
        0,
        8 * small * wide,
        out_shape=[shape((count * small, width), F32) for count, width in blocks]
        + [shape((1, small * per), F32) for _, per in vectors],
    )(*pieces)


def block_at(blocks, index, axis=0):
    return lax.dynamic_index_in_dim(blocks, index, axis, keepdims=False)


class Links:
    def __init__(self, mesh):
        self.dp, self.seq = mesh.shape["dp"], mesh.shape["seq"]
        self.bits = self.dp.bit_length() - 1
        assert self.dp == 1 << self.bits
        self.direct = self.dp == 2 * PARTS

    def across(self, value, flip):
        pairs = [
            (d * self.seq + s, (d ^ flip) * self.seq + s)
            for d in range(self.dp)
            for s in range(self.seq)
        ]
        return lax.ppermute(value, AXES, pairs)

    def along(self, value, step):
        pairs = [
            (d * self.seq + s, d * self.seq + (s + step) % self.seq)
            for d in range(self.dp)
            for s in range(self.seq)
        ]
        return lax.ppermute(value, AXES, pairs)

    def digit(self, bit):
        return (lax.axis_index("dp") >> bit) & 1

    def spots(self):
        place, dp = lax.axis_index("seq"), lax.axis_index("dp")
        side, chip = (dp & 1, dp >> 1) if self.direct else (0 * dp, 0 * dp)
        return jnp.stack([place, side, chip]).astype(jnp.int32)

    def turn(self, blocks):
        return lax.all_to_all(blocks, "seq", split_axis=0, concat_axis=0, tiled=True)

    def spread(self, held):
        return [held] + [self.across(held, 2 * part) for part in range(1, PARTS)]

    def swap(self, parts):
        parts = [part.reshape(-1, part.shape[-1]) for part in parts]
        return parts + [self.across(part, 1) for part in parts]

    def gather_whole(self, held):
        done = []
        for bit in range(self.bits):
            other, mine = self.across(held, 1 << bit), self.digit(bit)
            held = jnp.where(mine == 0, jnp.stack([held, other]), jnp.stack([other, held]))
        return held.reshape(self.dp * self.seq, *held.shape[self.bits + 1 :])

    def cut(self, whole):
        whole = whole.reshape(PARTS, 2, -1, whole.shape[-1])
        return [whole[part, side] for side in range(2) for part in range(PARTS)]

    def reduce_whole(self, keep, send):
        rows = keep.shape[0] * keep.shape[1] * 2 // (self.dp * self.seq)
        whole = jnp.stack([keep, send], axis=1)
        held = whole.reshape((2,) * self.bits + (self.seq, rows, keep.shape[-1]))
        for bit in reversed(range(self.bits)):
            mine = self.digit(bit)
            other = self.across(block_at(held, 1 - mine), 1 << bit)
            held = narrow(widen(block_at(held, mine)) + widen(other))
        return held


def shards(
    links,
    tokens,
    cotangent,
    lengths,
    packed_weight,
    query_bias,
    value_bias,
    output_weight,
    output_bias,
    first_gain,
    first_shift,
    inner_weight,
    inner_bias,
    outer_weight,
    outer_bias,
    second_gain,
    second_shift,
):
    row_count, places, width = tokens.shape
    seq, direct = links.seq, links.direct
    rows = row_count // seq
    dims = (seq, rows, places, width)
    small, tall = packed_weight.shape[0], outer_weight.shape[0]
    wide = inner_weight.shape[1]
    per = wide // width
    spots = links.spots()

    vectors = (
        query_bias, value_bias, output_bias, first_gain, first_shift,
        outer_bias, second_gain, second_shift, inner_bias,
    )
    held = links.turn(prepare_attention(seq, packed_weight, output_weight, vectors))
    feed_held = links.turn(after(prepare_feed(seq, inner_weight, outer_weight), held))
    if direct:
        held = links.spread(held)
        came = links.turn(after(tokens.reshape(dims), feed_held, *held))
        gathered = links.swap(held)
        feed_held = links.spread(feed_held)
    else:
        came = links.turn(after(tokens.reshape(dims), feed_held))
        gathered = links.cut(links.gather_whole(held))
        whole = links.gather_whole(feed_held)
        inner, outer = whole[..., :wide], whole[..., wide:]
        outer = outer.reshape(-1, small, per, width).swapaxes(1, 2)
        outer = outer.reshape(2 * PARTS * seq, per, -1, width).swapaxes(1, 2)
        inner, outer = inner.reshape(width, wide), outer.reshape(width, wide)
        feed_gathered = links.cut(jnp.concatenate([inner, outer], axis=1))
    cotangent_mine = links.turn(after(cotangent.reshape(dims), came))
    packed_whole, output_whole, rows_one, inner_bias_row = unite_attention(spots, gathered, wide)
    packed, flat = project(came, packed_whole, rows_one)
    context, probs = attend(spots, lengths, packed)
    context = context.reshape(-1, width)
    if direct:
        feed_held = [feed_held[0]] + [after(value, context) for value in feed_held[1:]]
        context = after(context, *feed_held)
        feed_gathered = links.swap(feed_held)
    normed_one, inverse_one, low = settle(context, flat, rows_one, output_whole)
    active, slope, normed_two, inverse_two, output, inner_whole, outer_whole = feed(
        spots, low, inner_bias_row, normed_one, rows_one, feed_gathered, dims
    )
    cotangent_mine = after(cotangent_mine, slope)
    output = after(output, cotangent_mine)
    cotangent_mine = after(cotangent_mine, output)
    (
        keep_inner, send_inner, keep_outer, send_outer, keep_vectors, send_vectors, hidden_grad,
    ) = feed_back(
        spots,
        cotangent_mine,
        normed_two,
        inverse_two,
        rows_one,
        low,
        inner_whole,
        outer_whole,
        active,
        slope,
    )
    hidden_grad = after(hidden_grad, send_inner, send_outer, send_vectors)
    first_up, context_grad, keep_output, send_output, sums = settle_back(
        spots, hidden_grad, normed_one, inverse_one, rows_one, context, output_whole
    )
    output = after(links.turn(output), sums)
    context_grad = after(context_grad, output)
    if direct:
        inner_came = after(links.across(send_inner, 1), sums)
        outer_came = after(links.across(send_outer, 1), sums)
        output_came = links.across(send_output, 1)
        vectors_came = after(links.across(send_vectors, 1), sums)
        pairs = [
            (keep_outer, outer_came),
            (keep_output, output_came),
            (keep_inner, inner_came),
            (keep_vectors, vectors_came),
        ]
        feed_sums = list(chip_sums("feed_chip_sums", spots, pairs, seq, small))
        context_grad = after(context_grad, *feed_sums[1:])
        feed_sums[1:] = [links.across(feed_sums[part], 2 * part) for part in range(1, PARTS)]
    context_grad = context_grad.reshape(rows, seq * places, width)
    prior, tokens_grad = (), []
    for row in range(rows):
        prior = attend_back(packed, probs, context_grad, row, prior)
        grad = tokens_back(prior[0], packed_whole, first_up, row)
        context_grad = after(context_grad, grad)
        sent = after(grad, tokens_grad[-1]) if row else grad
        tokens_grad.append(links.turn(sent.reshape(seq, places, width)))
    packed_grad, packed_sums = prior
    packed_grad = after(packed_grad, grad).reshape(-1, 3 * width)
    keep, send = weights_back(spots, packed_grad, flat, packed_sums, sums)
    output = copied(output, keep)
    if direct:
        feed_sums[1:] = [after(value, keep, output) for value in feed_sums[1:]]
        feed_total = total_of("feed_total", feed_sums, 10**10)
        came = after(links.across(send, 1), feed_total)
        attention_sums = list(
            chip_sums("attention_chip_sums", spots, [(keep, came)], seq, small)
        )
        feed_total = after(feed_total, *tokens_grad)
        attention_sums[1:] = [
            links.across(attention_sums[part], 2 * part) for part in range(1, PARTS)
        ]
        attention_total = total_pieces("attention_total", spots, attention_sums)
    else:
        reduced = [
            links.reduce_whole(*pair)
            for pair in (
                (keep_outer, send_outer),
                (keep_output, send_output),
                (keep_inner, send_inner),
                (keep_vectors, send_vectors),
            )
        ]
        reduced[0] = reduced[0].reshape(seq, per, small, width).swapaxes(1, 2)
        reduced[0] = reduced[0].reshape(seq, small, per * width)
        feed_total = jnp.concatenate(reduced, axis=2)
        attention_total = links.reduce_whole(keep, send)
        attention_total = [block_at(attention_total, (spots[0] + i) % seq) for i in range(seq)]
    feed_total = links.turn(feed_total)
    attention_total = [
        links.along(piece, step) if step else piece for step, piece in enumerate(attention_total)
    ]
    (
        outer_grad, output_grad, inner_grad,
        outer_bias_grad, second_gain_grad, second_shift_grad, inner_bias_grad,
    ) = finish(
        "finish_feed",
        [feed_total],
        [(per, width), (1, width), (1, wide)],
        [(0, 1), (1, 1), (2, 1), (3, per)],
    )
    tokens_grad = widen(jnp.stack(tokens_grad, axis=1))
    attention_total[1:] = [after(piece, inner_grad, tokens_grad) for piece in attention_total[1:]]
    (
        packed_weight_grad,
        query_bias_grad, value_bias_grad, output_bias_grad, first_gain_grad, first_shift_grad,
    ) = finish(
        "finish_attention", attention_total, [(1, 3 * width)], [(i, 1) for i in range(5)]
    )
    return (
        output.reshape(tokens.shape),
        tokens_grad.reshape(tokens.shape),
        packed_weight_grad,
        query_bias_grad.reshape(-1),
        value_bias_grad.reshape(-1),
        output_grad,
        output_bias_grad.reshape(-1),
        first_gain_grad.reshape(-1),
        first_shift_grad.reshape(-1),
        inner_grad,
        inner_bias_grad.reshape(-1),
        outer_grad,
        outer_bias_grad.reshape(-1),
        second_gain_grad.reshape(-1),
        second_shift_grad.reshape(-1),
    )


def solution(mesh):
    split = P(AXES)
    split_rows = P(AXES, None)
    packed_rows = P("dp", "seq", None)
    return jax.shard_map(
        partial(shards, Links(mesh)),
        mesh=mesh,
        in_specs=(
            packed_rows,
            packed_rows,
            P("dp", None),
            split_rows,
            split,
            split,
            split_rows,
            split,
            split,
            split,
            split_rows,
            split,
            split_rows,
            split,
            split,
            split,
        ),
        out_specs=(
            packed_rows,
            packed_rows,
            split_rows,
            split,
            split,
            split_rows,
            split,
            split,
            split,
            split_rows,
            split,
            split_rows,
            split,
            split,
            split,
        ),
        check_vma=False,
    )
```

```python
from functools import partial
import math

import jax
import jax.numpy as jnp
from jax import lax
from jax.experimental import pallas as pl
from jax.experimental.pallas import tpu as pltpu
from jax.sharding import PartitionSpec as P

HEAD_DIM = 64
LANES = 128
CHUNK = 64
PARTS = 4
EPSILON = 1e-06
AXES = ("dp", "seq")
BF16, F32 = jnp.bfloat16, jnp.float32

NN = (((1,), (0,)), ((), ()))
NT = (((1,), (1,)), ((), ()))
TN = (((0,), (0,)), ((), ()))


def narrow(value):
    return value.astype(BF16)


def widen(value):
    return value.astype(F32)


def after(value, *others):
    return lax.optimization_barrier((value,) + others)[0]


def dot(left, right, dims=NN):
    return lax.dot_general(left, right, dims, preferred_element_type=F32)


def shape(dims, dtype=BF16):
    return jax.ShapeDtypeStruct(dims, dtype)


def like(value):
    return jax.ShapeDtypeStruct(value.shape, value.dtype)


def fixed(dims, *index):
    at = tuple(index) or (0,) * len(dims)
    return pl.BlockSpec(dims, lambda *_: at)


SCALARS = pl.BlockSpec(memory_space=pltpu.SMEM)
ANYWHERE = pl.BlockSpec(memory_space=pl.ANY)


def row_sum(value):
    return jnp.sum(value, axis=0, keepdims=True)


def kernel(body, name, flops, touched, **options):
    return pl.pallas_call(
        body,
        name=name,
        compiler_params=pltpu.CompilerParams(vmem_limit_bytes=60 << 20),
        cost_estimate=pl.CostEstimate(flops=flops, bytes_accessed=touched, transcendentals=0),
        **options,
    )


def unite(target, own, other, spots):
    side, chip = spots[1], spots[2]
    rows = own[0].shape[0]
    for index in range(PARTS):
        for half, value in ((side, own[index]), (1 - side, other[index])):
            start = pl.multiple_of((2 * (chip ^ index) + half) * rows, rows)
            target[pl.ds(start, rows), :] = value[...]


def divide(source, keep, send, side, columns):
    count, rows = keep.shape[:2]
    for index in range(count):
        for half, target in ((side, keep), (1 - side, send)):
            start = pl.multiple_of((2 * index + half) * rows, rows)
            target[index, :, columns] = source[pl.ds(start, rows), :]


def gathered_specs(gathered, columns, index):
    block = (gathered[0].shape[0], columns)
    return [pl.BlockSpec(block, lambda *at: (0, index(*at)))] * len(gathered)


def as_columns(rows):
    width = rows[0].shape[1]
    padding = jnp.zeros((LANES - len(rows), width), F32)
    return jnp.concatenate(list(rows) + [padding], axis=0).T


def prepare_attention_body(packed_weight, output_weight, *rest):
    *vectors, out = rest
    seq, small, _ = out.shape
    lane = lax.broadcasted_iota(jnp.int32, (1, LANES), 1)
    block, column = 0.0, 0
    for vector in vectors:
        per = vector.shape[1] // small
        for part in range(per):
            value = jnp.where(spread_mask(small, per, part), vector[...], 0.0)
            value = jnp.sum(value, axis=1, keepdims=True)
            block = block + jnp.where(lane == column, value, 0.0)
            column += 1
    shard = jnp.concatenate(
        [narrow(packed_weight[...]), narrow(output_weight[...]), narrow(block)], axis=1
    )
    for index in range(seq):
        out[index] = shard


def prepare_attention(seq, packed_weight, output_weight, vectors):
    small, wide = packed_weight.shape
    vectors = [vector.reshape(1, -1) for vector in vectors]
    return kernel(
        prepare_attention_body,
        "prepare_attention",
        0,
        16 * small * wide,
        out_shape=shape((seq, small, wide + LANES + output_weight.shape[1])),
    )(packed_weight, output_weight, *vectors)


def prepare_feed_body(inner_weight, outer_weight, out):
    seq, small, _ = out.shape
    wide, width = inner_weight.shape[1], outer_weight.shape[1]
    out[0, :, :wide] = narrow(inner_weight[...])
    for index in range(outer_weight.shape[0] // small):
        start = wide + index * width
        block = outer_weight[index * small : (index + 1) * small]
        out[0, :, start : start + width] = narrow(block)
    for index in range(1, seq):
        out[index] = out[0]


def prepare_feed(seq, inner_weight, outer_weight):
    small, wide = inner_weight.shape
    return kernel(
        prepare_feed_body,
        "prepare_feed",
        0,
        16 * small * wide,
        out_shape=shape((seq, small, 2 * wide)),
    )(inner_weight, outer_weight)


def unite_attention_body(spots, *refs):
    parts, (packed, output, rows, bias, vectors) = refs[: 2 * PARTS], refs[2 * PARTS :]
    width, wide = packed.shape
    for target, start in ((packed, 0), (output, wide), (vectors, wide + width)):
        views = [part.at[:, start : start + target.shape[1]] for part in parts]
        unite(target, views[:PARTS], views[PARTS:], spots)
    rows[...] = widen(vectors[...]).T[:8]
    share, block = width // PARTS, bias.shape[1] // PARTS
    per = block // share
    for index in range(PARTS):
        line = 0.0
        for column in range(per):
            value = widen(vectors[index * share : (index + 1) * share, 8 + column : 9 + column])
            line = line + jnp.where(spread_mask(share, per, column), value, 0.0)
        bias[:, index * block : (index + 1) * block] = row_sum(line)


def unite_attention(spots, gathered, wide):
    rows, columns = gathered[0].shape
    width = 2 * PARTS * rows
    whole = pl.BlockSpec(memory_space=pltpu.VMEM)
    return kernel(
        unite_attention_body,
        "unite_attention",
        0,
        4 * width * columns,
        in_specs=[SCALARS] + [whole] * len(gathered),
        out_specs=[whole] * 4,
        out_shape=[
            shape((width, 3 * width)),
            shape((width, width)),
            shape((8, width), F32),
            shape((1, wide), F32),
        ],
        scratch_shapes=[pltpu.VMEM((width, LANES), BF16)],
    )(spots, *gathered)


def project_body(tokens, weight, rows, packed, flat):
    part = pl.program_id(0)
    seq, count, places, width = tokens.shape
    length = seq * places

    @pl.when(part == 0)
    def _():
        for row in range(count):
            flat[row * length : (row + 1) * length] = tokens[:, row].reshape(length, width)

    query, value = rows[0:1], rows[1:2]
    bias = jnp.where(part == 0, query, jnp.where(part == 2, value, jnp.zeros_like(query)))
    result = narrow(dot(flat[...], weight[...]) + bias)
    packed[...] = result.reshape(packed.shape)


def project(tokens, weight, rows):
    seq, count, places, width = tokens.shape
    length = seq * places
    return kernel(
        project_body,
        "project",
        6 * count * length * width * width,
        8 * count * length * width,
        grid=(3,),
        in_specs=[
            fixed(tokens.shape),
            pl.BlockSpec((width, width), lambda i: (0, i)),
            fixed(rows.shape),
        ],
        out_specs=[
            pl.BlockSpec((count, length, width), lambda i: (0, 0, i)),
            fixed((count * length, width)),
        ],
        out_shape=[shape((count, length, 3 * width)), shape((count * length, width))],
    )(tokens, weight, rows)


def pair_labels(places, lengths, row):
    label, bound = jnp.zeros_like(places), 0
    for pair in range(lengths.shape[1] - 1):
        bound = bound + lengths[row, pair]
        label = label + (places >= bound).astype(jnp.int32)
    return label


def attend_body(spots, lengths, query, key, value, context, probs, bias, scores):
    length = bias.shape[0]

    @pl.when(pl.program_id(1) == 0)
    def _():
        at = spots[0] * pl.num_programs(0) + pl.program_id(0)
        down = pair_labels(lax.broadcasted_iota(jnp.int32, (length, 1), 0), lengths, at)
        along = pair_labels(lax.broadcasted_iota(jnp.int32, (1, length), 1), lengths, at)
        bias[...] = jnp.where(down == along, 0.0, -1e30)

    lane = lax.broadcasted_iota(jnp.int32, (1, LANES), 1)
    values = value[0]
    queries = query[0] * BF16(HEAD_DIM**-0.5)
    for head in range(2):
        mine = (lane >= HEAD_DIM) == bool(head)
        scores[head] = dot(jnp.where(mine, queries, BF16(0)), key[0], NT)
    parts = []
    for head in range(2):
        for start in range(0, length, CHUNK):
            rows = slice(start, start + CHUNK)
            masked = scores[head, rows] + bias[rows]
            raised = jnp.exp(masked - jnp.max(masked, axis=-1, keepdims=True))
            total = jnp.sum(raised, axis=-1, keepdims=True)
            probs[0, head, rows] = narrow(raised * (1.0 / total))
        parts.append(dot(probs[0, head], values))
    context[0] = narrow(jnp.where(lane < HEAD_DIM, parts[0], parts[1]))


def head_pair(length, offset):
    return pl.BlockSpec((1, length, LANES), lambda r, p: (r, 0, offset + p))


def attend(spots, lengths, packed):
    rows, length, wide = packed.shape
    pairs = wide // 3 // LANES
    return kernel(
        attend_body,
        "attend",
        rows * pairs * 16 * length * length * LANES,
        rows * pairs * 8 * length * length,
        grid=(rows, pairs),
        in_specs=[SCALARS, SCALARS] + [head_pair(length, part * pairs) for part in range(3)],
        out_specs=[
            head_pair(length, 0),
            pl.BlockSpec((1, 2, length, length), lambda r, p: (r, p, 0, 0)),
        ],
        out_shape=[shape((rows, length, wide // 3)), shape((rows, 2 * pairs, length, length))],
        scratch_shapes=[pltpu.VMEM((length, length), F32), pltpu.VMEM((2, length, length), F32)],
    )(spots, lengths, packed, packed, packed)


def attend_back_body(query, key, value, upstream, probs, *rest):
    grads, sums, prob_grad, score_grad = rest[-4:]
    pair, pairs = pl.program_id(0), pl.num_programs(0)
    lane = lax.broadcasted_iota(jnp.int32, (1, LANES), 1)
    scale = BF16(HEAD_DIM**-0.5)
    queries, keys, values, up = query[0] * scale, key[0], value[0], upstream[0]
    scaled_keys = keys * scale
    length = keys.shape[0]
    query_parts, key_grad, value_grad = [], 0.0, 0.0
    mine = [(lane >= HEAD_DIM) == bool(head) for head in range(2)]
    ups = [jnp.where(lanes, up, BF16(0)) for lanes in mine]
    for head in range(2):
        prob_grad[head] = dot(ups[head], values, NT)
    for head in range(2):
        for start in range(0, length, CHUNK):
            rows = slice(start, start + CHUNK)
            softmaxed = widen(probs[0, head, rows])
            product = softmaxed * prob_grad[head, rows]
            weighted = jnp.sum(product, axis=-1, keepdims=True)
            score_grad[head, rows] = narrow(product - softmaxed * weighted)
    for head in range(2):
        queries_mine = jnp.where(mine[head], queries, BF16(0))
        query_parts.append(dot(score_grad[head], scaled_keys))
        key_grad = key_grad + dot(queries_mine, score_grad[head], TN)
        value_grad = value_grad + dot(ups[head], probs[0, head], TN)
    query_grad = jnp.where(lane < HEAD_DIM, query_parts[0], query_parts[1])
    for part, grad in enumerate((query_grad, key_grad.T, value_grad.T)):
        at = pl.ds(pl.multiple_of((part * pairs + pair) * LANES, LANES), LANES)
        rounded = narrow(grad)
        grads[0, :, at] = rounded
        sums[0, :, at] = row_sum(widen(rounded))


def attend_back(packed, probs, upstream, row, prior=()):
    rows, length, wide = packed.shape
    pairs = wide // 3 // LANES

    def columns(offset):
        return pl.BlockSpec((1, length, LANES), lambda p: (row, 0, offset + p))

    return kernel(
        attend_back_body,
        "attend_back",
        10**12 if row else 0,
        pairs * 8 * length * length,
        grid=(pairs,),
        in_specs=[columns(part * pairs) for part in range(3)]
        + [columns(0), pl.BlockSpec((1, 2, length, length), lambda p: (row, p, 0, 0))]
        + [ANYWHERE] * len(prior),
        out_specs=[
            pl.BlockSpec((1, length, wide), lambda p: (row, 0, 0)),
            pl.BlockSpec((1, 1, wide), lambda p: (row, 0, 0)),
        ],
        out_shape=[shape(packed.shape), shape((rows, 1, wide), F32)],
        scratch_shapes=[
            pltpu.VMEM((2, length, length), F32),
            pltpu.VMEM((2, length, length), BF16),
        ],
        input_output_aliases={5 + index: index for index in range(len(prior))},
    )(packed, packed, packed, upstream, probs, *prior)


def normed_of(summed):
    centred = summed - jnp.mean(summed, axis=-1, keepdims=True)
    variance = jnp.mean(centred * centred, axis=-1, keepdims=True)
    inverse = lax.rsqrt(variance + EPSILON)
    return centred * inverse, inverse


def norm_back(upstream, normed, inverse, gain):
    scaled = upstream * gain
    first_mean = jnp.mean(scaled, axis=-1, keepdims=True)
    second_mean = jnp.mean(scaled * normed, axis=-1, keepdims=True)
    return inverse * (scaled - first_mean - normed * second_mean)


def settle_body(context, tokens, rows, weight, normed, inverse, low):
    summed = widen(tokens[...]) + dot(context[...], weight[...]) + rows[2:3]
    normed[...], inverse[...] = normed_of(summed)
    low[...] = narrow(normed[...] * rows[3:4] + rows[4:5])


def settle(context, tokens, rows, weight):
    count, width = context.shape
    block = count // 2
    tall = pl.BlockSpec((block, width), lambda i: (i, 0))
    return kernel(
        settle_body,
        "settle",
        2 * count * width * width,
        10 * count * width,
        grid=(2,),
        in_specs=[tall, tall, fixed(rows.shape), fixed(weight.shape)],
        out_specs=[tall, pl.BlockSpec((block, 1), lambda i: (i, 0)), tall],
        out_shape=[shape((count, width), F32), shape((count, 1), F32), shape((count, width))],
    )(context, tokens, rows, weight)


def spread_mask(rows, per, column):
    down = lax.broadcasted_iota(jnp.int32, (rows, rows * per), 0)
    along = lax.broadcasted_iota(jnp.int32, (rows, rows * per), 1)
    return along == down * per + column


def stack_blocks(part):
    seq, rows, wide = part.shape
    width = wide // PARTS
    blocks = [
        widen(part[place, :, index * width : (index + 1) * width])
        for place in range(seq)
        for index in range(PARTS)
    ]
    return narrow(jnp.concatenate(blocks, axis=0))


def feed_body(spots, low, bias, normed_one, rows, *refs):
    inners, outers = refs[: 2 * PARTS], refs[2 * PARTS : 4 * PARTS]
    (
        active, slope, normed_two, inverse_two, output, inner_weight, outer_weight,
        branch, staged, sems,
    ) = refs[4 * PARTS :]
    step, steps = pl.program_id(0), pl.num_programs(0)
    wide = staged.shape[-1]
    copies = [
        pltpu.make_async_copy(
            outer.at[:, :, pl.ds(wide, wide)], staged.at[index], sems.at[index]
        )
        for index, outer in enumerate(outers)
    ]

    @pl.when(step == 0)
    def _():
        for copy in copies:
            copy.start()

    unite(inner_weight, inners[:PARTS], inners[PARTS:], spots)
    inner = dot(low[...], inner_weight[...]) + bias[...]
    share = 0.5 * (1.0 + lax.erf(inner * math.sqrt(0.5)))
    raised = jnp.exp(-0.5 * inner * inner) * (1.0 / math.sqrt(2.0 * math.pi))
    acted = narrow(inner * share)
    active[...] = acted
    slope[...] = narrow(share + inner * raised)
    for index in range(PARTS):

        @pl.when(step == spots[2] ^ index)
        def _():
            copies[index].wait()
            copies[PARTS + index].wait()
            half = outer_weight.shape[0] // 2
            for side, at in ((spots[1], index), (1 - spots[1], PARTS + index)):
                start = pl.multiple_of(side * half, half)
                outer_weight[pl.ds(start, half), :] = stack_blocks(staged.at[at])

    part = dot(acted, outer_weight[...])

    @pl.when(step == 0)
    def _():
        branch[...] = part

    @pl.when(step > 0)
    def _():
        branch[...] += part

    height = normed_one.shape[0]
    at = pl.ds(pl.multiple_of(step * height, height), height)
    branch[at, :] += normed_one[...] * rows[3:4] + (rows[4:5] + rows[5:6])

    @pl.when(step == steps - 1)
    def _():
        normed_two[...], inverse_two[...] = normed_of(branch[...])
        result = narrow(normed_two[...] * rows[6:7] + rows[7:8])
        seq, count, places, width = output.shape
        result = result.reshape(count, seq, places, width)
        for row in range(count):
            output[:, row] = result[row]


def feed(spots, low, bias, normed_one, rows, gathered, dims):
    count, width = low.shape
    wide = gathered[0].shape[1] // 2
    block = wide // PARTS
    deep = [part.reshape(dims[0], -1, 2 * wide) for part in gathered]
    all_of = fixed((count, width))
    across = pl.BlockSpec((count, block), lambda f: (0, f))
    return kernel(
        feed_body,
        "feed",
        4 * count * width * wide,
        12 * count * wide,
        grid=(PARTS,),
        in_specs=[
            SCALARS,
            all_of,
            pl.BlockSpec((1, block), lambda f: (0, f)),
            pl.BlockSpec((count // PARTS, width), lambda f: (f, 0)),
            fixed(rows.shape),
        ]
        + gathered_specs(gathered, block, lambda f: f)
        + [ANYWHERE] * len(deep),
        out_specs=[
            across,
            across,
            all_of,
            fixed((count, 1)),
            fixed(dims),
            pl.BlockSpec((width, block), lambda f: (0, f)),
            pl.BlockSpec((block, width), lambda f: (f, 0)),
        ],
        out_shape=[
            shape((count, wide)),
            shape((count, wide)),
            shape((count, width), F32),
            shape((count, 1), F32),
            shape(dims),
            shape((width, wide)),
            shape((wide, width)),
        ],
        scratch_shapes=[
            pltpu.VMEM((count, width), F32),
            pltpu.VMEM((len(deep),) + deep[0].shape[:2] + (wide,), BF16),
            pltpu.SemaphoreType.DMA((len(deep),)),
        ],
    )(spots, low, bias, normed_one, rows, *gathered, *deep)


def feed_back_body(
    spots, cotangent, normed_two, inverse_two, rows_one, low, inner_weight, outer_weight, active, slope,
    keep_inner, send_inner, keep_outer, send_outer, keep_vectors, send_vectors, hidden_grad,
    up, made, columns, pre, grads,
):
    step, steps, side = pl.program_id(0), pl.num_programs(0), spots[1]
    block = inner_weight.shape[-1]

    @pl.when(step == 0)
    def _():
        rows, width = cotangent.shape[1], cotangent.shape[-1]
        upstream = jnp.concatenate(
            [widen(cotangent[:, row]).reshape(-1, width) for row in range(rows)], axis=0
        )
        normed = normed_two[...]
        hidden_grad[...] = norm_back(upstream, normed, inverse_two[...], rows_one[6:7])
        up[...] = narrow(hidden_grad[...])
        columns[...] = as_columns(
            (row_sum(widen(up[...])), row_sum(upstream * normed), row_sum(upstream))
        )

    pre[...] = dot(up[...], outer_weight[...], NT)
    for start in range(0, pre.shape[0], 4 * CHUNK):
        down = slice(start, start + 4 * CHUNK)
        grads[down] = narrow(pre[down] * widen(slope[down]))
    inner_grad = grads[...]
    made[...] = narrow(dot(low[...], inner_grad, TN))
    divide(made, keep_inner, send_inner, side, slice(None))
    hidden_grad[...] += dot(inner_grad, inner_weight[...], NT)
    made[...] = narrow(dot(active[...], up[...], TN))
    divide(made, keep_outer, send_outer, side, slice(None))

    bias = row_sum(widen(inner_grad))
    share_rows = columns.shape[0] // PARTS
    per = block // share_rows
    lane = lax.broadcasted_iota(jnp.int32, (1, LANES), 1)
    total = 0.0
    for column in range(per):
        value = jnp.sum(
            jnp.where(spread_mask(share_rows, per, column), bias, 0.0), axis=1, keepdims=True
        )
        total = total + jnp.where(lane == 3 + column, value, 0.0)
    columns[pl.ds(pl.multiple_of(step * share_rows, share_rows), share_rows), :] += total

    @pl.when(step == steps - 1)
    def _():
        made[:, :LANES] = narrow(columns[...])
        divide(made.at[:, :LANES], keep_vectors, send_vectors, side, slice(None))


def feed_back(spots, cotangent, normed_two, inverse_two, rows, low, inner, outer, active, slope):
    count, width = low.shape
    wide = inner.shape[1]
    block = wide // PARTS
    all_of = fixed((count, width))
    across = pl.BlockSpec((count, block), lambda f: (0, f))
    first, second = (PARTS, width // PARTS // 2, wide), (PARTS, block // 2, width)
    third = first[:2] + (LANES,)
    right = pl.BlockSpec(first[:2] + (block,), lambda f: (0, 0, f))
    down = pl.BlockSpec((1,) + second[1:], lambda f: (f, 0, 0))
    return kernel(
        feed_back_body,
        "feed_back",
        8 * count * width * wide,
        12 * count * wide,
        grid=(PARTS,),
        in_specs=[SCALARS, fixed(cotangent.shape), all_of, fixed((count, 1)), fixed(rows.shape), all_of]
        + [
            pl.BlockSpec((width, block), lambda f: (0, f)),
            pl.BlockSpec((block, width), lambda f: (f, 0)),
            across,
            across,
        ],
        out_specs=[right, right, down, down, fixed(third), fixed(third), all_of],
        out_shape=[shape(dims) for dims in (first, first, second, second, third, third)]
        + [shape((count, width), F32)],
        scratch_shapes=[
            pltpu.VMEM((count, width), BF16),
            pltpu.VMEM((width, block), BF16),
            pltpu.VMEM((width, LANES), F32),
            pltpu.VMEM((count, block), F32),
            pltpu.VMEM((count, block), BF16),
        ],
    )(spots, cotangent, normed_two, inverse_two, rows, low, inner, outer, active, slope)


def settle_back_body(
    spots, hidden_grad, normed, inverse, rows, context, weight,
    first_up, context_grad, keep, send, sums, total, made,
):
    step, steps = pl.program_id(0), pl.num_programs(0)

    @pl.when(step == 0)
    def _():
        sums[...] = jnp.zeros_like(sums)
        total[...] = jnp.zeros_like(total)

    upstream = hidden_grad[...]
    up = norm_back(upstream, normed[...], inverse[...], rows[3:4])
    first_up[...] = up
    low = narrow(up)
    context_grad[...] = narrow(dot(low, weight[...], NT))
    total[...] += dot(context[...], low, TN)
    sums[0:1] += row_sum(widen(low))
    sums[1:2] += row_sum(upstream * normed[...])
    sums[2:3] += row_sum(upstream)

    @pl.when(step == steps - 1)
    def _():
        made[...] = narrow(total[...])
        divide(made, keep, send, spots[1], slice(None))


def settle_back(spots, hidden_grad, normed, inverse, rows, context, weight):
    count, width = context.shape
    block = count // 2
    tall = pl.BlockSpec((block, width), lambda i: (i, 0))
    dims = (PARTS, width // PARTS // 2, width)
    return kernel(
        settle_back_body,
        "settle_back",
        10**12,
        16 * count * width,
        grid=(2,),
        in_specs=[SCALARS, tall, tall, pl.BlockSpec((block, 1), lambda i: (i, 0))]
        + [fixed(rows.shape), tall, fixed((width, width))],
        out_specs=[tall, tall, fixed(dims), fixed(dims), fixed((8, width))],
        out_shape=[
            shape((count, width), F32),
            shape((count, width)),
            shape(dims),
            shape(dims),
            shape((8, width), F32),
        ],
        scratch_shapes=[pltpu.VMEM((width, width), F32), pltpu.VMEM((width, width), BF16)],
    )(spots, hidden_grad, normed, inverse, rows, context, weight)


def tokens_back_body(packed_grad, weight, first_up, grad):
    grad[...] = narrow(first_up[...] + dot(packed_grad[0], weight[...], NT))


def tokens_back(packed_grad, weight, first_up, row):
    _, length, wide = packed_grad.shape
    width = wide // 3
    half = length // 2
    return kernel(
        tokens_back_body,
        "tokens_back",
        2 * length * width * wide,
        8 * length * width,
        grid=(2,),
        in_specs=[
            pl.BlockSpec((1, half, wide), lambda i: (row, i, 0)),
            fixed((width, wide)),
            pl.BlockSpec((half, width), lambda i: (2 * row + i, 0)),
        ],
        out_specs=pl.BlockSpec((half, width), lambda i: (i, 0)),
        out_shape=shape((length, width)),
    )(packed_grad, weight, first_up)


def weights_back_body(spots, packed_grad, tokens, packed_sums, sums, keep, send, made):
    part, side = pl.program_id(0), spots[1]
    width = tokens.shape[1]
    made[...] = narrow(dot(tokens[...], packed_grad[...], TN))
    divide(made, keep, send, side, pl.ds(pl.multiple_of(part * width, width), width))

    @pl.when(part == 2)
    def _():
        packed = jnp.sum(packed_sums[...], axis=0)
        made[:, :LANES] = narrow(
            as_columns(
                (packed[:, :width], packed[:, 2 * width :], sums[0:1], sums[1:2], sums[2:3])
            )
        )
        divide(made.at[:, :LANES], keep, send, side, slice(3 * width, 3 * width + LANES))


def weights_back(spots, packed_grad, tokens, packed_sums, sums):
    count, width = tokens.shape
    dims = (PARTS, width // PARTS // 2, 3 * width + LANES)
    return kernel(
        weights_back_body,
        "weights_back",
        6 * count * width * width,
        8 * count * width,
        grid=(3,),
        in_specs=[SCALARS, pl.BlockSpec((count, width), lambda i: (0, i)), fixed(tokens.shape)]
        + [fixed(packed_sums.shape), fixed(sums.shape)],
        out_specs=[fixed(dims), fixed(dims)],
        out_shape=[shape(dims), shape(dims)],
        scratch_shapes=[pltpu.VMEM((width, width), BF16)],
    )(spots, packed_grad, tokens, packed_sums, sums)


def side_by_side(out, start, total):
    small, width = out.shape[0], total.shape[1]
    for height in range(0, total.shape[0], small):
        out[:, start : start + width] = narrow(total[height : height + small])
        start += width
    return start


def chip_sums(name, spots, pairs, seq, small):
    operands, in_specs = [], []
    wide = sum(kept.shape[1] // (seq * small) * kept.shape[2] for kept, _ in pairs)
    for kept, came in pairs:
        height = kept.shape[1] // seq
        for value in (kept, came):
            operands.append(value.reshape(PARTS, seq, height, value.shape[2]))
            in_specs.append(
                pl.BlockSpec(
                    (PARTS, None, height, value.shape[2]), lambda i, spots: (0, i, 0, 0)
                )
            )

    def body(spots, *refs):
        ins, outs = refs[: len(operands)], refs[len(operands) :]
        for part, out in enumerate(outs):
            start = 0
            chip = spots[2] ^ part
            for kept, came in zip(ins[::2], ins[1::2]):
                if kept.shape[1] == small:
                    out[:, start : start + kept.shape[2]] = kept[chip] + came[chip]
                    start += kept.shape[2]
                else:
                    start = side_by_side(out, start, widen(kept[chip]) + widen(came[chip]))

    return kernel(
        body,
        name,
        0,
        6 * PARTS * seq * small * wide,
        grid_spec=pltpu.PrefetchScalarGridSpec(
            num_scalar_prefetch=1,
            grid=(seq,),
            in_specs=in_specs,
            out_specs=[pl.BlockSpec((None, small, wide), lambda i, spots: (i, 0, 0))] * PARTS,
        ),
        out_shape=[shape((seq, small, wide))] * PARTS,
    )(spots, *operands)


def total_body(*refs):
    total = widen(refs[0][...])
    for ref in refs[1:-1]:
        total = total + widen(ref[...])
    refs[-1][...] = narrow(total)


def total_of(name, values, flops=0):
    seq, small, wide = values[0].shape
    block = pl.BlockSpec((None, small, wide), lambda i: (i, 0, 0))
    return kernel(
        total_body,
        name,
        flops,
        2 * (len(values) + 1) * seq * small * wide,
        grid=(seq,),
        in_specs=[block] * len(values),
        out_specs=block,
        out_shape=shape(values[0].shape),
    )(*values)


def total_pieces(name, spots, values):
    seq, small, wide = values[0].shape

    def body(spots, *refs):
        for step in range(seq):
            at = lax.rem(spots[0] + step, seq)
            total_body(*[ref.at[at] for ref in refs[: len(values)]], refs[len(values) + step])

    return kernel(
        body,
        name,
        0,
        2 * (len(values) + 1) * seq * small * wide,
        in_specs=[SCALARS] + [pl.BlockSpec(memory_space=pltpu.VMEM)] * len(values),
        out_specs=[pl.BlockSpec(memory_space=pltpu.VMEM)] * seq,
        out_shape=[shape((small, wide))] * seq,
    )(spots, *values)


def copied(value, *others):
    def body(source, target):
        target[...] = source[...]

    block = pl.BlockSpec((1,) + value.shape[1:], lambda i: (i,) + (0,) * (value.ndim - 1))
    return kernel(
        body,
        "copied",
        0,
        4 * math.prod(value.shape),
        grid=value.shape[:1],
        in_specs=[block],
        out_specs=block,
        out_shape=like(value),
    )(after(value, *others))


def finish_body(count, vectors, blocks, *refs):
    pieces, outs = refs[:count], refs[count:]
    if count == 1:
        pieces = [pieces[0].at[index] for index in range(pieces[0].shape[0])]
    total = widen(pieces[0][...])
    for piece in pieces[1:]:
        total = total + widen(piece[...])
    small, wide = total.shape
    start = 0
    for out, (count, width) in zip(outs, blocks):
        for index in range(count):
            out[index * small : (index + 1) * small] = total[:, start : start + width]
            start += width
    at = wide - LANES
    for out, (column, per) in zip(outs[len(blocks) :], vectors):
        line = 0.0
        for part in range(per):
            value = total[:, at + column + part : at + column + part + 1]
            line = line + jnp.where(spread_mask(small, per, part), value, 0.0)
        out[...] = row_sum(line)


def finish(name, pieces, blocks, vectors):
    small, wide = pieces[0].shape[-2:]
    return kernel(
        partial(finish_body, len(pieces), vectors, blocks),
        name,
        0,
        8 * small * wide,
        out_shape=[shape((count * small, width), F32) for count, width in blocks]
        + [shape((1, small * per), F32) for _, per in vectors],
    )(*pieces)


def block_at(blocks, index, axis=0):
    return lax.dynamic_index_in_dim(blocks, index, axis, keepdims=False)


class Links:
    def __init__(self, mesh):
        self.dp, self.seq = mesh.shape["dp"], mesh.shape["seq"]
        self.bits = self.dp.bit_length() - 1
        assert self.dp == 1 << self.bits
        self.direct = self.dp == 2 * PARTS

    def across(self, value, flip):
        pairs = [
            (d * self.seq + s, (d ^ flip) * self.seq + s)
            for d in range(self.dp)
            for s in range(self.seq)
        ]
        return lax.ppermute(value, AXES, pairs)

    def along(self, value, step):
        pairs = [
            (d * self.seq + s, d * self.seq + (s + step) % self.seq)
            for d in range(self.dp)
            for s in range(self.seq)
        ]
        return lax.ppermute(value, AXES, pairs)

    def digit(self, bit):
        return (lax.axis_index("dp") >> bit) & 1

    def spots(self):
        place, dp = lax.axis_index("seq"), lax.axis_index("dp")
        side, chip = (dp & 1, dp >> 1) if self.direct else (0 * dp, 0 * dp)
        return jnp.stack([place, side, chip]).astype(jnp.int32)

    def turn(self, blocks):
        return lax.all_to_all(blocks, "seq", split_axis=0, concat_axis=0, tiled=True)

    def spread(self, held):
        return [held] + [self.across(held, 2 * part) for part in range(1, PARTS)]

    def swap(self, parts):
        parts = [part.reshape(-1, part.shape[-1]) for part in parts]
        return parts + [self.across(part, 1) for part in parts]

    def gather_whole(self, held):
        done = []
        for bit in range(self.bits):
            other, mine = self.across(held, 1 << bit), self.digit(bit)
            held = jnp.where(mine == 0, jnp.stack([held, other]), jnp.stack([other, held]))
        return held.reshape(self.dp * self.seq, *held.shape[self.bits + 1 :])

    def cut(self, whole):
        whole = whole.reshape(PARTS, 2, -1, whole.shape[-1])
        return [whole[part, side] for side in range(2) for part in range(PARTS)]

    def reduce_whole(self, keep, send):
        rows = keep.shape[0] * keep.shape[1] * 2 // (self.dp * self.seq)
        whole = jnp.stack([keep, send], axis=1)
        held = whole.reshape((2,) * self.bits + (self.seq, rows, keep.shape[-1]))
        for bit in reversed(range(self.bits)):
            mine = self.digit(bit)
            other = self.across(block_at(held, 1 - mine), 1 << bit)
            held = narrow(widen(block_at(held, mine)) + widen(other))
        return held


def shards(
    links,
    tokens,
    cotangent,
    lengths,
    packed_weight,
    query_bias,
    value_bias,
    output_weight,
    output_bias,
    first_gain,
    first_shift,
    inner_weight,
    inner_bias,
    outer_weight,
    outer_bias,
    second_gain,
    second_shift,
):
    row_count, places, width = tokens.shape
    seq, direct = links.seq, links.direct
    rows = row_count // seq
    dims = (seq, rows, places, width)
    small, tall = packed_weight.shape[0], outer_weight.shape[0]
    wide = inner_weight.shape[1]
    per = wide // width
    spots = links.spots()

    vectors = (
        query_bias, value_bias, output_bias, first_gain, first_shift,
        outer_bias, second_gain, second_shift, inner_bias,
    )
    held = links.turn(prepare_attention(seq, packed_weight, output_weight, vectors))
    feed_held = links.turn(after(prepare_feed(seq, inner_weight, outer_weight), held))
    if direct:
        held = links.spread(held)
        came = links.turn(after(tokens.reshape(dims), feed_held, *held))
        gathered = links.swap(held)
        feed_held = links.spread(feed_held)
    else:
        came = links.turn(after(tokens.reshape(dims), feed_held))
        gathered = links.cut(links.gather_whole(held))
        whole = links.gather_whole(feed_held)
        inner, outer = whole[..., :wide], whole[..., wide:]
        outer = outer.reshape(-1, small, per, width).swapaxes(1, 2)
        outer = outer.reshape(2 * PARTS * seq, per, -1, width).swapaxes(1, 2)
        inner, outer = inner.reshape(width, wide), outer.reshape(width, wide)
        feed_gathered = links.cut(jnp.concatenate([inner, outer], axis=1))
    cotangent_mine = links.turn(after(cotangent.reshape(dims), came))
    packed_whole, output_whole, rows_one, inner_bias_row = unite_attention(spots, gathered, wide)
    packed, flat = project(came, packed_whole, rows_one)
    context, probs = attend(spots, lengths, packed)
    context = context.reshape(-1, width)
    if direct:
        feed_held = [feed_held[0]] + [after(value, context) for value in feed_held[1:]]
        context = after(context, *feed_held)
        feed_gathered = links.swap(feed_held)
    normed_one, inverse_one, low = settle(context, flat, rows_one, output_whole)
    active, slope, normed_two, inverse_two, output, inner_whole, outer_whole = feed(
        spots, low, inner_bias_row, normed_one, rows_one, feed_gathered, dims
    )
    cotangent_mine = after(cotangent_mine, slope)
    output = after(output, cotangent_mine)
    cotangent_mine = after(cotangent_mine, output)
    (
        keep_inner, send_inner, keep_outer, send_outer, keep_vectors, send_vectors, hidden_grad,
    ) = feed_back(
        spots,
        cotangent_mine,
        normed_two,
        inverse_two,
        rows_one,
        low,
        inner_whole,
        outer_whole,
        active,
        slope,
    )
    hidden_grad = after(hidden_grad, send_inner, send_outer, send_vectors)
    first_up, context_grad, keep_output, send_output, sums = settle_back(
        spots, hidden_grad, normed_one, inverse_one, rows_one, context, output_whole
    )
    output = after(links.turn(output), sums)
    context_grad = after(context_grad, output)
    if direct:
        inner_came = after(links.across(send_inner, 1), sums)
        outer_came = after(links.across(send_outer, 1), sums)
        output_came = links.across(send_output, 1)
        vectors_came = after(links.across(send_vectors, 1), sums)
        pairs = [
            (keep_outer, outer_came),
            (keep_output, output_came),
            (keep_inner, inner_came),
            (keep_vectors, vectors_came),
        ]
        feed_sums = list(chip_sums("feed_chip_sums", spots, pairs, seq, small))
        context_grad = after(context_grad, *feed_sums[1:])
        feed_sums[1:] = [links.across(feed_sums[part], 2 * part) for part in range(1, PARTS)]
    context_grad = context_grad.reshape(rows, seq * places, width)
    prior, tokens_grad = (), []
    for row in range(rows):
        prior = attend_back(packed, probs, context_grad, row, prior)
        grad = tokens_back(prior[0], packed_whole, first_up, row)
        context_grad = after(context_grad, grad)
        sent = after(grad, tokens_grad[-1]) if row else grad
        tokens_grad.append(links.turn(sent.reshape(seq, places, width)))
    packed_grad, packed_sums = prior
    packed_grad = after(packed_grad, grad).reshape(-1, 3 * width)
    keep, send = weights_back(spots, packed_grad, flat, packed_sums, sums)
    output = copied(output, keep)
    if direct:
        feed_sums[1:] = [after(value, keep, output) for value in feed_sums[1:]]
        feed_total = total_of("feed_total", feed_sums, 10**10)
        came = after(links.across(send, 1), feed_total)
        attention_sums = list(
            chip_sums("attention_chip_sums", spots, [(keep, came)], seq, small)
        )
        feed_total = after(feed_total, *tokens_grad)
        attention_sums[1:] = [
            links.across(attention_sums[part], 2 * part) for part in range(1, PARTS)
        ]
        attention_total = total_pieces("attention_total", spots, attention_sums)
    else:
        reduced = [
            links.reduce_whole(*pair)
            for pair in (
                (keep_outer, send_outer),
                (keep_output, send_output),
                (keep_inner, send_inner),
                (keep_vectors, send_vectors),
            )
        ]
        reduced[0] = reduced[0].reshape(seq, per, small, width).swapaxes(1, 2)
        reduced[0] = reduced[0].reshape(seq, small, per * width)
        feed_total = jnp.concatenate(reduced, axis=2)
        attention_total = links.reduce_whole(keep, send)
        attention_total = [block_at(attention_total, (spots[0] + i) % seq) for i in range(seq)]
    feed_total = links.turn(feed_total)
    attention_total = [
        links.along(piece, step) if step else piece for step, piece in enumerate(attention_total)
    ]
    (
        outer_grad, output_grad, inner_grad,
        outer_bias_grad, second_gain_grad, second_shift_grad, inner_bias_grad,
    ) = finish(
        "finish_feed",
        [feed_total],
        [(per, width), (1, width), (1, wide)],
        [(0, 1), (1, 1), (2, 1), (3, per)],
    )
    tokens_grad = widen(jnp.stack(tokens_grad, axis=1))
    attention_total[1:] = [after(piece, inner_grad, tokens_grad) for piece in attention_total[1:]]
    (
        packed_weight_grad,
        query_bias_grad, value_bias_grad, output_bias_grad, first_gain_grad, first_shift_grad,
    ) = finish(
        "finish_attention", attention_total, [(1, 3 * width)], [(i, 1) for i in range(5)]
    )
    return (
        output.reshape(tokens.shape),
        tokens_grad.reshape(tokens.shape),
        packed_weight_grad,
        query_bias_grad.reshape(-1),
        value_bias_grad.reshape(-1),
        output_grad,
        output_bias_grad.reshape(-1),
        first_gain_grad.reshape(-1),
        first_shift_grad.reshape(-1),
        inner_grad,
        inner_bias_grad.reshape(-1),
        outer_grad,
        outer_bias_grad.reshape(-1),
        second_gain_grad.reshape(-1),
        second_shift_grad.reshape(-1),
    )


def solution(mesh):
    split = P(AXES)
    split_rows = P(AXES, None)
    packed_rows = P("dp", "seq", None)
    return jax.shard_map(
        partial(shards, Links(mesh)),
        mesh=mesh,
        in_specs=(
            packed_rows,
            packed_rows,
            P("dp", None),
            split_rows,
            split,
            split,
            split_rows,
            split,
            split,
            split,
            split_rows,
            split,
            split_rows,
            split,
            split,
            split,
        ),
        out_specs=(
            packed_rows,
            packed_rows,
            split_rows,
            split,
            split,
            split_rows,
            split,
            split,
            split,
            split_rows,
            split,
            split_rows,
            split,
            split,
            split,
        ),
        check_vma=False,
    )
```
